128 devices in a mesh: seq: 64 (over z, y, x), tensor: 2 (over core).
Axes of the slice: x: 4, y: 4, z: 4, core: 2. Of those that a mesh axis runs over, the one named last changes fastest.
Arguments:
- tokens: bfloat16 [8192, 1536], P('seq'), may hold values from -7.5 to 7.5
- attn_weight: bfloat16 [3, 1536, 1536], P(None, None, 'tensor'), may hold values from -2 to 2
- out_weight: bfloat16 [1536, 1536], P('tensor'), may hold values from -0.15625 to 0.15625
- norm_attn: float32 [1536], replicated, may hold values from 0.25 to 1.75
- norm_moe: float32 [1536], replicated, may hold values from 0.25 to 1.75
- routes: int32 [8192, 2], P('seq'), may hold values from 0 to 15, all different within a row; in each aligned block of 128 rows (0 to 127, 128 to 255, ...) at most 24 rows name the same one
- route_weight: float32 [8192, 2], P('seq'), may hold values from 0.1 to 1
- expert_in: bfloat16 [64, 2, 1536, 1536], P('seq', None, None, 'tensor'), may hold values from -0.15625 to 0.15625
- expert_out: bfloat16 [64, 1536, 1536], P('seq', 'tensor'), may hold values from -0.078125 to 0.078125
Outputs:
- layer_out: bfloat16 [8192, 1536], P('seq', 'tensor')
The draws below stay inside these ranges and needn't reach their ends.
Inputs may be any that keep to these rules, and one draw needn't show every extreme that they name: `routes`: in the rows of one device no expert is named by more than 24 rows, a bound that some block reaches; the two experts of a token differ.
All inputs are finite; a program needn't handle non-finite values.
Results may differ from the reference program's by a relative error of at most 0.017.
The reference program's roundings to bfloat16 on the way count: a program that leaves them out, or rounds other values in their place, can miss the bound.
Values may be sent and summed in bfloat16 or wider, within the bound.
A program may use at most 192 MiB of HBM per device.

```python
import math
import jax
import jax.numpy as jnp
import numpy as np
from jax import lax

D = 1536
FF = 6144
HEADS = 16
EXPERTS = 16
HD = 96
TOK_DEV = 128
TOKENS = 8192
SPLIT = 4
CAP = 24
N_SEQ = 64


def draw_attn_weight(key, part):
    key = jax.random.fold_in(key, 11)
    drawn_values = jax.random.normal(key, (3, D, HEADS * HD), jnp.float32) * D ** (-0.5)
    return drawn_values.astype(jnp.bfloat16)


def column_ramp(low_scale, rise):
    place = jnp.arange(D, dtype=jnp.float32) / (D - 1.0)
    return low_scale * jnp.exp(place * jnp.log(rise))


def draw_tokens(key, part):
    key = jax.random.fold_in(key, 23)
    drawn_values = jnp.clip(jax.random.normal(key, (TOKENS, D), jnp.float32), -5.0, 5.0) * column_ramp(0.5, 3.0)[None, :]
    return drawn_values.astype(jnp.bfloat16)


def level_of(rng, shape, pieces, low, top_value):
    level = 1.0
    for dim, blocks in pieces:
        draws = jax.random.uniform(jax.random.fold_in(jax.random.fold_in(rng, 6), dim), (blocks,), jnp.float32, low / len(pieces), top_value / len(pieces))
        level = level * jnp.repeat(jnp.exp(draws), shape[dim] // blocks).reshape((-1,) + (1,) * (len(shape) - 1 - dim))
    return level


def assign_block(rng, own, number, rows, number_of, top, reach, slope):
    sequence = jax.random.permutation(rng, number_of)
    crowded, common = load_shares(number_of, rows * top, reach, slope, True), load_shares(number_of, rows * top, reach, slope, False)
    places = jnp.arange(number_of)

    def named(sizes, offset_by):
        used = int((sizes > 0).sum())
        fixed = max(1, used // 4)
        passed = fixed + (places - fixed + offset_by * (used - fixed)) % max(1, number_of - fixed)
        return jnp.zeros((number_of,), jnp.int32).at[sequence[jnp.where(places < fixed, places, passed)]].set(jnp.asarray(sizes, jnp.int32))

    sizes = jnp.where(number % 4 == 0, named(crowded, number // 4), named(common, number - number // 4 - 1))
    mixed = jax.random.permutation(jax.random.fold_in(own, 3), number_of)
    source_of, receiver = mixed[0:number_of // 2 * 2:2], mixed[1:number_of // 2 * 2:2]
    room = jnp.minimum(sizes[source_of] - 1, reach - sizes[receiver]) // 2
    room = jnp.where((source_of == sequence[0]) | (receiver == sequence[0]) | (sizes[receiver] == 0), 0, jnp.maximum(room, 0))
    passed = jax.random.randint(jax.random.fold_in(own, 4), (number_of // 2,), 0, 1 << 20) % (room + 1)
    sizes = sizes.at[source_of].add(-passed).at[receiver].add(passed)
    labels = jnp.searchsorted(jnp.cumsum(sizes), jnp.arange(rows * top), side="right").astype(jnp.int32)
    grid = labels.reshape(top, rows).T
    grid = grid[jax.random.permutation(jax.random.fold_in(own, 1), rows)]
    offset_by = jax.random.randint(jax.random.fold_in(own, 2), (rows, 1), 0, top)
    return jnp.take_along_axis(grid, (jnp.arange(top)[None, :] + offset_by) % top, axis=1)


def load_shares(count, total, most, skew, full):
    loads = [(1 << 20) // math.isqrt(standing ** skew) + 1 for standing in range(1, count + 1)]
    largest = most if full else min(most, max(-(-total // count), total * loads[0] // sum(loads)))
    least = 1 if total - largest >= count - 1 else 0
    counts, spare = [largest] + [least] * (count - 1), total - largest - least * (count - 1)
    while spare > 0:
        movable = [i for i in range(1, count) if counts[i] < largest] or [i for i in range(1, count) if counts[i] < most]
        pool, budget = sum([loads[i] for i in movable]), spare
        for i in movable:
            more = min(most - counts[i], max(1, budget * loads[i] // pool), spare)
            counts[i] = counts[i] + more
            spare = spare - more
    return np.array(counts)


def centred(key, extent, scale, reach, shards=(), kind=jnp.bfloat16):
    factor_of = level_of(key, extent, shards, -0.22, 0.18) if shards else 1.0
    values = jax.random.normal(key, extent, jnp.float32) * scale * factor_of
    return jnp.minimum(jnp.maximum(values, -reach), reach).astype(kind)


def setup_inputs(seed: int = 0) -> dict:
    arg_keys = jax.random.split(jax.random.key(seed), 10)
    tokens = draw_tokens(jax.random.fold_in(arg_keys[9], 71), 0)
    attn_weight = draw_attn_weight(jax.random.fold_in(arg_keys[9], 71), 0)
    out_weight = centred(arg_keys[2], (HEADS * HD, D), (HEADS * HD) ** -0.5, 0.15625, ((0, 2),))
    norm_attn = jnp.clip(1.0 + 0.15 * jax.random.normal(arg_keys[3], (D,), jnp.float32), 0.25, 1.75)
    norm_moe = jnp.clip(1.0 + 0.15 * jax.random.normal(arg_keys[4], (D,), jnp.float32), 0.25, 1.75)
    routes_keys = jax.random.split(jax.random.fold_in(arg_keys[5], 1), TOKENS // TOK_DEV)
    routes_turns = jax.random.permutation(jax.random.fold_in(arg_keys[5], 3), TOKENS // TOK_DEV)
    routes = jax.vmap(lambda own, number: assign_block(jax.random.fold_in(arg_keys[5], 2), own, number, TOK_DEV, EXPERTS, 2, CAP, 1))(routes_keys, routes_turns).reshape((TOKENS, 2))
    route_weight = jnp.clip(0.1 + 0.9 * jax.random.uniform(arg_keys[6], (TOKENS, 2), jnp.float32) ** level_of(arg_keys[6], (TOKENS, 2), ((0, 64),), -0.2, 0.2), 0.1, 1.0)
    expert_in = centred(arg_keys[7], (EXPERTS * SPLIT, 2, D, FF // SPLIT), D ** -0.5, 0.15625, ((0, 64), (3, 2)))
    expert_out = centred(arg_keys[8], (EXPERTS * SPLIT, FF // SPLIT, D), FF ** -0.5, 0.078125, ((0, 64), (1, 2)))
    return dict(tokens=tokens, attn_weight=attn_weight, out_weight=out_weight, norm_attn=norm_attn, norm_moe=norm_moe, routes=routes, route_weight=route_weight, expert_in=expert_in, expert_out=expert_out)


eps = 1e-06

def rms_scale(values, gain_row):
    mean_square = lax.optimization_barrier(jnp.mean(values * values, axis=-1, keepdims=True))
    return values * lax.rsqrt(mean_square + eps) * gain_row

def slot_index(route_rows, expert_count, capacity):
    flat_ids = route_rows.reshape(-1).astype(jnp.int32)
    onehot = (flat_ids[:, None] == jnp.arange(expert_count, dtype=jnp.int32)[None, :]).astype(jnp.int32)
    before = jnp.cumsum(onehot, axis=0) - onehot
    return (flat_ids * capacity + lax.optimization_barrier(jnp.sum(before * onehot, axis=1))).astype(jnp.int32)

def head_attend(parts):
    query_head, key_head, value_head = parts
    scores = jnp.dot(query_head, key_head.T, preferred_element_type=jnp.float32) * HD ** (-0.5)
    row_peak = lax.optimization_barrier(jnp.max(scores, axis=1, keepdims=True))
    exp_scores = jnp.exp(scores - row_peak)
    row_total = lax.optimization_barrier(jnp.sum(exp_scores, axis=1, keepdims=True))
    prob_rows = exp_scores.astype(jnp.bfloat16)
    return (jnp.dot(prob_rows, value_head, preferred_element_type=jnp.float32) / row_total).astype(jnp.bfloat16)

def expert_apply(parts):
    rows_in, weights_in, weights_out = parts
    flat_rows = rows_in.reshape(-1, D)
    total = jnp.zeros((flat_rows.shape[0], D), jnp.float32)
    for piece in range(SPLIT):
        gate_value = jnp.dot(flat_rows, weights_in[piece, 0], preferred_element_type=jnp.float32)
        up_value = jnp.dot(flat_rows, weights_in[piece, 1], preferred_element_type=jnp.float32)
        activated = (jax.nn.silu(gate_value) * up_value).astype(jnp.bfloat16)
        part_rows = jnp.dot(activated, weights_out[piece], preferred_element_type=jnp.float32).astype(jnp.bfloat16)
        total = total + part_rows.astype(jnp.float32)
    return total.astype(jnp.bfloat16).reshape(N_SEQ, CAP, D)

def reference(tokens, attn_weight, out_weight, norm_attn, norm_moe, routes, route_weight, expert_in, expert_out):
    normed = rms_scale(tokens.astype(jnp.float32), norm_attn).astype(jnp.bfloat16)
    queries = jnp.dot(normed, attn_weight[0], preferred_element_type=jnp.float32).astype(jnp.bfloat16)
    keys_all = jnp.dot(normed, attn_weight[1], preferred_element_type=jnp.float32).astype(jnp.bfloat16)
    values_all = jnp.dot(normed, attn_weight[2], preferred_element_type=jnp.float32).astype(jnp.bfloat16)

    def by_head(matrix):
        return matrix.reshape(TOKENS, HEADS, HD).transpose(1, 0, 2)
    heads_out = lax.map(head_attend, (by_head(queries), by_head(keys_all), by_head(values_all)))
    heads_out = heads_out.transpose(1, 0, 2).reshape(TOKENS, HEADS * HD)
    hidden_state = tokens.astype(jnp.float32) + jnp.dot(heads_out, out_weight, preferred_element_type=jnp.float32)
    moe_in = rms_scale(hidden_state, norm_moe).astype(jnp.bfloat16)
    blocks = moe_in.reshape(N_SEQ, TOK_DEV, D)
    route_blocks = routes.reshape(N_SEQ, TOK_DEV, 2)
    indices = jax.vmap(lambda route_rows: slot_index(route_rows, EXPERTS, CAP))(route_blocks)

    def fill_block(block_rows, index_rows):
        empty_rows = jnp.zeros((EXPERTS * CAP, D), jnp.bfloat16)
        return empty_rows.at[index_rows].set(jnp.repeat(block_rows, 2, axis=0))
    buffer = jax.vmap(fill_block)(blocks, indices).reshape(N_SEQ, EXPERTS, CAP, D).transpose(1, 0, 2, 3)
    grouped_in = expert_in.reshape(EXPERTS, SPLIT, 2, D, FF // SPLIT)
    grouped_out = expert_out.reshape(EXPERTS, SPLIT, FF // SPLIT, D)
    expert_rows = lax.map(expert_apply, (buffer, grouped_in, grouped_out))
    per_source = expert_rows.transpose(1, 0, 2, 3).reshape(N_SEQ, EXPERTS * CAP, D)
    picked = jax.vmap(lambda table_rows, index_rows: table_rows[index_rows])(per_source, indices)
    picked = picked.reshape(TOKENS, 2, D).astype(jnp.float32)
    combined = lax.optimization_barrier(jnp.sum(picked * route_weight[:, :, None], axis=1))
    return (hidden_state + combined).astype(jnp.bfloat16)
```

```python
import math

import jax
import jax.numpy as jnp
from jax import lax
from jax.experimental import pallas as pl
from jax.experimental.pallas import tpu as pltpu
from jax.sharding import PartitionSpec as P

MESH = pl.DeviceIdType.MESH
D = 1536
HALF = 768
QUART = 384
HD = 96
TOK = 128
EXPERTS = 16
CAP = 24
EPS = 1e-6
F32 = jnp.float32
BF16 = jnp.bfloat16
SCALE = HD ** (-0.5) * math.log2(math.e)


def dot(a, b):
    return jnp.dot(a, b, preferred_element_type=F32)


def remote(src, dst, send_sem, recv_sem, device):
    return pltpu.make_async_remote_copy(
        src_ref=src,
        dst_ref=dst,
        send_sem=send_sem,
        recv_sem=recv_sem,
        device_id=device,
        device_id_type=MESH,
    )


def layer_kernel(
    tokens,
    attn_w,
    out_w,
    norm_attn,
    norm_moe,
    routes,
    route_weight,
    expert_in,
    expert_out,
    out,
    w_buf,
    ow_buf,
    wi_buf,
    wd_buf,
    w_sem,
    kv_send,
    q_send,
    q_t,
    kvb,
    q_pad,
    peak,
    acc,
    o_send,
    heads_t,
    proj_send,
    proj_recv,
    moe_half,
    disp,
    xbuf,
    rows_in,
    y_own,
    y_send,
    y_recv,
    parts,
    diag_recv,
    side_recv,
    back,
    ret,
    kv_ss,
    kv_rs,
    q_ss,
    q_rs,
    ring_ss,
    ring_rs,
    twin_ss,
    twin_rs,
    o_ss,
    o_rs,
    proj_sem,
    d_ss,
    d_rs,
    xr_ss,
    xr_rs,
    xt_ss,
    xt_rs,
    y_ss,
    y_rs,
    r_ss,
    r_rs,
    b_ss,
    b_rs,
):
    s = lax.axis_index("seq")
    c = lax.axis_index("tensor")
    x = s % 4
    plane = s // 4
    z = plane // 4
    y = plane % 4
    side = z // 2
    slot = (z % 2) * 4 + y
    left = (s - x + (x + 3) % 4, c)
    right = (s - x + (x + 1) % 4, c)
    twin = (s, 1 - c)

    def mate(i):
        return ((2 * c + i // 4) * 16 + (i % 4) * 4 + x, side)

    def is_me(i):
        return jnp.logical_and(c == side, i == slot)

    def plane_dev(p):
        return (p * 4 + x, c)

    weight_copies = [
        pltpu.make_async_copy(attn_w.at[1], w_buf.at[1], w_sem.at[1]),
        pltpu.make_async_copy(attn_w.at[2], w_buf.at[2], w_sem.at[2]),
        pltpu.make_async_copy(attn_w.at[0], w_buf.at[0], w_sem.at[0]),
        pltpu.make_async_copy(out_w, ow_buf, w_sem.at[3]),
        pltpu.make_async_copy(expert_in.at[0], wi_buf, w_sem.at[4]),
        pltpu.make_async_copy(expert_out.at[0, :, pl.ds(0, HALF)], wd_buf.at[0], w_sem.at[5]),
        pltpu.make_async_copy(expert_out.at[0, :, pl.ds(HALF, HALF)], wd_buf.at[1], w_sem.at[6]),
    ]
    for copy in weight_copies:
        copy.start()

    barrier = pltpu.get_barrier_semaphore()

    def greet(device):
        pl.semaphore_signal(barrier, inc=1, device_id=device, device_id_type=MESH)

    for device in (left, right, twin):
        greet(device)

    @pl.loop(0, 8)
    def _(i):
        @pl.when(jnp.logical_not(is_me(i)))
        def _():
            greet(mate(i))

    @pl.loop(0, 16)
    def _(p):
        @pl.when(p != plane)
        def _():
            greet(plane_dev(p))

    tok = tokens[...].astype(F32)
    mean_square = jnp.mean(tok * tok, axis=1, keepdims=True)
    normed = (tok * lax.rsqrt(mean_square + EPS) * norm_attn[...]).astype(BF16)
    weight_copies[0].wait()
    kv_send[:, 0:HD, :] = dot(normed, w_buf[1]).T.astype(BF16).reshape(8, HD, TOK)
    weight_copies[1].wait()
    kv_send[:, HD : 2 * HD, :] = dot(normed, w_buf[2]).T.astype(BF16).reshape(8, HD, TOK)

    pl.semaphore_wait(barrier, 3 + 15 + 8 - jnp.where(c == side, 1, 0))

    def exchange(i, src, dst, send_sem, recv_sem, start):
        copy = remote(src, dst, send_sem, recv_sem, mate(i))

        @pl.when(jnp.logical_not(is_me(i)))
        def _():
            if start:
                copy.start()
            else:
                copy.wait_send()

        if start:

            @pl.when(is_me(i))
            def _():
                pltpu.make_async_copy(src, dst, recv_sem).start()

    def lanes(i):
        return pl.ds(pl.multiple_of(i * TOK, TOK), TOK)

    def kv_copy(i, start):
        exchange(
            i,
            kv_send.at[i],
            kvb.at[0, pl.ds(0, 2 * HD), lanes(slot)],
            kv_ss.at[i],
            kv_rs.at[slot],
            start,
        )

    def q_copy(i, start):
        exchange(i, q_send.at[i], q_t.at[:, lanes(slot)], q_ss.at[i], q_rs.at[slot], start)

    @pl.loop(0, 8)
    def _(i):
        kv_copy((i + slot) % 8, True)

    weight_copies[2].wait()
    q_send[...] = (dot(normed, w_buf[0]) * SCALE).T.astype(BF16).reshape(8, HD, TOK)

    @pl.loop(0, 8)
    def _(i):
        q_copy((i + slot) % 8, True)

    @pl.loop(0, 8)
    def _(b):
        kvb[b, 2 * HD : 2 * HD + 32, :] = jnp.ones((32, 8 * TOK), BF16)

    peak[...] = jnp.full(peak.shape, -1e30, F32)
    acc[...] = jnp.zeros(acc.shape, F32)
    q_pad[:, HD:] = jnp.zeros((8 * TOK, TOK - HD), BF16)

    expert_ids = lax.broadcasted_iota(jnp.int32, (TOK, EXPERTS), 1)
    hot = [(routes[:, k : k + 1] == expert_ids).astype(F32) for k in range(2)]
    earlier = (
        lax.broadcasted_iota(jnp.int32, (TOK, TOK), 0)
        > lax.broadcasted_iota(jnp.int32, (TOK, TOK), 1)
    ).astype(BF16)
    before = dot(earlier, (hot[0] + hot[1]).astype(BF16))
    place = [
        jnp.sum(before * hot[k], axis=1, keepdims=True)
        + routes[:, k : k + 1].astype(F32) * (2.0 * CAP)
        for k in range(2)
    ]

    def kv_part(dx, dc, h):
        return kvb.at[2 * dx + dc, pl.ds(0, 2 * HD), pl.ds(h * 512, 512)]

    def ring_copy(to, src_dx, dst_dx, h):
        device = right if to == 0 else left
        return remote(
            kv_part(src_dx, 0, h),
            kv_part(dst_dx, 0, h),
            ring_ss.at[dst_dx, h],
            ring_rs.at[dst_dx, h],
            device,
        )

    def twin_copy(dx, h):
        return remote(kv_part(dx, 0, h), kv_part(dx, 1, h), twin_ss.at[dx, h], twin_rs.at[dx, h], twin)

    ring_own = [[ring_copy(0, 0, 3, h), ring_copy(1, 0, 1, h)] for h in range(2)]
    ring_on = [ring_copy(0, 3, 2, 0), ring_copy(1, 1, 2, 1)]
    for h in range(2):

        @pl.loop(4 * h, 4 * h + 4)
        def _(i):
            remote(
                kv_send.at[i],
                kvb.at[0, pl.ds(0, 2 * HD), lanes(i)],
                kv_ss.at[i],
                kv_rs.at[i],
                mate(i),
            ).wait_recv()

        ring_own[h][0].start()
        ring_own[h][1].start()
        twin_copy(0, h).start()

    @pl.loop(0, 8)
    def _(i):
        remote(q_send.at[i], q_t.at[:, lanes(i)], q_ss.at[i], q_rs.at[i], mate(i)).wait_recv()
        rows = pl.ds(pl.multiple_of(i * TOK, TOK), TOK)
        q_pad[rows, 0:HD] = q_t[:, lanes(i)].astype(F32).T.astype(BF16)

    def attend(dx, dc):
        b = 2 * dx + dc

        @pl.loop(0, 4)
        def _(i):
            rows = pl.ds(pl.multiple_of(i * 256, 256), 256)
            scores = dot(q_pad[rows, :], kvb[b, 0:TOK, :])
            old = peak[rows, :]
            new = jnp.maximum(old, jnp.max(scores, axis=1, keepdims=True))
            probs = jnp.exp2(scores - new[:, 0:1]).astype(BF16)
            update = lax.dot_general(
                probs,
                kvb[b, HD : HD + TOK, :],
                (((1,), (1,)), ((), ())),
                preferred_element_type=F32,
            )
            acc[rows, :] = acc[rows, :] * jnp.exp2(old - new) + update
            peak[rows, :] = new

    attend(0, 0)
    twin_copy(0, 0).wait_recv()
    twin_copy(0, 1).wait_recv()
    attend(0, 1)
    for h in range(2):
        ring_own[h][0].wait_recv()
        if h == 0:
            ring_on[0].start()
        twin_copy(3, h).start()
        ring_own[h][1].wait_recv()
        if h == 1:
            ring_on[1].start()
        twin_copy(1, h).start()
    attend(3, 0)
    attend(1, 0)
    for dx in (3, 1):
        twin_copy(dx, 0).wait_recv()
        twin_copy(dx, 1).wait_recv()
        attend(dx, 1)
    for h in range(2):
        ring_on[h].wait_recv()
        twin_copy(2, h).start()
    attend(2, 0)
    twin_copy(2, 0).wait_recv()
    twin_copy(2, 1).wait_recv()
    attend(2, 1)

    def o_copy(i, start):
        exchange(
            i,
            o_send.at[i],
            heads_t.at[pl.ds(pl.multiple_of(slot * HD, HD), HD), :],
            o_ss.at[i],
            o_rs.at[slot],
            start,
        )

    @pl.loop(0, 8)
    def _(i):
        rows = pl.ds(pl.multiple_of(i * TOK, TOK), TOK)
        turned = acc[rows, :].T
        o_send[i] = (turned[0:HD, :] / turned[HD : HD + 1, :]).astype(BF16)
        o_copy(i, True)

    weight_copies[3].wait()

    @pl.loop(0, 8)
    def _(i):
        remote(
            o_send.at[i],
            heads_t.at[pl.ds(pl.multiple_of(i * HD, HD), HD), :],
            o_ss.at[i],
            o_rs.at[i],
            mate(i),
        ).wait_recv()

    heads = heads_t[...].astype(F32).T.astype(BF16)
    proj = dot(heads, ow_buf[...])
    proj_send[...] = proj.astype(BF16)
    proj_copy = remote(proj_send, proj_recv, proj_sem.at[0], proj_sem.at[1], twin)
    proj_copy.start()

    row_ids = lax.broadcasted_iota(jnp.int32, (2 * EXPERTS * CAP, TOK), 0).astype(F32)
    turned = [jnp.broadcast_to(place[k], (TOK, TOK)).T[0:1, :] for k in range(2)]
    low = jnp.logical_or(row_ids == turned[0], row_ids == turned[1])
    high = jnp.logical_or(row_ids == turned[0] + CAP, row_ids == turned[1] + CAP)
    spread = jnp.concatenate([low.astype(F32).astype(BF16), high.astype(F32).astype(BF16)], axis=1)

    proj_copy.wait_recv()
    hidden = tokens[...].astype(F32) + proj + proj_recv[...].astype(F32)
    inverse = lax.rsqrt(jnp.mean(hidden * hidden, axis=1, keepdims=True) + EPS)
    moe = hidden * inverse * norm_moe[...]
    y_own[0, 0:TOK, :] = hidden[:, 0:HALF]
    y_own[1, 0:TOK, :] = hidden[:, HALF:]
    moe_half[2] = y_own[c, 0:TOK, :]
    moe_half[0] = moe[:, 0:HALF]
    moe_half[1] = moe[:, HALF:]
    mine = moe_half[c].astype(BF16)
    stacked = jnp.concatenate([mine[:, 0:QUART], mine[:, QUART:]], axis=0)
    disp[...] = dot(spread, stacked).astype(BF16).reshape(EXPERTS, 2 * CAP, QUART)

    def plane_send(p, src, dst, send_sem, recv_sem):
        @pl.when(p != plane)
        def _():
            remote(src, dst, send_sem, recv_sem, plane_dev(p)).start()

        @pl.when(p == plane)
        def _():
            pltpu.make_async_copy(src, dst, recv_sem).start()

    for a in range(4):

        @pl.loop(0, 4)
        def _(b):
            p = ((z + a) % 4) * 4 + (y + b) % 4
            plane_send(p, disp.at[p], xbuf.at[0, c, plane], d_ss.at[p], d_rs.at[plane])

    def x_part(dx, core, a):
        return xbuf.at[dx, core, pl.ds(((z + 4 - a) % 4) * 4, 4)]

    def x_ring(to, src_dx, dst_dx, a):
        return remote(
            x_part(src_dx, c, a),
            x_part(dst_dx, c, a),
            xr_ss.at[dst_dx, a],
            xr_rs.at[dst_dx, a],
            right if to == 0 else left,
        )

    def x_twin(dx, a, arriving):
        core = 1 - c if arriving else c
        return remote(x_part(dx, core, a), x_part(dx, core, a), xt_ss.at[dx, a], xt_rs.at[dx, a], twin)

    for a in range(4):

        @pl.loop(0, 4)
        def _(b):
            p = ((z + 4 - a) % 4) * 4 + b
            remote(disp.at[p], xbuf.at[0, c, p], d_ss.at[p], d_rs.at[p], plane_dev(p)).wait_recv()

        x_ring(0, 0, 3, a).start()
        x_ring(1, 0, 1, a).start()
        x_twin(0, a, False).start()

    def y_copy(dx):
        return remote(y_send.at[dx], y_recv.at[dx], y_ss.at[dx], y_rs.at[dx], twin)

    def chunk(dx):
        for core in range(2):
            piece = xbuf[dx, core].astype(F32)
            for h in range(2):
                at = core * HALF + h * QUART
                rows_in[:, at : at + QUART] = (
                    piece[:, h * CAP : (h + 1) * CAP, :].reshape(EXPERTS * CAP, QUART).astype(BF16)
                )
        rows = rows_in[...]
        gate = dot(rows, wi_buf[0])
        up = dot(rows, wi_buf[1])
        active = (gate / (1.0 + jnp.exp(-gate)) * up).astype(BF16)
        y_send[dx] = dot(active, wd_buf[1 - c]).astype(BF16)
        y_copy(dx).start()
        y_own[dx] = dot(active, wd_buf[c])

    def settle(dx):
        y_copy(dx).wait_recv()
        total = (y_own[dx] + y_recv[dx].astype(F32)).reshape(EXPERTS, CAP, HALF)
        parts[dx, :, 0:CAP, :] = total[:, :, 0:QUART].astype(BF16)
        parts[dx, :, CAP:, :] = total[:, :, QUART:].astype(BF16)

    for copy in weight_copies[4:]:
        copy.wait()
    for a in range(4):
        x_twin(0, a, True).wait_recv()
    chunk(0)
    for a in range(4):
        x_ring(0, 0, 3, a).wait_recv()
        if a < 2:
            x_ring(0, 3, 2, a).start()
        x_twin(3, a, False).start()
        x_ring(1, 0, 1, a).wait_recv()
        if a >= 2:
            x_ring(1, 1, 2, a).start()
        x_twin(1, a, False).start()
    settle(0)

    def half(h):
        return pl.ds(8 * h, 8)

    def far_copy(h):
        return remote(
            parts.at[2, half(h)], diag_recv.at[h], r_ss.at[h], r_rs.at[h], right if h == 0 else left
        )

    def near_copy(dx, h):
        return remote(
            parts.at[dx, half(h)],
            side_recv.at[dx // 2, half(h)],
            r_ss.at[2 + (dx // 2) * 2 + h],
            r_rs.at[2 + (dx // 2) * 2 + h],
            right if dx == 1 else left,
        )

    for a in range(4):
        x_twin(3, a, True).wait_recv()
    chunk(3)
    for a in range(4):
        x_twin(1, a, True).wait_recv()
    chunk(1)
    settle(3)
    near_copy(3, 0).start()
    settle(1)
    near_copy(1, 1).start()
    for a in range(4):
        x_ring(0 if a < 2 else 1, 0, 2, a).wait_recv()
        x_twin(2, a, False).start()
    for a in range(4):
        x_twin(2, a, True).wait_recv()
    chunk(2)
    settle(2)
    far_copy(0).start()
    far_copy(1).start()
    far_copy(0).wait_recv()
    parts[1, 0:8] = (parts[1, 0:8].astype(F32) + diag_recv[0].astype(F32)).astype(BF16)
    near_copy(1, 0).start()
    far_copy(1).wait_recv()
    parts[3, 8:16] = (parts[3, 8:16].astype(F32) + diag_recv[1].astype(F32)).astype(BF16)
    near_copy(3, 1).start()
    for h in range(2):
        near_copy(1, h).wait_recv()
        near_copy(3, h).wait_recv()
        at = slice(8 * h, 8 * h + 8)
        back[at] = (
            parts[0, at].astype(F32) + side_recv[0, at].astype(F32) + side_recv[1, at].astype(F32)
        ).astype(BF16)

    @pl.loop(0, 16)
    def _(i):
        p = ((z + i // 4) % 4) * 4 + (y + i) % 4
        plane_send(p, back.at[p], ret.at[plane], b_ss.at[p], b_rs.at[plane])

    col_ids = lax.broadcasted_iota(jnp.int32, (TOK, 2 * EXPERTS * CAP), 1).astype(F32)
    picks = jnp.concatenate(
        [
            (col_ids == place[k] + float(h * CAP)).astype(F32).astype(BF16)
            for k in range(2)
            for h in range(2)
        ],
        axis=0,
    )

    @pl.loop(0, 16)
    def _(p):
        remote(back.at[p], ret.at[p], b_ss.at[p], b_rs.at[p], plane_dev(p)).wait_recv()

    picked = dot(picks, ret[...].reshape(2 * EXPERTS * CAP, QUART))
    for h in range(2):
        cols = slice(h * QUART, (h + 1) * QUART)
        first = picked[h * TOK : (h + 1) * TOK]
        second = picked[(2 + h) * TOK : (3 + h) * TOK]
        out[:, cols] = (
            moe_half[2, :, cols] + route_weight[:, 0:1] * first + route_weight[:, 1:2] * second
        ).astype(BF16)

    @pl.loop(0, 8)
    def _(i):
        kv_copy(i, False)
        q_copy(i, False)
        o_copy(i, False)

    for h in range(2):
        ring_own[h][0].wait_send()
        ring_own[h][1].wait_send()
        ring_on[h].wait_send()
        for dx in range(4):
            twin_copy(dx, h).wait_send()
    proj_copy.wait_send()

    @pl.loop(0, 16)
    def _(p):
        @pl.when(p != plane)
        def _():
            remote(disp.at[p], xbuf.at[0, c, plane], d_ss.at[p], d_rs.at[plane], plane_dev(p)).wait_send()
            remote(back.at[p], ret.at[plane], b_ss.at[p], b_rs.at[plane], plane_dev(p)).wait_send()

    for a in range(4):
        x_ring(0, 0, 3, a).wait_send()
        x_ring(1, 0, 1, a).wait_send()
        (x_ring(0, 3, 2, a) if a < 2 else x_ring(1, 1, 2, a)).wait_send()
        for dx in range(4):
            x_twin(dx, a, False).wait_send()
    for dx in range(4):
        y_copy(dx).wait_send()
    for h in range(2):
        far_copy(h).wait_send()
        near_copy(1, h).wait_send()
        near_copy(3, h).wait_send()


def on_device(
    tokens,
    attn_weight,
    out_weight,
    norm_attn,
    norm_moe,
    routes,
    route_weight,
    expert_in,
    expert_out,
):
    vmem = pl.BlockSpec(memory_space=pltpu.VMEM)
    hbm = pl.BlockSpec(memory_space=pl.ANY)
    dma = pltpu.SemaphoreType.DMA
    pairs = (EXPERTS, 2 * CAP, QUART)
    scratch = [
        pltpu.VMEM((3, D, HALF), BF16),
        pltpu.VMEM((HALF, D), BF16),
        pltpu.VMEM((2, D, HALF), BF16),
        pltpu.VMEM((2, HALF, HALF), BF16),
        dma((7,)),
        pltpu.VMEM((8, 2 * HD, TOK), BF16),
        pltpu.VMEM((8, HD, TOK), BF16),
        pltpu.VMEM((HD, 8 * TOK), BF16),
        pltpu.VMEM((8, 2 * HD + 32, 8 * TOK), BF16),
        pltpu.VMEM((8 * TOK, TOK), BF16),
        pltpu.VMEM((8 * TOK, TOK), F32),
        pltpu.VMEM((8 * TOK, TOK), F32),
        pltpu.VMEM((8, HD, TOK), BF16),
        pltpu.VMEM((HALF, TOK), BF16),
        pltpu.VMEM((TOK, D), BF16),
        pltpu.VMEM((TOK, D), BF16),
        pltpu.VMEM((3, TOK, HALF), F32),
        pltpu.VMEM(pairs, BF16),
        pltpu.VMEM((4, 2) + pairs, BF16),
        pltpu.VMEM((EXPERTS * CAP, D), BF16),
        pltpu.VMEM((4, EXPERTS * CAP, HALF), F32),
        pltpu.VMEM((4, EXPERTS * CAP, HALF), BF16),
        pltpu.VMEM((4, EXPERTS * CAP, HALF), BF16),
        pltpu.VMEM((4,) + pairs, BF16),
        pltpu.VMEM((2, 8, 2 * CAP, QUART), BF16),
        pltpu.VMEM((2,) + pairs, BF16),
        pltpu.VMEM(pairs, BF16),
        pltpu.VMEM(pairs, BF16),
        dma((8,)),
        dma((8,)),
        dma((8,)),
        dma((8,)),
        dma((4, 2)),
        dma((4, 2)),
        dma((4, 2)),
        dma((4, 2)),
        dma((8,)),
        dma((8,)),
        dma((2,)),
        dma((16,)),
        dma((16,)),
        dma((4, 4)),
        dma((4, 4)),
        dma((4, 4)),
        dma((4, 4)),
        dma((4,)),
        dma((4,)),
        dma((6,)),
        dma((6,)),
        dma((16,)),
        dma((16,)),
    ]
    return pl.pallas_call(
        layer_kernel,
        out_shape=jax.ShapeDtypeStruct((TOK, HALF), BF16),
        in_specs=[vmem, hbm, hbm, vmem, vmem, vmem, vmem, hbm, hbm],
        out_specs=vmem,
        scratch_shapes=scratch,
        compiler_params=pltpu.CompilerParams(
            collective_id=0, has_side_effects=True, vmem_limit_bytes=60 * 1024 * 1024
        ),
        cost_estimate=pl.CostEstimate(
            flops=30_000_000_000, bytes_accessed=17_000_000, transcendentals=9_000_000
        ),
    )(
        tokens,
        attn_weight,
        out_weight,
        norm_attn.reshape(1, D),
        norm_moe.reshape(1, D),
        routes,
        route_weight,
        expert_in,
        expert_out,
    )


def solution(mesh):
    return jax.shard_map(
        on_device,
        mesh=mesh,
        in_specs=(
            P("seq", None),
            P(None, None, "tensor"),
            P("tensor", None),
            P(),
            P(),
            P("seq", None),
            P("seq", None),
            P("seq", None, None, "tensor"),
            P("seq", "tensor", None),
        ),
        out_specs=P("seq", "tensor"),
        check_vma=False,
    )
```

```python
import math

import jax
import jax.numpy as jnp
from jax import lax
from jax.experimental import pallas as pl
from jax.experimental.pallas import tpu as pltpu
from jax.sharding import PartitionSpec as P

MESH = pl.DeviceIdType.MESH
D = 1536
HALF = 768
BULK = 512
REST = 256
ORDER = (2, 1, 3, 0)
FAR_FIRST = sorted(
    ((a, b) for a in range(4) for b in range(4)),
    key=lambda o: -(min(o[0], 4 - o[0]) + min(o[1], 4 - o[1])),
)
HD = 96
TOK = 128
EXPERTS = 16
CAP = 24
EPS = 1e-6
F32 = jnp.float32
BF16 = jnp.bfloat16
SCALE = HD ** (-0.5) * math.log2(math.e)


def dot(a, b):
    return jnp.dot(a, b, preferred_element_type=F32)


def remote(src, dst, send_sem, recv_sem, device):
    return pltpu.make_async_remote_copy(
        src_ref=src,
        dst_ref=dst,
        send_sem=send_sem,
        recv_sem=recv_sem,
        device_id=device,
        device_id_type=MESH,
    )


def layer_kernel(
    tokens,
    attn_w,
    out_w,
    norm_attn,
    norm_moe,
    routes,
    route_weight,
    expert_in,
    expert_out,
    out,
    w_buf,
    ow_buf,
    wd_buf,
    w_sem,
    kv_send,
    q_send,
    q_t,
    kvb,
    k_nat,
    peak,
    acc,
    o_send,
    heads_t,
    proj_send,
    proj_recv,
    moe_half,
    info,
    tok_rest,
    disp_bulk,
    disp_wide,
    disp_rest,
    x_bulk,
    x_rest,
    rows_bulk,
    rows_rest,
    sums,
    y_send,
    y_recv,
    parts,
    diag_recv,
    side_recv,
    back,
    ret,
    rest_send,
    rest_recv,
    sum_send,
    sum_recv,
    kv_ss,
    kv_rs,
    q_ss,
    q_rs,
    ring_ss,
    ring_rs,
    twin_ss,
    twin_rs,
    o_ss,
    o_rs,
    proj_sem,
    info_ss,
    info_rs,
    tok_ss,
    tok_rs,
    d_ss,
    d_rs,
    e_ss,
    e_rs,
    xr_ss,
    xr_rs,
    xt_ss,
    xt_rs,
    xe_ss,
    xe_rs,
    y_ss,
    y_rs,
    r_ss,
    r_rs,
    rest_ss,
    rest_rs,
    sum_ss,
    sum_rs,
    b_ss,
    b_rs,
):
    s = lax.axis_index("seq")
    c = lax.axis_index("tensor")
    x = s % 4
    plane = s // 4
    z = plane // 4
    y = plane % 4
    side = z // 2
    slot = (z % 2) * 4 + y
    left = (s - x + (x + 3) % 4, c)
    right = (s - x + (x + 1) % 4, c)
    twin = (s, 1 - c)

    def along(dx):
        return (s - x + (x + dx) % 4, c)

    def mate(i):
        return ((2 * c + i // 4) * 16 + (i % 4) * 4 + x, side)

    def is_me(i):
        return jnp.logical_and(c == side, i == slot)

    def plane_dev(p):
        return (p * 4 + x, c)

    weight_copies = [
        pltpu.make_async_copy(attn_w.at[1], w_buf.at[1], w_sem.at[1]),
        pltpu.make_async_copy(attn_w.at[2], w_buf.at[2], w_sem.at[2]),
        pltpu.make_async_copy(attn_w.at[0], w_buf.at[0], w_sem.at[0]),
        pltpu.make_async_copy(out_w, ow_buf, w_sem.at[3]),
        pltpu.make_async_copy(expert_out.at[0, :, pl.ds(0, HALF)], wd_buf.at[0], w_sem.at[4]),
        pltpu.make_async_copy(expert_out.at[0, :, pl.ds(HALF, HALF)], wd_buf.at[1], w_sem.at[5]),
    ]
    moves = (
        (0, 0, BULK),
        (HALF, BULK, BULK),
        (BULK, 2 * BULK, REST),
        (HALF + BULK, 2 * BULK + REST, REST),
    )
    weight_copies += [
        pltpu.make_async_copy(
            expert_in.at[0, k, pl.ds(start, rows)],
            w_buf.at[1 + k, pl.ds(to, rows)],
            w_sem.at[6 + 4 * k + i],
        )
        for k in range(2)
        for i, (start, to, rows) in enumerate(moves)
    ]
    for copy in weight_copies[:3]:
        copy.start()

    barrier = pltpu.get_barrier_semaphore()

    def greet(device):
        pl.semaphore_signal(barrier, inc=1, device_id=device, device_id_type=MESH)

    for device in (left, right, along(2), twin):
        greet(device)

    @pl.loop(0, 8)
    def _(i):
        @pl.when(jnp.logical_not(is_me(i)))
        def _():
            greet(mate(i))

    @pl.loop(0, 16)
    def _(p):
        @pl.when(p != plane)
        def _():
            greet(plane_dev(p))

    tok = tokens[...].astype(F32)
    mean_square = jnp.mean(tok * tok, axis=1, keepdims=True)
    normed = (tok * lax.rsqrt(mean_square + EPS) * norm_attn[...].reshape(1, D)).astype(BF16)

    def exchange(i, src, dst, send_sem, recv_sem, start):
        copy = remote(src, dst, send_sem, recv_sem, mate(i))

        @pl.when(jnp.logical_not(is_me(i)))
        def _():
            if start:
                copy.start()
            else:
                copy.wait_send()

        if start:

            @pl.when(is_me(i))
            def _():
                pltpu.make_async_copy(src, dst, recv_sem).start()

    def far(a):
        return (z + jnp.where(c == side, 1, 0) + a) % 2

    def lanes(i):
        return pl.ds(pl.multiple_of(i * TOK, TOK), TOK)

    def kv_copy(h, i, start):
        exchange(
            i,
            kv_send.at[h, i],
            kvb.at[0, pl.ds(h * HD, HD), lanes(slot)],
            kv_ss.at[h, i],
            kv_rs.at[h, slot],
            start,
        )

    def q_copy(i, start):
        exchange(i, q_send.at[i], q_t.at[pl.ds(0, HD), lanes(slot)], q_ss.at[i], q_rs.at[slot], start)

    for h in range(2):
        weight_copies[h].wait()
        kv_send[h] = dot(normed, w_buf[1 + h]).T.astype(BF16).reshape(8, HD, TOK)
        if h == 0:
            pl.semaphore_wait(barrier, 4 + 15 + 8 - jnp.where(c == side, 1, 0))

        for b in ORDER:

            @pl.loop(0, 2)
            def _(a):
                kv_copy(h, far(a) * 4 + (y + b) % 4, True)

    weight_copies[2].wait()
    q_send[...] = (dot(normed, w_buf[0]) * SCALE).T.astype(BF16).reshape(8, HD, TOK)
    for b in ORDER:

        @pl.loop(0, 2)
        def _(a):
            q_copy(far(a) * 4 + (y + b) % 4, True)

    for copy in weight_copies[3:]:
        copy.start()

    @pl.loop(0, 8)
    def _(b):
        kvb[b, 2 * HD : 2 * HD + 32, :] = jnp.ones((32, 8 * TOK), BF16)

    peak[...] = jnp.full(peak.shape, -1e30, F32)
    acc[...] = jnp.zeros(acc.shape, F32)
    q_t[HD:, :] = jnp.zeros((TOK - HD, 8 * TOK), BF16)

    expert_ids = lax.broadcasted_iota(jnp.int32, (EXPERTS, TOK), 0)
    hot = [(routes[k : k + 1, :] == expert_ids).astype(F32) for k in range(2)]
    earlier = (
        lax.broadcasted_iota(jnp.int32, (TOK, TOK), 0)
        < lax.broadcasted_iota(jnp.int32, (TOK, TOK), 1)
    ).astype(BF16)
    before = dot((hot[0] + hot[1]).astype(BF16), earlier)
    place = [
        jnp.sum(before * hot[k], axis=0, keepdims=True)
        + routes[k : k + 1, :].astype(F32) * float(CAP)
        for k in range(2)
    ]
    info[0] = jnp.zeros((8, TOK), F32)
    for k in range(2):
        info[0, k : k + 1, :] = place[k]
        info[0, 2 + k : 3 + k, :] = route_weight[k : k + 1, :]

    def to_line(ref, send_sem, recv_sem, dx):
        return remote(
            ref.at[0], ref.at[4 - dx], send_sem.at[dx], recv_sem.at[4 - dx], along(dx)
        )

    for dx in (2, 1, 3):
        to_line(info, info_ss, info_rs, dx).start()

    def kv_part(dx, dc, h):
        return kvb.at[2 * dx + dc, pl.ds(h * HD, HD)]

    def ring_copy(to, src_dx, dst_dx, h):
        device = right if to == 0 else left
        return remote(
            kv_part(src_dx, 0, h),
            kv_part(dst_dx, 0, h),
            ring_ss.at[dst_dx, h],
            ring_rs.at[dst_dx, h],
            device,
        )

    def twin_copy(dx, h):
        return remote(kv_part(dx, 0, h), kv_part(dx, 1, h), twin_ss.at[dx, h], twin_rs.at[dx, h], twin)

    ring_own = [[ring_copy(0, 0, 3, h), ring_copy(1, 0, 1, h)] for h in range(2)]
    ring_on = [ring_copy(0, 3, 2, 0), ring_copy(1, 1, 2, 1)]
    for h in range(2):

        @pl.loop(0, 8)
        def _(i):
            remote(
                kv_send.at[h, i],
                kvb.at[0, pl.ds(h * HD, HD), lanes(i)],
                kv_ss.at[h, i],
                kv_rs.at[h, i],
                mate(i),
            ).wait_recv()

        ring_own[h][0].start()
        ring_own[h][1].start()
        twin_copy(0, h).start()

    @pl.loop(0, 8)
    def _(i):
        remote(
            q_send.at[i], q_t.at[pl.ds(0, HD), lanes(i)], q_ss.at[i], q_rs.at[i], mate(i)
        ).wait_recv()

    def attend(dx, dc):
        b = 2 * dx + dc

        k_nat[...] = kvb[b, 0:TOK, :].astype(F32).T.astype(BF16)
        scores = dot(k_nat[...], q_t[...])
        old = peak[...]
        new = jnp.maximum(old, jnp.max(scores, axis=0, keepdims=True))
        probs = jnp.exp2(scores - new).astype(BF16)
        update = dot(kvb[b, HD : HD + TOK, :], probs)
        acc[...] = acc[...] * jnp.exp2(old - new) + update
        peak[...] = new

    attend(0, 0)
    ring_own[0][0].wait_recv()
    ring_on[0].start()
    twin_copy(3, 0).start()
    ring_own[0][1].wait_recv()
    twin_copy(1, 0).start()
    twin_copy(0, 0).wait_recv()
    twin_copy(0, 1).wait_recv()
    attend(0, 1)
    ring_own[1][1].wait_recv()
    ring_on[1].start()
    twin_copy(1, 1).start()
    ring_own[1][0].wait_recv()
    twin_copy(3, 1).start()
    attend(3, 0)
    attend(1, 0)
    for dx in (3, 1):
        twin_copy(dx, 0).wait_recv()
        twin_copy(dx, 1).wait_recv()
        attend(dx, 1)
    for h in range(2):
        ring_on[h].wait_recv()
        twin_copy(2, h).start()
    attend(2, 0)
    twin_copy(2, 0).wait_recv()
    twin_copy(2, 1).wait_recv()
    attend(2, 1)

    def o_copy(i, start):
        exchange(
            i,
            o_send.at[i],
            heads_t.at[pl.ds(pl.multiple_of(slot * HD, HD), HD), :],
            o_ss.at[i],
            o_rs.at[slot],
            start,
        )

    @pl.loop(0, 8)
    def _(i):
        o_send[i] = (acc[0:HD, lanes(i)] / acc[HD : HD + 1, lanes(i)]).astype(BF16)
        o_copy(i, True)

    weight_copies[3].wait()

    @pl.loop(0, 8)
    def _(i):
        remote(
            o_send.at[i],
            heads_t.at[pl.ds(pl.multiple_of(i * HD, HD), HD), :],
            o_ss.at[i],
            o_rs.at[i],
            mate(i),
        ).wait_recv()

    heads = heads_t[...].astype(F32).T.astype(BF16)
    proj = dot(heads, ow_buf[...])
    proj_send[...] = proj.astype(BF16)
    proj_copy = remote(proj_send, proj_recv, proj_sem.at[0], proj_sem.at[1], twin)
    proj_copy.start()

    def spread(dx):
        ids = lax.broadcasted_iota(jnp.int32, (EXPERTS * CAP, TOK), 0).astype(F32)
        hit = jnp.logical_or(ids == info[dx, 0:1, :], ids == info[dx, 1:2, :])
        return hit.astype(F32).astype(BF16)

    def column(row):
        return jnp.broadcast_to(row, (TOK, TOK)).T[:, 0:1]

    def combine(dx, table):
        ids = lax.broadcasted_iota(jnp.int32, (TOK, EXPERTS * CAP), 1).astype(F32)
        total = None
        for k in range(2):
            picks = (ids == column(info[dx, k : k + 1, :])).astype(F32).astype(BF16)
            term = dot(picks, table) * column(info[dx, 2 + k : 3 + k, :])
            total = term if total is None else total + term
        return total

    for dx in (1, 3, 2):
        to_line(info, info_ss, info_rs, 4 - dx).wait_recv()
    proj_copy.wait_recv()
    hidden = tokens[...].astype(F32) + proj + proj_recv[...].astype(F32)
    inverse = lax.rsqrt(jnp.mean(hidden * hidden, axis=1, keepdims=True) + EPS)
    moe = hidden * inverse * norm_moe[...].reshape(1, D)
    sums[0, 0, 0:TOK, :] = hidden[:, 0:HALF]
    sums[0, 1, 0:TOK, :] = hidden[:, HALF:]
    moe_half[2] = sums[0, c, 0:TOK, :]
    moe_half[0] = moe[:, 0:HALF]
    moe_half[1] = moe[:, HALF:]
    mine = moe_half[c].astype(BF16)

    tok_rest[0] = mine[:, BULK:]
    for dx in (2, 1, 3):
        to_line(tok_rest, tok_ss, tok_rs, dx).start()
    own = spread(0)
    rows = dot(own, mine[:, 0:BULK]).reshape(EXPERTS, CAP, BULK)
    disp_bulk[:, 0:CAP, :] = rows[:, :, 0:REST].astype(BF16)
    disp_bulk[:, CAP:, :] = rows[:, :, REST:].astype(BF16)

    def over_plane(a, b, src, dst, send_sem, recv_sem):
        p = ((z + a) % 4) * 4 + (y + b) % 4
        if a == 0 and b == 0:
            return pltpu.make_async_copy(src.at[p], dst.at[plane], recv_sem.at[plane])
        return remote(src.at[p], dst.at[plane], send_sem.at[p], recv_sem.at[plane], plane_dev(p))

    def bulk_copy(a, b):
        return over_plane(a, b, disp_bulk, x_bulk.at[0, c], d_ss, d_rs)

    def rest_copy(a, b):
        return over_plane(a, b, disp_rest, x_rest.at[c], e_ss, e_rs)

    for a, b in FAR_FIRST:
        bulk_copy(a, b).start()
    disp_wide[:, 0:CAP, :] = dot(own, tok_rest[0]).reshape(EXPERTS, CAP, REST)
    for dx in (1, 3, 2):
        to_line(tok_rest, tok_ss, tok_rs, 4 - dx).wait_recv()
        disp_wide[:, dx * CAP : (dx + 1) * CAP, :] = dot(spread(dx), tok_rest[dx]).reshape(
            EXPERTS, CAP, REST
        )
    disp_rest[...] = disp_wide[...].astype(BF16)
    for a, b in FAR_FIRST:
        rest_copy(a, b).start()

    def group(a):
        return pl.ds(((z + 4 - a) % 4) * 4, 4)

    def x_ring(to, src_dx, dst_dx, a):
        return remote(
            x_bulk.at[src_dx, c, group(a)],
            x_bulk.at[dst_dx, c, group(a)],
            xr_ss.at[dst_dx, a],
            xr_rs.at[dst_dx, a],
            right if to == 0 else left,
        )

    def x_twin(dx, a, arriving):
        part = x_bulk.at[dx, 1 - c if arriving else c, group(a)]
        return remote(part, part, xt_ss.at[dx, a], xt_rs.at[dx, a], twin)

    def rest_twin(a, arriving):
        part = x_rest.at[1 - c if arriving else c, group(a)]
        return remote(part, part, xe_ss.at[a], xe_rs.at[a], twin)

    def wait_group(a, src, dst, send_sem, recv_sem):
        @pl.loop(0, 4)
        def _(b):
            p = ((z + 4 - a) % 4) * 4 + b
            remote(src.at[p], dst.at[p], send_sem.at[p], recv_sem.at[p], plane_dev(p)).wait_recv()

    for a in ORDER:
        wait_group(a, disp_bulk, x_bulk.at[0, c], d_ss, d_rs)
        x_ring(0, 0, 3, a).start()
        x_ring(1, 0, 1, a).start()
        x_twin(0, a, False).start()

    def y_copy(dx):
        return remote(y_send.at[dx], y_recv.at[dx], y_ss.at[dx], y_rs.at[dx], twin)

    def first_part(dx):
        for a in ORDER:
            x_twin(dx, a, True).wait_recv()
        for core in range(2):
            piece = x_bulk[dx, core].astype(F32)
            for h in range(2):
                at = core * BULK + h * REST
                rows_bulk[:, at : at + REST] = (
                    piece[:, h * CAP : (h + 1) * CAP, :].reshape(EXPERTS * CAP, REST).astype(BF16)
                )
        for k in range(2):
            sums[dx, k] = dot(rows_bulk[...], w_buf[1 + k, 0 : 2 * BULK, :])

    def second_part(dx):
        for core in range(2):
            wide = x_rest[core].astype(F32)
            rows_rest[:, core * REST : (core + 1) * REST] = (
                wide[:, dx * CAP : (dx + 1) * CAP, :].reshape(EXPERTS * CAP, REST).astype(BF16)
            )
        rows = rows_rest[...]
        gate = sums[dx, 0] + dot(rows, w_buf[1, 2 * BULK :, :])
        up = sums[dx, 1] + dot(rows, w_buf[2, 2 * BULK :, :])
        active = (gate / (1.0 + jnp.exp(-gate)) * up).astype(BF16)
        y_send[dx] = dot(active, wd_buf[1 - c]).astype(BF16)
        y_copy(dx).start()
        sums[dx, 0] = dot(active, wd_buf[c])

    def settle(dx):
        y_copy(dx).wait_recv()
        total = (sums[dx, 0] + y_recv[dx].astype(F32)).reshape(EXPERTS, CAP, HALF)
        parts[dx, :, 0:CAP, :] = total[:, :, 0:REST].astype(BF16)
        parts[dx, :, CAP:, :] = total[:, :, REST:BULK].astype(BF16)
        pair, at = (0 if dx >= 2 else 1), (0 if dx in (2, 1) else CAP)
        rest_send[pair, :, at : at + CAP, :] = total[:, :, BULK:].astype(BF16)

    for copy in weight_copies[4:]:
        copy.wait()
    first_part(0)
    for i, a in enumerate(ORDER):
        x_ring(0, 0, 3, a).wait_recv()
        if i < 2:
            x_ring(0, 3, 2, a).start()
        x_twin(3, a, False).start()
        x_ring(1, 0, 1, a).wait_recv()
        if i >= 2:
            x_ring(1, 1, 2, a).start()
        x_twin(1, a, False).start()
    first_part(3)
    first_part(1)
    for a in ORDER:
        wait_group(a, disp_rest, x_rest.at[c], e_ss, e_rs)
        rest_twin(a, False).start()
    for i, a in enumerate(ORDER):
        x_ring(0 if i < 2 else 1, 0, 2, a).wait_recv()
        x_twin(2, a, False).start()
    first_part(2)
    for a in ORDER:
        rest_twin(a, True).wait_recv()

    def half(h):
        return pl.ds(8 * h, 8)

    def far_copy(h):
        return remote(
            parts.at[2, half(h)], diag_recv.at[h], r_ss.at[h], r_rs.at[h], right if h == 0 else left
        )

    def near_copy(dx, h):
        return remote(
            parts.at[dx, half(h)],
            side_recv.at[dx // 2, half(h)],
            r_ss.at[2 + (dx // 2) * 2 + h],
            r_rs.at[2 + (dx // 2) * 2 + h],
            right if dx == 1 else left,
        )

    def rest_back(pair, a, b):
        return over_plane(
            a, b, rest_send.at[pair], rest_recv.at[pair], rest_ss.at[pair], rest_rs.at[pair]
        )

    def back_copy(a, b):
        return over_plane(a, b, back, ret, b_ss, b_rs)

    def sum_copy(dx):
        return remote(
            sum_send.at[dx], sum_recv.at[4 - dx], sum_ss.at[dx], sum_rs.at[4 - dx], along(dx)
        )

    second_part(2)
    second_part(3)
    settle(2)
    far_copy(0).start()
    far_copy(1).start()
    settle(3)
    near_copy(3, 0).start()
    for a, b in FAR_FIRST:
        rest_back(0, a, b).start()
    second_part(1)
    second_part(0)
    settle(1)
    near_copy(1, 1).start()
    settle(0)
    for a, b in FAR_FIRST:
        rest_back(1, a, b).start()
    far_copy(0).wait_recv()
    parts[1, 0:8] = (parts[1, 0:8].astype(F32) + diag_recv[0].astype(F32)).astype(BF16)
    near_copy(1, 0).start()
    far_copy(1).wait_recv()
    parts[3, 8:16] = (parts[3, 8:16].astype(F32) + diag_recv[1].astype(F32)).astype(BF16)
    near_copy(3, 1).start()

    def rest_sums(pair):
        @pl.loop(0, 16)
        def _(p):
            remote(
                rest_send.at[pair, p],
                rest_recv.at[pair, p],
                rest_ss.at[pair, p],
                rest_rs.at[pair, p],
                plane_dev(p),
            ).wait_recv()

        both = rest_recv[pair].astype(F32)
        found = []
        for i, dx in enumerate((2, 3) if pair == 0 else (1, 0)):
            table = both[:, i * CAP : (i + 1) * CAP, :].reshape(EXPERTS * CAP, REST).astype(BF16)
            found.append(combine(dx, table))
        return found

    found = rest_sums(0)
    for i, dx in enumerate((2, 3)):
        sum_send[dx] = found[i].astype(BF16)
        sum_copy(dx).start()
    for h in range(2):
        near_copy(1, h).wait_recv()
        near_copy(3, h).wait_recv()
        at = slice(8 * h, 8 * h + 8)
        back[at] = (
            parts[0, at].astype(F32) + side_recv[0, at].astype(F32) + side_recv[1, at].astype(F32)
        ).astype(BF16)
    for a, b in FAR_FIRST:
        back_copy(a, b).start()
    found = rest_sums(1)
    sum_send[1] = found[0].astype(BF16)
    sum_copy(1).start()
    rest = moe_half[2, :, BULK:] + found[1]
    for dx in (2, 1, 3):
        sum_copy(4 - dx).wait_recv()
        rest = rest + sum_recv[dx].astype(F32)
    out[:, BULK:] = rest.astype(BF16)

    @pl.loop(0, 16)
    def _(p):
        remote(back.at[p], ret.at[p], b_ss.at[p], b_rs.at[p], plane_dev(p)).wait_recv()

    both = ret[...].astype(F32)
    for h in range(2):
        cols = slice(h * REST, (h + 1) * REST)
        table = both[:, h * CAP : (h + 1) * CAP, :].reshape(EXPERTS * CAP, REST).astype(BF16)
        out[:, cols] = (moe_half[2, :, cols] + combine(0, table)).astype(BF16)

    @pl.loop(0, 8)
    def _(i):
        kv_copy(0, i, False)
        kv_copy(1, i, False)
        q_copy(i, False)
        o_copy(i, False)

    for h in range(2):
        ring_own[h][0].wait_send()
        ring_own[h][1].wait_send()
        ring_on[h].wait_send()
        for dx in range(4):
            twin_copy(dx, h).wait_send()
    proj_copy.wait_send()

    for a, b in FAR_FIRST[:15]:
        bulk_copy(a, b).wait_send()
        rest_copy(a, b).wait_send()
        rest_back(0, a, b).wait_send()
        rest_back(1, a, b).wait_send()
        back_copy(a, b).wait_send()
    for dx in (1, 2, 3):
        to_line(info, info_ss, info_rs, dx).wait_send()
        to_line(tok_rest, tok_ss, tok_rs, dx).wait_send()
        sum_copy(dx).wait_send()
    for i, a in enumerate(ORDER):
        x_ring(0, 0, 3, a).wait_send()
        x_ring(1, 0, 1, a).wait_send()
        (x_ring(0, 3, 2, a) if i < 2 else x_ring(1, 1, 2, a)).wait_send()
        for dx in range(4):
            x_twin(dx, a, False).wait_send()
        rest_twin(a, False).wait_send()
    for dx in range(4):
        y_copy(dx).wait_send()
    for h in range(2):
        far_copy(h).wait_send()
        near_copy(1, h).wait_send()
        near_copy(3, h).wait_send()


def on_device(
    tokens,
    attn_weight,
    out_weight,
    norm_attn,
    norm_moe,
    routes,
    route_weight,
    expert_in,
    expert_out,
):
    vmem = pl.BlockSpec(memory_space=pltpu.VMEM)
    hbm = pl.BlockSpec(memory_space=pl.ANY)
    dma = pltpu.SemaphoreType.DMA
    pairs = (EXPERTS, 2 * CAP, REST)
    fours = (EXPERTS, 4 * CAP, REST)
    scratch = [
        pltpu.VMEM((3, D, HALF), BF16),
        pltpu.VMEM((HALF, D), BF16),
        pltpu.VMEM((2, HALF, HALF), BF16),
        dma((14,)),
        pltpu.VMEM((2, 8, HD, TOK), BF16),
        pltpu.VMEM((8, HD, TOK), BF16),
        pltpu.VMEM((TOK, 8 * TOK), BF16),
        pltpu.VMEM((8, 2 * HD + 32, 8 * TOK), BF16),
        pltpu.VMEM((8 * TOK, TOK), BF16),
        pltpu.VMEM((1, 8 * TOK), F32),
        pltpu.VMEM((TOK, 8 * TOK), F32),
        pltpu.VMEM((8, HD, TOK), BF16),
        pltpu.VMEM((HALF, TOK), BF16),
        pltpu.VMEM((TOK, D), BF16),
        pltpu.VMEM((TOK, D), BF16),
        pltpu.VMEM((3, TOK, HALF), F32),
        pltpu.VMEM((4, 8, TOK), F32),
        pltpu.VMEM((4, TOK, REST), BF16),
        pltpu.VMEM(pairs, BF16),
        pltpu.VMEM(fours, F32),
        pltpu.VMEM(fours, BF16),
        pltpu.VMEM((4, 2) + pairs, BF16),
        pltpu.VMEM((2,) + fours, BF16),
        pltpu.VMEM((EXPERTS * CAP, 2 * BULK), BF16),
        pltpu.VMEM((EXPERTS * CAP, 2 * REST), BF16),
        pltpu.VMEM((4, 2, EXPERTS * CAP, HALF), F32),
        pltpu.VMEM((4, EXPERTS * CAP, HALF), BF16),
        pltpu.VMEM((4, EXPERTS * CAP, HALF), BF16),
        pltpu.VMEM((4,) + pairs, BF16),
        pltpu.VMEM((2, 8, 2 * CAP, REST), BF16),
        pltpu.VMEM((2,) + pairs, BF16),
        pltpu.VMEM(pairs, BF16),
        pltpu.VMEM(pairs, BF16),
        pltpu.VMEM((2,) + pairs, BF16),
        pltpu.VMEM((2,) + pairs, BF16),
        pltpu.VMEM((4, TOK, REST), BF16),
        pltpu.VMEM((4, TOK, REST), BF16),
        dma((2, 8)),
        dma((2, 8)),
        dma((8,)),
        dma((8,)),
        dma((4, 2)),
        dma((4, 2)),
        dma((4, 2)),
        dma((4, 2)),
        dma((8,)),
        dma((8,)),
        dma((2,)),
        dma((4,)),
        dma((4,)),
        dma((4,)),
        dma((4,)),
        dma((16,)),
        dma((16,)),
        dma((16,)),
        dma((16,)),
        dma((4, 4)),
        dma((4, 4)),
        dma((4, 4)),
        dma((4, 4)),
        dma((4,)),
        dma((4,)),
        dma((4,)),
        dma((4,)),
        dma((6,)),
        dma((6,)),
        dma((2, 16)),
        dma((2, 16)),
        dma((4,)),
        dma((4,)),
        dma((16,)),
        dma((16,)),
    ]
    return pl.pallas_call(
        layer_kernel,
        out_shape=jax.ShapeDtypeStruct((TOK, HALF), BF16),
        in_specs=[vmem, hbm, hbm, vmem, vmem, vmem, vmem, hbm, hbm],
        out_specs=vmem,
        scratch_shapes=scratch,
        compiler_params=pltpu.CompilerParams(
            collective_id=0, has_side_effects=True, vmem_limit_bytes=60 * 1024 * 1024
        ),
        cost_estimate=pl.CostEstimate(
            flops=30_000_000_000, bytes_accessed=17_000_000, transcendentals=9_000_000
        ),
    )(
        tokens,
        attn_weight,
        out_weight,
        norm_attn,
        norm_moe,
        routes.T,
        route_weight.T,
        expert_in,
        expert_out,
    )


def solution(mesh):
    return jax.shard_map(
        on_device,
        mesh=mesh,
        in_specs=(
            P("seq", None),
            P(None, None, "tensor"),
            P("tensor", None),
            P(),
            P(),
            P("seq", None),
            P("seq", None),
            P("seq", None, None, "tensor"),
            P("seq", "tensor", None),
        ),
        out_specs=P("seq", "tensor"),
        check_vma=False,
    )
```

```python
import math

import jax
import jax.numpy as jnp
from jax import lax
from jax.experimental import pallas as pl
from jax.experimental.pallas import tpu as pltpu
from jax.sharding import PartitionSpec as P

MESH = pl.DeviceIdType.MESH
D = 1536
HALF = 768
BULK = 512
REST = 256
ORDER = (2, 1, 3, 0)
GROUPS = (0, 1, 3, 2)
HD = 96
TOK = 128
EXPERTS = 16
CAP = 24
EPS = 1e-6
F32 = jnp.float32
BF16 = jnp.bfloat16
SCALE = HD ** (-0.5) * math.log2(math.e)


def dot(a, b):
    return jnp.dot(a, b, preferred_element_type=F32)


def remote(src, dst, send_sem, recv_sem, device):
    return pltpu.make_async_remote_copy(
        src_ref=src,
        dst_ref=dst,
        send_sem=send_sem,
        recv_sem=recv_sem,
        device_id=device,
        device_id_type=MESH,
    )


def layer_kernel(
    tokens_in,
    attn_w,
    out_w,
    norm_attn_in,
    norm_moe_in,
    routes_in,
    route_weight_in,
    expert_in,
    expert_out,
    out,
    tokens,
    norm_attn,
    norm_moe,
    routes,
    route_weight,
    small_sem,
    w_buf,
    ow_buf,
    wd_buf,
    w_sem,
    normed_buf,
    kv_send,
    q_t,
    kvb,
    score_buf,
    top,
    peak,
    acc,
    o_send,
    heads_t,
    proj_send,
    proj_recv,
    moe_half,
    info,
    spread,
    picks,
    shares,
    tok_rest,
    disp_bulk,
    disp_wide,
    disp_rest,
    x_bulk,
    x_rest,
    rows_bulk,
    rows_rest,
    sums,
    y_send,
    y_recv,
    parts,
    diag_recv,
    side_recv,
    back,
    ret,
    rest_send,
    rest_recv,
    sum_send,
    sum_recv,
    kv_ss,
    kv_rs,
    q_ss,
    q_rs,
    ring_ss,
    ring_rs,
    twin_ss,
    twin_rs,
    o_ss,
    o_rs,
    proj_sem,
    info_ss,
    info_rs,
    tok_ss,
    tok_rs,
    d_ss,
    d_rs,
    e_ss,
    e_rs,
    xr_ss,
    xr_rs,
    xt_ss,
    xt_rs,
    xe_ss,
    xe_rs,
    y_ss,
    y_rs,
    r_ss,
    r_rs,
    rest_ss,
    rest_rs,
    sum_ss,
    sum_rs,
    b_ss,
    b_rs,
):
    s = lax.axis_index("seq")
    c = lax.axis_index("tensor")
    x = s % 4
    plane = s // 4
    z = plane // 4
    y = plane % 4
    side = z // 2
    slot = (z % 2) * 4 + y
    left = (s - x + (x + 3) % 4, c)
    right = (s - x + (x + 1) % 4, c)
    twin = (s, 1 - c)

    def along(dx):
        return (s - x + (x + dx) % 4, c)

    def mate(i):
        return ((2 * c + i // 4) * 16 + (i % 4) * 4 + x, side)

    def is_me(i):
        return jnp.logical_and(c == side, i == slot)

    def plane_dev(p):
        return (p * 4 + x, c)

    barrier = pltpu.get_barrier_semaphore()

    def greet(device):
        pl.semaphore_signal(barrier, inc=1, device_id=device, device_id_type=MESH)

    for device in (left, right, along(2), twin):
        greet(device)

    @pl.loop(0, 8)
    def _(i):
        @pl.when(jnp.logical_not(is_me(i)))
        def _():
            greet(mate(i))

    @pl.loop(0, 16)
    def _(p):
        @pl.when(p != plane)
        def _():
            greet(plane_dev(p))

    small = [
        pltpu.make_async_copy(src, dst, small_sem.at[i])
        for i, (src, dst) in enumerate(
            (
                (tokens_in, tokens),
                (norm_attn_in, norm_attn),
                (routes_in, routes),
                (route_weight_in, route_weight),
                (norm_moe_in, norm_moe),
            )
        )
    ]
    for copy in small:
        copy.start()

    weight_copies = [
        pltpu.make_async_copy(attn_w.at[1], w_buf.at[1], w_sem.at[1]),
        pltpu.make_async_copy(attn_w.at[2], w_buf.at[2], w_sem.at[2]),
        pltpu.make_async_copy(attn_w.at[0], w_buf.at[0], w_sem.at[0]),
        pltpu.make_async_copy(out_w, ow_buf, w_sem.at[3]),
        pltpu.make_async_copy(expert_out.at[0, :, pl.ds(0, HALF)], wd_buf.at[0], w_sem.at[4]),
        pltpu.make_async_copy(expert_out.at[0, :, pl.ds(HALF, HALF)], wd_buf.at[1], w_sem.at[5]),
    ]
    moves = (
        (0, 0, BULK),
        (HALF, BULK, BULK),
        (BULK, 2 * BULK, REST),
        (HALF + BULK, 2 * BULK + REST, REST),
    )
    weight_copies += [
        pltpu.make_async_copy(
            expert_in.at[0, k, pl.ds(start, rows)],
            w_buf.at[1 + k, pl.ds(to, rows)],
            w_sem.at[6 + 4 * k + i],
        )
        for k in range(2)
        for i, (start, to, rows) in enumerate(moves)
    ]
    for copy in weight_copies[:3]:
        copy.start()

    small[0].wait()
    small[1].wait()
    tok = tokens[...].astype(F32)
    mean_square = jnp.mean(tok * tok, axis=1, keepdims=True)
    normed_buf[...] = (tok * lax.rsqrt(mean_square + EPS) * norm_attn[...].reshape(1, D)).astype(BF16)

    def exchange(i, src, dst, send_sem, recv_sem, start):
        copy = remote(src, dst, send_sem, recv_sem, mate(i))

        @pl.when(jnp.logical_not(is_me(i)))
        def _():
            if start:
                copy.start()
            else:
                copy.wait_send()

        if start:

            @pl.when(is_me(i))
            def _():
                pltpu.make_async_copy(src, dst, recv_sem).start()

    def far(a):
        return (z + jnp.where(c == side, 1, 0) + a) % 2

    def lanes(i):
        return pl.ds(pl.multiple_of(i * TOK, TOK), TOK)

    def kv_copy(h, i, start):
        exchange(
            i,
            kv_send.at[h, i],
            kvb.at[0, pl.ds(h * HD, HD), lanes(slot)],
            kv_ss.at[h, i],
            kv_rs.at[h, slot],
            start,
        )

    def q_copy(i, start):
        exchange(i, kv_send.at[2, i], q_t.at[:, lanes(slot)], q_ss.at[i], q_rs.at[slot], start)

    @pl.loop(0, 3)
    def _(h):
        at = (h + 1) % 3
        pltpu.make_async_copy(attn_w.at[at], w_buf.at[at], w_sem.at[at]).wait()
        scale = jnp.where(h == 2, SCALE, 1.0)
        kv_send[h] = (dot(normed_buf[...], w_buf[at]) * scale).T.astype(BF16).reshape(8, HD, TOK)

    for copy in weight_copies[3:]:
        copy.start()

    @pl.loop(0, 8)
    def _(b):
        kvb[b, 2 * HD : 2 * HD + 32, :] = jnp.ones((32, 8 * TOK), BF16)

    peak[...] = jnp.full(peak.shape, -1e30, F32)
    acc[...] = jnp.zeros(acc.shape, F32)

    for copy in small[2:]:
        copy.wait()
    expert_ids = lax.broadcasted_iota(jnp.int32, (EXPERTS, TOK), 0)
    hot = [(routes[k : k + 1, :] == expert_ids).astype(F32) for k in range(2)]
    earlier = (
        lax.broadcasted_iota(jnp.int32, (TOK, TOK), 0)
        < lax.broadcasted_iota(jnp.int32, (TOK, TOK), 1)
    ).astype(BF16)
    before = dot((hot[0] + hot[1]).astype(BF16), earlier)
    place = [
        jnp.sum(before * hot[k], axis=0, keepdims=True)
        + routes[k : k + 1, :].astype(F32) * float(CAP)
        for k in range(2)
    ]
    info[0] = jnp.zeros((8, TOK), F32)
    for k in range(2):
        info[0, k : k + 1, :] = place[k]
        info[0, 2 + k : 3 + k, :] = route_weight[k : k + 1, :]

    pl.semaphore_wait(barrier, 4 + 15 + 8 - jnp.where(c == side, 1, 0))
    @pl.loop(0, 16)
    def _(i):
        kv_copy(i // 8, far(i) * 4 + (y + 2 + 3 * (i // 2)) % 4, True)

    @pl.loop(0, 8)
    def _(i):
        q_copy(far(i) * 4 + (y + 2 + 3 * (i // 2)) % 4, True)

    def to_line(ref, send_sem, recv_sem, dx):
        return remote(
            ref.at[0], ref.at[4 - dx], send_sem.at[dx], recv_sem.at[4 - dx], along(dx)
        )

    for dx in (2, 1, 3):
        to_line(info, info_ss, info_rs, dx).start()

    def kv_part(dx, dc, h):
        return kvb.at[2 * dx + dc, pl.ds(h * HD, HD)]

    def ring_copy(to, src_dx, dst_dx, h):
        device = right if to == 0 else left
        return remote(
            kv_part(src_dx, 0, h),
            kv_part(dst_dx, 0, h),
            ring_ss.at[dst_dx, h],
            ring_rs.at[dst_dx, h],
            device,
        )

    def twin_copy(dx, h):
        return remote(kv_part(dx, 0, h), kv_part(dx, 1, h), twin_ss.at[dx, h], twin_rs.at[dx, h], twin)

    ring_own = [[ring_copy(0, 0, 3, h), ring_copy(1, 0, 1, h)] for h in range(2)]
    ring_on = [ring_copy(0, 3, 2, 0), ring_copy(1, 1, 2, 1)]
    for h in range(2):

        @pl.loop(0, 8)
        def _(i):
            remote(
                kv_send.at[h, i],
                kvb.at[0, pl.ds(h * HD, HD), lanes(i)],
                kv_ss.at[h, i],
                kv_rs.at[h, i],
                mate(i),
            ).wait_recv()

        ring_own[h][0].start()
        ring_own[h][1].start()
        twin_copy(0, h).start()

    @pl.loop(0, 8)
    def _(i):
        remote(
            kv_send.at[2, i], q_t.at[:, lanes(i)], q_ss.at[i], q_rs.at[i], mate(i)
        ).wait_recv()

    def block(step):
        dc = jnp.where(step < 2, step, jnp.where(step < 6, step // 4, step - 6))
        dx = jnp.where(step < 2, 0, jnp.where(step < 6, 3 - 2 * (step % 2), 2))
        return 2 * dx + dc

    def scores_of(b, at):
        return dot(kvb[b, 0:HD, at : at + 256].astype(F32).T.astype(BF16), q_t[...])

    def attend(this, following):
        old = peak[...]
        new = jnp.maximum(old, top[...])
        update = acc[...] * jnp.exp2(old - new)
        highest = None
        for at in range(0, 8 * TOK, 256):
            if following is not None:
                scores = scores_of(following, at)
                here = jnp.max(scores, axis=0, keepdims=True)
                highest = here if highest is None else jnp.maximum(highest, here)
            probs = jnp.exp2(score_buf[at : at + 256, :] - new).astype(BF16)
            update = update + dot(kvb[this, HD : HD + TOK, at : at + 256], probs)
            if following is not None:
                score_buf[at : at + 256, :] = scores
        acc[...] = update
        peak[...] = new
        if following is not None:
            top[...] = highest

    highest = None
    for at in range(0, 8 * TOK, 256):
        scores = scores_of(0, at)
        here = jnp.max(scores, axis=0, keepdims=True)
        highest = here if highest is None else jnp.maximum(highest, here)
        score_buf[at : at + 256, :] = scores
    top[...] = highest

    @pl.loop(1, 8)
    def _(step):
        @pl.when(step == 1)
        def _():
            twin_copy(0, 0).wait_recv()

        @pl.when(step == 2)
        def _():
            ring_own[0][0].wait_recv()
            ring_on[0].start()
            twin_copy(3, 0).start()
            ring_own[0][1].wait_recv()
            twin_copy(1, 0).start()
            twin_copy(0, 1).wait_recv()

        @pl.when(step == 3)
        def _():
            ring_own[1][1].wait_recv()
            ring_on[1].start()
            twin_copy(1, 1).start()
            ring_own[1][0].wait_recv()
            twin_copy(3, 1).start()

        @pl.when(step == 4)
        def _():
            twin_copy(3, 0).wait_recv()

        @pl.when(step == 5)
        def _():
            twin_copy(1, 0).wait_recv()
            twin_copy(3, 1).wait_recv()

        @pl.when(step == 6)
        def _():
            ring_on[0].wait_recv()
            twin_copy(2, 0).start()
            twin_copy(1, 1).wait_recv()

        @pl.when(step == 7)
        def _():
            ring_on[1].wait_recv()
            twin_copy(2, 1).start()
            twin_copy(2, 0).wait_recv()

        attend(block(step - 1), block(step))

    twin_copy(2, 1).wait_recv()
    attend(5, None)

    def o_copy(i, start):
        exchange(
            i,
            o_send.at[i],
            heads_t.at[pl.ds(pl.multiple_of(slot * HD, HD), HD), :],
            o_ss.at[i],
            o_rs.at[slot],
            start,
        )

    @pl.loop(0, 8)
    def _(i):
        o_send[i] = (acc[0:HD, lanes(i)] / acc[HD : HD + 1, lanes(i)]).astype(BF16)
        o_copy(i, True)

    weight_copies[3].wait()

    @pl.loop(0, 8)
    def _(i):
        remote(
            o_send.at[i],
            heads_t.at[pl.ds(pl.multiple_of(i * HD, HD), HD), :],
            o_ss.at[i],
            o_rs.at[i],
            mate(i),
        ).wait_recv()

    heads = heads_t[...].astype(F32).T.astype(BF16)
    proj = dot(heads, ow_buf[...])
    proj_send[...] = proj.astype(BF16)
    proj_copy = remote(proj_send, proj_recv, proj_sem.at[0], proj_sem.at[1], twin)
    proj_copy.start()

    def column(row):
        return jnp.broadcast_to(row, (TOK, TOK)).T

    def fill_spread(dx):
        ids = lax.broadcasted_iota(jnp.int32, (EXPERTS * CAP, TOK), 0).astype(F32)
        hit = jnp.logical_or(ids == info[dx, 0:1, :], ids == info[dx, 1:2, :])
        spread[dx] = hit.astype(F32).astype(BF16)

    def fill_picks(dx):
        ids = lax.broadcasted_iota(jnp.int32, (TOK, EXPERTS * CAP), 1).astype(F32)
        for k in range(2):
            hit = ids == column(info[dx, k : k + 1, :])[:, 0:1]
            picks[dx, k * TOK : (k + 1) * TOK, :] = hit.astype(F32).astype(BF16)
            shares[dx, k] = column(info[dx, 2 + k : 3 + k, :])

    def combine(dx, table):
        rows = dot(picks[dx], table)
        return rows[0:TOK] * shares[dx, 0, :, 0:1] + rows[TOK:] * shares[dx, 1, :, 0:1]

    for dx in (1, 3, 2):
        to_line(info, info_ss, info_rs, 4 - dx).wait_recv()
    for dx in range(4):
        fill_spread(dx)
    proj_copy.wait_recv()
    hidden = tokens[...].astype(F32) + proj + proj_recv[...].astype(F32)
    inverse = lax.rsqrt(jnp.mean(hidden * hidden, axis=1, keepdims=True) + EPS)
    moe = hidden * inverse * norm_moe[...].reshape(1, D)
    sums[0, 0, 0:TOK, :] = hidden[:, 0:HALF]
    sums[0, 1, 0:TOK, :] = hidden[:, HALF:]
    moe_half[2] = sums[0, c, 0:TOK, :]
    moe_half[0] = moe[:, 0:HALF]
    moe_half[1] = moe[:, HALF:]
    mine = moe_half[c].astype(BF16)

    tok_rest[0] = mine[:, BULK:]
    for dx in (2, 1, 3):
        to_line(tok_rest, tok_ss, tok_rs, dx).start()
    rows = dot(spread[0], mine[:, 0:BULK]).reshape(EXPERTS, CAP, BULK)
    disp_bulk[:, 0:CAP, :] = rows[:, :, 0:REST].astype(BF16)
    disp_bulk[:, CAP:, :] = rows[:, :, REST:].astype(BF16)

    def over_plane(src, dst, send_sem, recv_sem, near=False):
        @pl.loop(0, 16)
        def _(i):
            turn = i // 4
            if near:
                a = jnp.where(turn == 2, 3, jnp.where(turn == 3, 2, turn))
            else:
                a = (2 + 3 * turn) % 4
            p = ((z + a) % 4) * 4 + (y + 2 + 3 * i) % 4

            @pl.when(p == plane)
            def _():
                pltpu.make_async_copy(src.at[p], dst.at[plane], recv_sem.at[plane]).start()

            @pl.when(p != plane)
            def _():
                remote(
                    src.at[p], dst.at[plane], send_sem.at[p], recv_sem.at[plane], plane_dev(p)
                ).start()

    def plane_gone(src, dst, send_sem, recv_sem, p):
        remote(src.at[p], dst.at[plane], send_sem.at[p], recv_sem.at[plane], plane_dev(p)).wait_send()

    bulk_way = (disp_bulk, x_bulk.at[0, c], d_ss, d_rs)
    rest_way = (disp_rest, x_rest.at[c], e_ss, e_rs)
    over_plane(*bulk_way, near=True)

    def group(a):
        return pl.ds(((z + 4 - a) % 4) * 4, 4)

    def x_ring(to, src_dx, dst_dx, a):
        return remote(
            x_bulk.at[src_dx, c, group(a)],
            x_bulk.at[dst_dx, c, group(a)],
            xr_ss.at[dst_dx, a],
            xr_rs.at[dst_dx, a],
            right if to == 0 else left,
        )

    def x_twin(dx, a, arriving):
        part = x_bulk.at[dx, 1 - c if arriving else c, group(a)]
        return remote(part, part, xt_ss.at[dx, a], xt_rs.at[dx, a], twin)

    def rest_twin(a, arriving):
        part = x_rest.at[1 - c if arriving else c, group(a)]
        return remote(part, part, xe_ss.at[a], xe_rs.at[a], twin)

    def wait_group(a, src, dst, send_sem, recv_sem):
        @pl.loop(0, 4)
        def _(b):
            p = ((z + 4 - a) % 4) * 4 + b
            remote(src.at[p], dst.at[p], send_sem.at[p], recv_sem.at[p], plane_dev(p)).wait_recv()

    def ring_group(a):
        wait_group(a, *bulk_way)
        x_ring(0, 0, 3, a).start()
        x_ring(1, 0, 1, a).start()
        x_twin(0, a, False).start()

    ring_group(GROUPS[0])
    disp_wide[:, 0:CAP, :] = dot(spread[0], tok_rest[0]).reshape(EXPERTS, CAP, REST)
    for dx in (1, 3, 2):
        to_line(tok_rest, tok_ss, tok_rs, 4 - dx).wait_recv()
        disp_wide[:, dx * CAP : (dx + 1) * CAP, :] = dot(spread[dx], tok_rest[dx]).reshape(
            EXPERTS, CAP, REST
        )
    disp_rest[...] = disp_wide[...].astype(BF16)
    over_plane(*rest_way)

    for a in GROUPS[1:]:
        ring_group(a)
    for dx in range(4):
        fill_picks(dx)

    def y_copy(dx):
        return remote(y_send.at[dx], y_recv.at[dx], y_ss.at[dx], y_rs.at[dx], twin)

    def first_part(dx):
        for core in range(2):
            piece = x_bulk[dx, core].astype(F32)
            for h in range(2):
                at = core * BULK + h * REST
                rows_bulk[:, at : at + REST] = (
                    piece[:, h * CAP : (h + 1) * CAP, :].reshape(EXPERTS * CAP, REST).astype(BF16)
                )
        for k in range(2):
            sums[dx, k] = dot(rows_bulk[...], w_buf[1 + k, 0 : 2 * BULK, :])

    def second_part(dx):
        rows = rows_rest[dx]
        gate = sums[dx, 0] + dot(rows, w_buf[1, 2 * BULK :, :])
        up = sums[dx, 1] + dot(rows, w_buf[2, 2 * BULK :, :])
        active = (gate / (1.0 + jnp.exp(-gate)) * up).astype(BF16)
        y_send[dx] = dot(active, wd_buf[1 - c]).astype(BF16)
        y_copy(dx).start()
        sums[dx, 0] = dot(active, wd_buf[c])

    def settle(dx):
        y_copy(dx).wait_recv()
        total = (sums[dx, 0] + y_recv[dx].astype(F32)).reshape(EXPERTS, CAP, HALF)
        parts[dx, :, 0:CAP, :] = total[:, :, 0:REST].astype(BF16)
        parts[dx, :, CAP:, :] = total[:, :, REST:BULK].astype(BF16)
        pair, at = (0 if dx in (1, 3) else 1), (0 if dx > 1 else CAP)
        rest_send[pair, :, at : at + CAP, :] = total[:, :, BULK:].astype(BF16)

    for copy in weight_copies[4:]:
        copy.wait()
    def half(h):
        return pl.ds(8 * h, 8)

    def far_copy(h):
        return remote(
            parts.at[2, half(h)], diag_recv.at[h], r_ss.at[h], r_rs.at[h], right if h == 0 else left
        )

    def near_copy(dx, h):
        return remote(
            parts.at[dx, half(h)],
            side_recv.at[dx // 2, half(h)],
            r_ss.at[2 + (dx // 2) * 2 + h],
            r_rs.at[2 + (dx // 2) * 2 + h],
            right if dx == 1 else left,
        )

    rest_back = [
        (rest_send.at[pair], rest_recv.at[pair], rest_ss.at[pair], rest_rs.at[pair])
        for pair in range(2)
    ]
    back_way = (back, ret, b_ss, b_rs)

    def sum_copy(dx):
        return remote(
            sum_send.at[dx], sum_recv.at[4 - dx], sum_ss.at[dx], sum_rs.at[4 - dx], along(dx)
        )

    @pl.loop(0, 8)
    def _(step):
        def at(number):
            return pl.when(step == number)

        @at(0)
        def _():
            for a in GROUPS:
                x_twin(0, a, True).wait_recv()

        @at(1)
        def _():
            for i, a in enumerate(GROUPS):
                x_ring(0, 0, 3, a).wait_recv()
                if i < 2:
                    x_ring(0, 3, 2, a).start()
                x_twin(3, a, False).start()
                x_ring(1, 0, 1, a).wait_recv()
                if i >= 2:
                    x_ring(1, 1, 2, a).start()
                x_twin(1, a, False).start()
            for a in GROUPS:
                x_twin(3, a, True).wait_recv()

        @at(2)
        def _():
            for a in GROUPS:
                x_twin(1, a, True).wait_recv()

        @at(3)
        def _():
            for a in ORDER:
                wait_group(a, *rest_way)
                rest_twin(a, False).start()
            for a in ORDER:
                rest_twin(a, True).wait_recv()
            for core in range(2):
                wide = x_rest[core].astype(F32)
                for dx in range(4):
                    rows_rest[dx, :, core * REST : (core + 1) * REST] = (
                        wide[:, dx * CAP : (dx + 1) * CAP, :]
                        .reshape(EXPERTS * CAP, REST)
                        .astype(BF16)
                    )

        @at(4)
        def _():
            for i, a in enumerate(GROUPS):
                x_ring(0 if i < 2 else 1, 0, 2, a).wait_recv()
                x_twin(2, a, False).start()

        @at(5)
        def _():
            for a in GROUPS:
                x_twin(2, a, True).wait_recv()

        @at(6)
        def _():
            settle(3)
            near_copy(3, 0).start()
            settle(1)
            near_copy(1, 1).start()
            over_plane(*rest_back[0])

        @at(7)
        def _():
            settle(2)
            far_copy(0).start()
            far_copy(1).start()

        is_first = jnp.logical_or(step < 3, step == 5)
        dx = jnp.where(
            jnp.logical_or(step == 0, step == 7),
            0,
            jnp.where(
                jnp.logical_or(step == 1, step == 3),
                3,
                jnp.where(jnp.logical_or(step == 2, step == 4), 1, 2),
            ),
        )

        @pl.when(is_first)
        def _():
            first_part(dx)

        @pl.when(jnp.logical_not(is_first))
        def _():
            second_part(dx)

    settle(0)
    over_plane(*rest_back[1])
    far_copy(0).wait_recv()
    parts[1, 0:8] = (parts[1, 0:8].astype(F32) + diag_recv[0].astype(F32)).astype(BF16)
    near_copy(1, 0).start()
    far_copy(1).wait_recv()
    parts[3, 8:16] = (parts[3, 8:16].astype(F32) + diag_recv[1].astype(F32)).astype(BF16)
    near_copy(3, 1).start()

    def rest_sums(pair):
        @pl.loop(0, 16)
        def _(p):
            remote(
                rest_send.at[pair, p],
                rest_recv.at[pair, p],
                rest_ss.at[pair, p],
                rest_rs.at[pair, p],
                plane_dev(p),
            ).wait_recv()

        both = rest_recv[pair].astype(F32)
        found = []
        for i, dx in enumerate((3, 1) if pair == 0 else (2, 0)):
            table = both[:, i * CAP : (i + 1) * CAP, :].reshape(EXPERTS * CAP, REST).astype(BF16)
            found.append(combine(dx, table))
        return found

    found = rest_sums(0)
    for i, dx in enumerate((3, 1)):
        sum_send[dx] = found[i].astype(BF16)
        sum_copy(dx).start()
    for h in range(2):
        near_copy(1, h).wait_recv()
        near_copy(3, h).wait_recv()
        at = slice(8 * h, 8 * h + 8)
        back[at] = (
            parts[0, at].astype(F32) + side_recv[0, at].astype(F32) + side_recv[1, at].astype(F32)
        ).astype(BF16)
    over_plane(*back_way)
    found = rest_sums(1)
    sum_send[2] = found[0].astype(BF16)
    sum_copy(2).start()
    rest = moe_half[2, :, BULK:] + found[1]
    for dx in (2, 1, 3):
        sum_copy(4 - dx).wait_recv()
        rest = rest + sum_recv[dx].astype(F32)
    out[:, BULK:] = rest.astype(BF16)

    @pl.loop(0, 16)
    def _(p):
        remote(back.at[p], ret.at[p], b_ss.at[p], b_rs.at[p], plane_dev(p)).wait_recv()

    both = ret[...].astype(F32)
    for h in range(2):
        cols = slice(h * REST, (h + 1) * REST)
        table = both[:, h * CAP : (h + 1) * CAP, :].reshape(EXPERTS * CAP, REST).astype(BF16)
        out[:, cols] = (moe_half[2, :, cols] + combine(0, table)).astype(BF16)

    @pl.loop(0, 8)
    def _(i):
        kv_copy(0, i, False)
        kv_copy(1, i, False)
        q_copy(i, False)
        o_copy(i, False)

    for h in range(2):
        ring_own[h][0].wait_send()
        ring_own[h][1].wait_send()
        ring_on[h].wait_send()
        for dx in range(4):
            twin_copy(dx, h).wait_send()
    proj_copy.wait_send()

    @pl.loop(0, 16)
    def _(p):
        @pl.when(p != plane)
        def _():
            for way in (bulk_way, rest_way, rest_back[0], rest_back[1], back_way):
                plane_gone(*way, p)

    for dx in (1, 2, 3):
        to_line(info, info_ss, info_rs, dx).wait_send()
        to_line(tok_rest, tok_ss, tok_rs, dx).wait_send()
        sum_copy(dx).wait_send()
    for i, a in enumerate(GROUPS):
        x_ring(0, 0, 3, a).wait_send()
        x_ring(1, 0, 1, a).wait_send()
        (x_ring(0, 3, 2, a) if i < 2 else x_ring(1, 1, 2, a)).wait_send()
        for dx in range(4):
            x_twin(dx, a, False).wait_send()
        rest_twin(a, False).wait_send()
    for dx in range(4):
        y_copy(dx).wait_send()
    for h in range(2):
        far_copy(h).wait_send()
        near_copy(1, h).wait_send()
        near_copy(3, h).wait_send()


def on_device(
    tokens,
    attn_weight,
    out_weight,
    norm_attn,
    norm_moe,
    routes,
    route_weight,
    expert_in,
    expert_out,
):
    vmem = pl.BlockSpec(memory_space=pltpu.VMEM)
    hbm = pl.BlockSpec(memory_space=pl.ANY)
    dma = pltpu.SemaphoreType.DMA
    pairs = (EXPERTS, 2 * CAP, REST)
    fours = (EXPERTS, 4 * CAP, REST)
    scratch = [
        pltpu.VMEM((TOK, D), BF16),
        pltpu.VMEM((D,), F32),
        pltpu.VMEM((D,), F32),
        pltpu.VMEM((2, TOK), jnp.int32),
        pltpu.VMEM((2, TOK), F32),
        dma((5,)),
        pltpu.VMEM((3, D, HALF), BF16),
        pltpu.VMEM((HALF, D), BF16),
        pltpu.VMEM((2, HALF, HALF), BF16),
        dma((14,)),
        pltpu.VMEM((TOK, D), BF16),
        pltpu.VMEM((3, 8, HD, TOK), BF16),
        pltpu.VMEM((HD, 8 * TOK), BF16),
        pltpu.VMEM((8, 2 * HD + 32, 8 * TOK), BF16),
        pltpu.VMEM((8 * TOK, 8 * TOK), F32),
        pltpu.VMEM((1, 8 * TOK), F32),
        pltpu.VMEM((1, 8 * TOK), F32),
        pltpu.VMEM((TOK, 8 * TOK), F32),
        pltpu.VMEM((8, HD, TOK), BF16),
        pltpu.VMEM((HALF, TOK), BF16),
        pltpu.VMEM((TOK, D), BF16),
        pltpu.VMEM((TOK, D), BF16),
        pltpu.VMEM((3, TOK, HALF), F32),
        pltpu.VMEM((4, 8, TOK), F32),
        pltpu.VMEM((4, EXPERTS * CAP, TOK), BF16),
        pltpu.VMEM((4, 2 * TOK, EXPERTS * CAP), BF16),
        pltpu.VMEM((4, 2, TOK, TOK), F32),
        pltpu.VMEM((4, TOK, REST), BF16),
        pltpu.VMEM(pairs, BF16),
        pltpu.VMEM(fours, F32),
        pltpu.VMEM(fours, BF16),
        pltpu.VMEM((4, 2) + pairs, BF16),
        pltpu.VMEM((2,) + fours, BF16),
        pltpu.VMEM((EXPERTS * CAP, 2 * BULK), BF16),
        pltpu.VMEM((4, EXPERTS * CAP, 2 * REST), BF16),
        pltpu.VMEM((4, 2, EXPERTS * CAP, HALF), F32),
        pltpu.VMEM((4, EXPERTS * CAP, HALF), BF16),
        pltpu.VMEM((4, EXPERTS * CAP, HALF), BF16),
        pltpu.VMEM((4,) + pairs, BF16),
        pltpu.VMEM((2, 8, 2 * CAP, REST), BF16),
        pltpu.VMEM((2,) + pairs, BF16),
        pltpu.VMEM(pairs, BF16),
        pltpu.VMEM(pairs, BF16),
        pltpu.VMEM((2,) + pairs, BF16),
        pltpu.VMEM((2,) + pairs, BF16),
        pltpu.VMEM((4, TOK, REST), BF16),
        pltpu.VMEM((4, TOK, REST), BF16),
        dma((2, 8)),
        dma((2, 8)),
        dma((8,)),
        dma((8,)),
        dma((4, 2)),
        dma((4, 2)),
        dma((4, 2)),
        dma((4, 2)),
        dma((8,)),
        dma((8,)),
        dma((2,)),
        dma((4,)),
        dma((4,)),
        dma((4,)),
        dma((4,)),
        dma((16,)),
        dma((16,)),
        dma((16,)),
        dma((16,)),
        dma((4, 4)),
        dma((4, 4)),
        dma((4, 4)),
        dma((4, 4)),
        dma((4,)),
        dma((4,)),
        dma((4,)),
        dma((4,)),
        dma((6,)),
        dma((6,)),
        dma((2, 16)),
        dma((2, 16)),
        dma((4,)),
        dma((4,)),
        dma((16,)),
        dma((16,)),
    ]
    return pl.pallas_call(
        layer_kernel,
        out_shape=jax.ShapeDtypeStruct((TOK, HALF), BF16),
        in_specs=[hbm] * 9,
        out_specs=vmem,
        scratch_shapes=scratch,
        compiler_params=pltpu.CompilerParams(
            collective_id=0, has_side_effects=True, vmem_limit_bytes=60 * 1024 * 1024
        ),
        cost_estimate=pl.CostEstimate(
            flops=30_000_000_000, bytes_accessed=17_000_000, transcendentals=9_000_000
        ),
    )(
        tokens,
        attn_weight,
        out_weight,
        norm_attn,
        norm_moe,
        routes.T,
        route_weight.T,
        expert_in,
        expert_out,
    )


def solution(mesh):
    return jax.shard_map(
        on_device,
        mesh=mesh,
        in_specs=(
            P("seq", None),
            P(None, None, "tensor"),
            P("tensor", None),
            P(),
            P(),
            P("seq", None),
            P("seq", None),
            P("seq", None, None, "tensor"),
            P("seq", "tensor", None),
        ),
        out_specs=P("seq", "tensor"),
        check_vma=False,
    )
```

```python
import math

import jax
import jax.numpy as jnp
from jax import lax
from jax.experimental import pallas as pl
from jax.experimental.pallas import tpu as pltpu
from jax.sharding import PartitionSpec as P

MESH = pl.DeviceIdType.MESH
D = 1536
HALF = 768
BULK = 512
REST = 256
ORDER = (2, 1, 3, 0)
GROUPS = (0, 1, 3, 2)
HD = 96
TOK = 128
EXPERTS = 16
CAP = 24
EPS = 1e-6
F32 = jnp.float32
BF16 = jnp.bfloat16
SCALE = HD ** (-0.5) * math.log2(math.e)


def dot(a, b):
    return jnp.dot(a, b, preferred_element_type=F32)


def remote(src, dst, send_sem, recv_sem, device):
    return pltpu.make_async_remote_copy(
        src_ref=src,
        dst_ref=dst,
        send_sem=send_sem,
        recv_sem=recv_sem,
        device_id=device,
        device_id_type=MESH,
    )


def layer_kernel(
    tokens_in,
    attn_w,
    out_w,
    norm_attn_in,
    norm_moe_in,
    routes_in,
    route_weight_in,
    expert_in,
    expert_out,
    out,
    tokens,
    norm_attn,
    norm_moe,
    routes,
    route_weight,
    small_sem,
    w_buf,
    ow_buf,
    wd_buf,
    w_sem,
    normed_buf,
    kv_send,
    q_t,
    kvb,
    score_buf,
    top,
    peak,
    acc,
    o_send,
    heads_t,
    proj_send,
    proj_recv,
    moe_half,
    info,
    spread,
    picks,
    shares,
    tok_rest,
    disp_bulk,
    disp_wide,
    disp_rest,
    x_bulk,
    x_rest,
    rows_bulk,
    rows_rest,
    sums,
    y_send,
    y_recv,
    parts,
    diag_recv,
    side_recv,
    back,
    ret,
    rest_send,
    rest_recv,
    sum_send,
    sum_recv,
    kv_ss,
    kv_rs,
    q_ss,
    q_rs,
    ring_ss,
    ring_rs,
    twin_ss,
    twin_rs,
    o_ss,
    o_rs,
    proj_sem,
    info_ss,
    info_rs,
    tok_ss,
    tok_rs,
    d_ss,
    d_rs,
    e_ss,
    e_rs,
    xr_ss,
    xr_rs,
    xt_ss,
    xt_rs,
    xe_ss,
    xe_rs,
    y_ss,
    y_rs,
    r_ss,
    r_rs,
    rest_ss,
    rest_rs,
    sum_ss,
    sum_rs,
    b_ss,
    b_rs,
):
    s = lax.axis_index("seq")
    c = lax.axis_index("tensor")
    x = s % 4
    plane = s // 4
    z = plane // 4
    y = plane % 4
    side = z // 2
    slot = (z % 2) * 4 + y
    left = (s - x + (x + 3) % 4, c)
    right = (s - x + (x + 1) % 4, c)
    twin = (s, 1 - c)

    def along(dx):
        return (s - x + (x + dx) % 4, c)

    def mate(i):
        return ((2 * c + i // 4) * 16 + (i % 4) * 4 + x, side)

    def is_me(i):
        return jnp.logical_and(c == side, i == slot)

    def plane_dev(p):
        return (p * 4 + x, c)

    barrier = pltpu.get_barrier_semaphore()

    def greet(device):
        pl.semaphore_signal(barrier, inc=1, device_id=device, device_id_type=MESH)

    for device in (left, right, along(2), twin):
        greet(device)

    @pl.loop(0, 8)
    def _(i):
        @pl.when(jnp.logical_not(is_me(i)))
        def _():
            greet(mate(i))

    @pl.loop(0, 16)
    def _(p):
        @pl.when(p != plane)
        def _():
            greet(plane_dev(p))

    small = [
        pltpu.make_async_copy(src, dst, small_sem.at[i])
        for i, (src, dst) in enumerate(
            (
                (tokens_in, tokens),
                (norm_attn_in, norm_attn),
                (routes_in, routes),
                (route_weight_in, route_weight),
                (norm_moe_in, norm_moe),
            )
        )
    ]
    for copy in small:
        copy.start()

    weight_copies = [
        pltpu.make_async_copy(attn_w.at[1], w_buf.at[1], w_sem.at[1]),
        pltpu.make_async_copy(attn_w.at[2], w_buf.at[2], w_sem.at[2]),
        pltpu.make_async_copy(attn_w.at[0], w_buf.at[0], w_sem.at[0]),
        pltpu.make_async_copy(out_w, ow_buf, w_sem.at[3]),
        pltpu.make_async_copy(expert_out.at[0, :, pl.ds(0, HALF)], wd_buf.at[0], w_sem.at[4]),
        pltpu.make_async_copy(expert_out.at[0, :, pl.ds(HALF, HALF)], wd_buf.at[1], w_sem.at[5]),
    ]
    moves = (
        (0, 0, BULK),
        (HALF, BULK, BULK),
        (BULK, 2 * BULK, REST),
        (HALF + BULK, 2 * BULK + REST, REST),
    )
    weight_copies += [
        pltpu.make_async_copy(
            expert_in.at[0, k, pl.ds(start, rows)],
            w_buf.at[1 + k, pl.ds(to, rows)],
            w_sem.at[6 + 4 * k + i],
        )
        for k in range(2)
        for i, (start, to, rows) in enumerate(moves)
    ]
    for copy in weight_copies[:3]:
        copy.start()

    small[0].wait()
    small[1].wait()
    tok = tokens[...].astype(F32)
    mean_square = jnp.mean(tok * tok, axis=1, keepdims=True)
    normed_buf[...] = (tok * lax.rsqrt(mean_square + EPS) * norm_attn[...].reshape(1, D)).astype(BF16)

    def exchange(i, src, dst, send_sem, recv_sem, start):
        copy = remote(src, dst, send_sem, recv_sem, mate(i))

        @pl.when(jnp.logical_not(is_me(i)))
        def _():
            if start:
                copy.start()
            else:
                copy.wait_send()

        if start:

            @pl.when(is_me(i))
            def _():
                pltpu.make_async_copy(src, dst, recv_sem).start()

    def far(a):
        return (z + jnp.where(c == side, 1, 0) + a) % 2

    def lanes(i):
        return pl.ds(pl.multiple_of(i * TOK, TOK), TOK)

    def kv_copy(h, i, start):
        exchange(
            i,
            kv_send.at[h, i],
            kvb.at[0, pl.ds(h * HD, HD), lanes(slot)],
            kv_ss.at[h, i],
            kv_rs.at[h, slot],
            start,
        )

    def q_copy(i, start):
        exchange(i, kv_send.at[2, i], q_t.at[:, lanes(slot)], q_ss.at[i], q_rs.at[slot], start)

    @pl.loop(0, 3)
    def _(h):
        at = (h + 1) % 3
        pltpu.make_async_copy(attn_w.at[at], w_buf.at[at], w_sem.at[at]).wait()
        scale = jnp.where(h == 2, SCALE, 1.0)
        kv_send[h] = (dot(normed_buf[...], w_buf[at]) * scale).T.astype(BF16).reshape(8, HD, TOK)

    for copy in weight_copies[3:]:
        copy.start()

    @pl.loop(0, 8)
    def _(b):
        kvb[b, 2 * HD : 2 * HD + 32, :] = jnp.ones((32, 8 * TOK), BF16)

    peak[...] = jnp.full(peak.shape, -1e30, F32)
    acc[...] = jnp.zeros(acc.shape, F32)

    for copy in small[2:]:
        copy.wait()
    expert_ids = lax.broadcasted_iota(jnp.int32, (EXPERTS, TOK), 0)
    hot = [(routes[k : k + 1, :] == expert_ids).astype(F32) for k in range(2)]
    earlier = (
        lax.broadcasted_iota(jnp.int32, (TOK, TOK), 0)
        < lax.broadcasted_iota(jnp.int32, (TOK, TOK), 1)
    ).astype(BF16)
    before = dot((hot[0] + hot[1]).astype(BF16), earlier)
    place = [
        jnp.sum(before * hot[k], axis=0, keepdims=True)
        + routes[k : k + 1, :].astype(F32) * float(CAP)
        for k in range(2)
    ]
    info[0] = jnp.zeros((8, TOK), F32)
    for k in range(2):
        info[0, k : k + 1, :] = place[k]
        info[0, 2 + k : 3 + k, :] = route_weight[k : k + 1, :]

    pl.semaphore_wait(barrier, 4 + 15 + 8 - jnp.where(c == side, 1, 0))
    @pl.loop(0, 16)
    def _(i):
        kv_copy(i // 8, far(i) * 4 + (y + 2 + 3 * (i // 2)) % 4, True)

    @pl.loop(0, 8)
    def _(i):
        q_copy(far(i) * 4 + (y + 2 + 3 * (i // 2)) % 4, True)

    def to_line(ref, send_sem, recv_sem, dx):
        return remote(
            ref.at[0], ref.at[4 - dx], send_sem.at[dx], recv_sem.at[4 - dx], along(dx)
        )

    for dx in (2, 1, 3):
        to_line(info, info_ss, info_rs, dx).start()

    def kv_part(dx, dc, h):
        return kvb.at[2 * dx + dc, pl.ds(h * HD, HD)]

    def ring_copy(to, src_dx, dst_dx, h):
        device = right if to == 0 else left
        return remote(
            kv_part(src_dx, 0, h),
            kv_part(dst_dx, 0, h),
            ring_ss.at[dst_dx, h],
            ring_rs.at[dst_dx, h],
            device,
        )

    def twin_copy(dx, h):
        return remote(kv_part(dx, 0, h), kv_part(dx, 1, h), twin_ss.at[dx, h], twin_rs.at[dx, h], twin)

    ring_own = [[ring_copy(0, 0, 3, h), ring_copy(1, 0, 1, h)] for h in range(2)]
    ring_on = [ring_copy(0, 3, 2, 0), ring_copy(1, 1, 2, 1)]
    for h in range(2):

        @pl.loop(0, 8)
        def _(i):
            remote(
                kv_send.at[h, i],
                kvb.at[0, pl.ds(h * HD, HD), lanes(i)],
                kv_ss.at[h, i],
                kv_rs.at[h, i],
                mate(i),
            ).wait_recv()

        ring_own[h][0].start()
        ring_own[h][1].start()
        twin_copy(0, h).start()

    @pl.loop(0, 8)
    def _(i):
        remote(
            kv_send.at[2, i], q_t.at[:, lanes(i)], q_ss.at[i], q_rs.at[i], mate(i)
        ).wait_recv()

    def block(step):
        dc = jnp.where(step < 2, step, jnp.where(step < 6, step // 4, step - 6))
        dx = jnp.where(step < 2, 0, jnp.where(step < 6, 3 - 2 * (step % 2), 2))
        return 2 * dx + dc

    def scores_of(b, at):
        return dot(kvb[b, 0:HD, at : at + 256].astype(F32).T.astype(BF16), q_t[...])

    def attend(this, following):
        old = peak[...]
        new = jnp.maximum(old, top[...])
        update = acc[...] * jnp.exp2(old - new)
        highest = None
        for at in range(0, 8 * TOK, 256):
            if following is not None:
                scores = scores_of(following, at)
                here = jnp.max(scores, axis=0, keepdims=True)
                highest = here if highest is None else jnp.maximum(highest, here)
            probs = jnp.exp2(score_buf[at : at + 256, :] - new).astype(BF16)
            update = update + dot(kvb[this, HD : HD + TOK, at : at + 256], probs)
            if following is not None:
                score_buf[at : at + 256, :] = scores
        acc[...] = update
        peak[...] = new
        if following is not None:
            top[...] = highest

    highest = None
    for at in range(0, 8 * TOK, 256):
        scores = scores_of(0, at)
        here = jnp.max(scores, axis=0, keepdims=True)
        highest = here if highest is None else jnp.maximum(highest, here)
        score_buf[at : at + 256, :] = scores
    top[...] = highest

    @pl.loop(1, 8)
    def _(step):
        @pl.when(step == 1)
        def _():
            twin_copy(0, 0).wait_recv()

        @pl.when(step == 2)
        def _():
            ring_own[0][0].wait_recv()
            ring_on[0].start()
            twin_copy(3, 0).start()
            ring_own[0][1].wait_recv()
            twin_copy(1, 0).start()
            twin_copy(0, 1).wait_recv()

        @pl.when(step == 3)
        def _():
            ring_own[1][1].wait_recv()
            ring_on[1].start()
            twin_copy(1, 1).start()
            ring_own[1][0].wait_recv()
            twin_copy(3, 1).start()

        @pl.when(step == 4)
        def _():
            twin_copy(3, 0).wait_recv()

        @pl.when(step == 5)
        def _():
            twin_copy(1, 0).wait_recv()
            twin_copy(3, 1).wait_recv()

        @pl.when(step == 6)
        def _():
            ring_on[0].wait_recv()
            twin_copy(2, 0).start()
            twin_copy(1, 1).wait_recv()

        @pl.when(step == 7)
        def _():
            ring_on[1].wait_recv()
            twin_copy(2, 1).start()
            twin_copy(2, 0).wait_recv()

        attend(block(step - 1), block(step))

    twin_copy(2, 1).wait_recv()
    attend(5, None)

    def o_copy(i, start):
        exchange(
            i,
            o_send.at[i],
            heads_t.at[pl.ds(pl.multiple_of(slot * HD, HD), HD), :],
            o_ss.at[i],
            o_rs.at[slot],
            start,
        )

    @pl.loop(0, 8)
    def _(i):
        o_send[i] = (acc[0:HD, lanes(i)] / acc[HD : HD + 1, lanes(i)]).astype(BF16)
        o_copy(i, True)

    weight_copies[3].wait()

    @pl.loop(0, 8)
    def _(i):
        remote(
            o_send.at[i],
            heads_t.at[pl.ds(pl.multiple_of(i * HD, HD), HD), :],
            o_ss.at[i],
            o_rs.at[i],
            mate(i),
        ).wait_recv()

    heads = heads_t[...].astype(F32).T.astype(BF16)
    proj = dot(heads, ow_buf[...])
    proj_send[...] = proj.astype(BF16)
    proj_copy = remote(proj_send, proj_recv, proj_sem.at[0], proj_sem.at[1], twin)
    proj_copy.start()

    def column(row):
        return jnp.broadcast_to(row, (TOK, TOK)).T

    def fill_spread(dx):
        ids = lax.broadcasted_iota(jnp.int32, (EXPERTS * CAP, TOK), 0).astype(F32)
        hit = jnp.logical_or(ids == info[dx, 0:1, :], ids == info[dx, 1:2, :])
        spread[dx] = hit.astype(F32).astype(BF16)

    def fill_picks(dx):
        ids = lax.broadcasted_iota(jnp.int32, (TOK, EXPERTS * CAP), 1).astype(F32)
        for k in range(2):
            hit = ids == column(info[dx, k : k + 1, :])[:, 0:1]
            picks[dx, k * TOK : (k + 1) * TOK, :] = hit.astype(F32).astype(BF16)
            shares[dx, k] = column(info[dx, 2 + k : 3 + k, :])

    def combine(dx, table):
        rows = dot(picks[dx], table)
        return rows[0:TOK] * shares[dx, 0, :, 0:1] + rows[TOK:] * shares[dx, 1, :, 0:1]

    for dx in (1, 3, 2):
        to_line(info, info_ss, info_rs, 4 - dx).wait_recv()
    for dx in range(4):
        fill_spread(dx)
    proj_copy.wait_recv()
    hidden = tokens[...].astype(F32) + proj + proj_recv[...].astype(F32)
    inverse = lax.rsqrt(jnp.mean(hidden * hidden, axis=1, keepdims=True) + EPS)
    moe = hidden * inverse * norm_moe[...].reshape(1, D)
    sums[0, 0, 0:TOK, :] = hidden[:, 0:HALF]
    sums[0, 1, 0:TOK, :] = hidden[:, HALF:]
    moe_half[2] = sums[0, c, 0:TOK, :]
    moe_half[0] = moe[:, 0:HALF]
    moe_half[1] = moe[:, HALF:]
    mine = moe_half[c].astype(BF16)

    tok_rest[0] = mine[:, BULK:]
    for dx in (2, 1, 3):
        to_line(tok_rest, tok_ss, tok_rs, dx).start()
    rows = dot(spread[0], mine[:, 0:BULK]).reshape(EXPERTS, CAP, BULK)
    disp_bulk[:, 0:CAP, :] = rows[:, :, 0:REST].astype(BF16)
    disp_bulk[:, CAP:, :] = rows[:, :, REST:].astype(BF16)

    def to_plane(p, src, dst, send_sem, recv_sem):
        @pl.when(p == plane)
        def _():
            pltpu.make_async_copy(src.at[p], dst.at[plane], recv_sem.at[plane]).start()

        @pl.when(p != plane)
        def _():
            remote(
                src.at[p], dst.at[plane], send_sem.at[p], recv_sem.at[plane], plane_dev(p)
            ).start()

    def over_plane(src, dst, send_sem, recv_sem, near=False):
        @pl.loop(0, 16)
        def _(i):
            turn = i // 4
            if near:
                a = jnp.where(turn == 2, 3, jnp.where(turn == 3, 2, turn))
            else:
                a = (2 + 3 * turn) % 4
            p = ((z + a) % 4) * 4 + (y + 2 + 3 * i) % 4
            to_plane(p, src, dst, send_sem, recv_sem)

    def plane_gone(src, dst, send_sem, recv_sem, p):
        remote(src.at[p], dst.at[plane], send_sem.at[p], recv_sem.at[plane], plane_dev(p)).wait_send()

    bulk_way = (disp_bulk, x_bulk.at[0, c], d_ss, d_rs)
    rest_way = (disp_rest, x_rest.at[c], e_ss, e_rs)
    over_plane(*bulk_way, near=True)

    def group(a):
        return pl.ds(((z + 4 - a) % 4) * 4, 4)

    def x_ring(to, src_dx, dst_dx, a):
        return remote(
            x_bulk.at[src_dx, c, group(a)],
            x_bulk.at[dst_dx, c, group(a)],
            xr_ss.at[dst_dx, a],
            xr_rs.at[dst_dx, a],
            right if to == 0 else left,
        )

    def x_twin(dx, a, arriving):
        part = x_bulk.at[dx, 1 - c if arriving else c, group(a)]
        return remote(part, part, xt_ss.at[dx, a], xt_rs.at[dx, a], twin)

    def rest_twin(a, arriving):
        part = x_rest.at[1 - c if arriving else c, group(a)]
        return remote(part, part, xe_ss.at[a], xe_rs.at[a], twin)

    def wait_group(a, src, dst, send_sem, recv_sem):
        @pl.loop(0, 4)
        def _(b):
            p = ((z + 4 - a) % 4) * 4 + b
            remote(src.at[p], dst.at[p], send_sem.at[p], recv_sem.at[p], plane_dev(p)).wait_recv()

    def ring_group(a):
        wait_group(a, *bulk_way)
        x_ring(0, 0, 3, a).start()
        x_ring(1, 0, 1, a).start()
        x_twin(0, a, False).start()

    ring_group(GROUPS[0])
    disp_wide[:, 0:CAP, :] = dot(spread[0], tok_rest[0]).reshape(EXPERTS, CAP, REST)
    for dx in (1, 3, 2):
        to_line(tok_rest, tok_ss, tok_rs, 4 - dx).wait_recv()
        disp_wide[:, dx * CAP : (dx + 1) * CAP, :] = dot(spread[dx], tok_rest[dx]).reshape(
            EXPERTS, CAP, REST
        )
    disp_rest[...] = disp_wide[...].astype(BF16)
    over_plane(*rest_way)

    for a in GROUPS[1:]:
        ring_group(a)
    for dx in range(4):
        fill_picks(dx)

    def y_copy(dx):
        return remote(y_send.at[dx], y_recv.at[dx], y_ss.at[dx], y_rs.at[dx], twin)

    def first_part(dx):
        for core in range(2):
            piece = x_bulk[dx, core].astype(F32)
            for h in range(2):
                at = core * BULK + h * REST
                rows_bulk[:, at : at + REST] = (
                    piece[:, h * CAP : (h + 1) * CAP, :].reshape(EXPERTS * CAP, REST).astype(BF16)
                )
        for k in range(2):
            sums[dx, k] = dot(rows_bulk[...], w_buf[1 + k, 0 : 2 * BULK, :])

    def second_part(dx):
        rows = rows_rest[dx]
        gate = sums[dx, 0] + dot(rows, w_buf[1, 2 * BULK :, :])
        up = sums[dx, 1] + dot(rows, w_buf[2, 2 * BULK :, :])
        active = (gate / (1.0 + jnp.exp(-gate)) * up).astype(BF16)
        y_send[dx] = dot(active, wd_buf[1 - c]).astype(BF16)
        y_copy(dx).start()
        sums[dx, 0] = dot(active, wd_buf[c])

    def settle(dx):
        y_copy(dx).wait_recv()
        total = (sums[dx, 0] + y_recv[dx].astype(F32)).reshape(EXPERTS, CAP, HALF)
        parts[dx, :, 0:CAP, :] = total[:, :, 0:REST].astype(BF16)
        parts[dx, :, CAP:, :] = total[:, :, REST:BULK].astype(BF16)
        pair, at = (0 if dx in (1, 3) else 1), (0 if dx > 1 else CAP)
        rest_send[pair, :, at : at + CAP, :] = total[:, :, BULK:].astype(BF16)

    for copy in weight_copies[4:]:
        copy.wait()
    def piece_of(h, q):
        return pl.ds(8 * h + 4 * q, 4)

    def far_copy(h, q):
        return remote(
            parts.at[2, piece_of(h, q)],
            diag_recv.at[h, pl.ds(4 * q, 4)],
            r_ss.at[h, q],
            r_rs.at[h, q],
            right if h == 0 else left,
        )

    def near_copy(dx, h, q):
        number = 2 + (dx // 2) * 2 + h
        return remote(
            parts.at[dx, piece_of(h, q)],
            side_recv.at[dx // 2, piece_of(h, q)],
            r_ss.at[number, q],
            r_rs.at[number, q],
            right if dx == 1 else left,
        )

    rest_back = [
        (rest_send.at[pair], rest_recv.at[pair], rest_ss.at[pair], rest_rs.at[pair])
        for pair in range(2)
    ]
    back_way = (back, ret, b_ss, b_rs)

    def sum_copy(dx):
        return remote(
            sum_send.at[dx], sum_recv.at[4 - dx], sum_ss.at[dx], sum_rs.at[4 - dx], along(dx)
        )

    @pl.loop(0, 8)
    def _(step):
        def at(number):
            return pl.when(step == number)

        @at(0)
        def _():
            for a in GROUPS:
                x_twin(0, a, True).wait_recv()

        @at(1)
        def _():
            for i, a in enumerate(GROUPS):
                x_ring(0, 0, 3, a).wait_recv()
                if i < 2:
                    x_ring(0, 3, 2, a).start()
                x_twin(3, a, False).start()
                x_ring(1, 0, 1, a).wait_recv()
                if i >= 2:
                    x_ring(1, 1, 2, a).start()
                x_twin(1, a, False).start()
            for a in GROUPS:
                x_twin(3, a, True).wait_recv()

        @at(2)
        def _():
            for a in GROUPS:
                x_twin(1, a, True).wait_recv()

        @at(3)
        def _():
            for a in ORDER:
                wait_group(a, *rest_way)
                rest_twin(a, False).start()
            for a in ORDER:
                rest_twin(a, True).wait_recv()
            for core in range(2):
                wide = x_rest[core].astype(F32)
                for dx in range(4):
                    rows_rest[dx, :, core * REST : (core + 1) * REST] = (
                        wide[:, dx * CAP : (dx + 1) * CAP, :]
                        .reshape(EXPERTS * CAP, REST)
                        .astype(BF16)
                    )

        @at(4)
        def _():
            for i, a in enumerate(GROUPS):
                x_ring(0 if i < 2 else 1, 0, 2, a).wait_recv()
                x_twin(2, a, False).start()

        @at(5)
        def _():
            for a in GROUPS:
                x_twin(2, a, True).wait_recv()

        @at(6)
        def _():
            settle(3)
            for q in range(2):
                near_copy(3, 0, q).start()
            settle(1)
            for q in range(2):
                near_copy(1, 1, q).start()
            over_plane(*rest_back[0])

        @at(7)
        def _():
            settle(2)
            for q in range(2):
                far_copy(0, q).start()
                far_copy(1, q).start()

        is_first = jnp.logical_or(step < 3, step == 5)
        dx = jnp.where(
            jnp.logical_or(step == 0, step == 7),
            0,
            jnp.where(
                jnp.logical_or(step == 1, step == 3),
                3,
                jnp.where(jnp.logical_or(step == 2, step == 4), 1, 2),
            ),
        )

        @pl.when(is_first)
        def _():
            first_part(dx)

        @pl.when(jnp.logical_not(is_first))
        def _():
            second_part(dx)

    settle(0)
    over_plane(*rest_back[1])
    for q in range(2):
        for h, dx in ((0, 1), (1, 3)):
            far_copy(h, q).wait_recv()
            at = slice(8 * h + 4 * q, 8 * h + 4 * q + 4)
            far_part = diag_recv[h, 4 * q : 4 * q + 4].astype(F32)
            parts[dx, at] = (parts[dx, at].astype(F32) + far_part).astype(BF16)
            near_copy(dx, h, q).start()

    def rest_sums(pair):
        @pl.loop(0, 16)
        def _(p):
            remote(
                rest_send.at[pair, p],
                rest_recv.at[pair, p],
                rest_ss.at[pair, p],
                rest_rs.at[pair, p],
                plane_dev(p),
            ).wait_recv()

        both = rest_recv[pair].astype(F32)
        found = []
        for i, dx in enumerate((3, 1) if pair == 0 else (2, 0)):
            table = both[:, i * CAP : (i + 1) * CAP, :].reshape(EXPERTS * CAP, REST).astype(BF16)
            found.append(combine(dx, table))
        return found

    found = rest_sums(0)
    for i, dx in enumerate((3, 1)):
        sum_send[dx] = found[i].astype(BF16)
        sum_copy(dx).start()
    for q in range(2):
        for h in range(2):
            near_copy(1, h, q).wait_recv()
            near_copy(3, h, q).wait_recv()
            at = slice(8 * h + 4 * q, 8 * h + 4 * q + 4)
            near_parts = side_recv[0, at].astype(F32) + side_recv[1, at].astype(F32)
            back[at] = (parts[0, at].astype(F32) + near_parts).astype(BF16)

        @pl.loop(0, 8)
        def _(i):
            to_plane(2 * 4 * far(i) + 4 * q + (y + 2 + 3 * (i // 2)) % 4, *back_way)

    found = rest_sums(1)
    sum_send[2] = found[0].astype(BF16)
    sum_copy(2).start()
    rest = moe_half[2, :, BULK:] + found[1]
    for dx in (2, 1, 3):
        sum_copy(4 - dx).wait_recv()
        rest = rest + sum_recv[dx].astype(F32)
    out[:, BULK:] = rest.astype(BF16)

    @pl.loop(0, 16)
    def _(p):
        remote(back.at[p], ret.at[p], b_ss.at[p], b_rs.at[p], plane_dev(p)).wait_recv()

    both = ret[...].astype(F32)
    for h in range(2):
        cols = slice(h * REST, (h + 1) * REST)
        table = both[:, h * CAP : (h + 1) * CAP, :].reshape(EXPERTS * CAP, REST).astype(BF16)
        out[:, cols] = (moe_half[2, :, cols] + combine(0, table)).astype(BF16)

    @pl.loop(0, 8)
    def _(i):
        kv_copy(0, i, False)
        kv_copy(1, i, False)
        q_copy(i, False)
        o_copy(i, False)

    for h in range(2):
        ring_own[h][0].wait_send()
        ring_own[h][1].wait_send()
        ring_on[h].wait_send()
        for dx in range(4):
            twin_copy(dx, h).wait_send()
    proj_copy.wait_send()

    @pl.loop(0, 16)
    def _(p):
        @pl.when(p != plane)
        def _():
            for way in (bulk_way, rest_way, rest_back[0], rest_back[1], back_way):
                plane_gone(*way, p)

    for dx in (1, 2, 3):
        to_line(info, info_ss, info_rs, dx).wait_send()
        to_line(tok_rest, tok_ss, tok_rs, dx).wait_send()
        sum_copy(dx).wait_send()
    for i, a in enumerate(GROUPS):
        x_ring(0, 0, 3, a).wait_send()
        x_ring(1, 0, 1, a).wait_send()
        (x_ring(0, 3, 2, a) if i < 2 else x_ring(1, 1, 2, a)).wait_send()
        for dx in range(4):
            x_twin(dx, a, False).wait_send()
        rest_twin(a, False).wait_send()
    for dx in range(4):
        y_copy(dx).wait_send()
    for h in range(2):
        for q in range(2):
            far_copy(h, q).wait_send()
            near_copy(1, h, q).wait_send()
            near_copy(3, h, q).wait_send()


def on_device(
    tokens,
    attn_weight,
    out_weight,
    norm_attn,
    norm_moe,
    routes,
    route_weight,
    expert_in,
    expert_out,
):
    vmem = pl.BlockSpec(memory_space=pltpu.VMEM)
    hbm = pl.BlockSpec(memory_space=pl.ANY)
    dma = pltpu.SemaphoreType.DMA
    pairs = (EXPERTS, 2 * CAP, REST)
    fours = (EXPERTS, 4 * CAP, REST)
    scratch = [
        pltpu.VMEM((TOK, D), BF16),
        pltpu.VMEM((D,), F32),
        pltpu.VMEM((D,), F32),
        pltpu.VMEM((2, TOK), jnp.int32),
        pltpu.VMEM((2, TOK), F32),
        dma((5,)),
        pltpu.VMEM((3, D, HALF), BF16),
        pltpu.VMEM((HALF, D), BF16),
        pltpu.VMEM((2, HALF, HALF), BF16),
        dma((14,)),
        pltpu.VMEM((TOK, D), BF16),
        pltpu.VMEM((3, 8, HD, TOK), BF16),
        pltpu.VMEM((HD, 8 * TOK), BF16),
        pltpu.VMEM((8, 2 * HD + 32, 8 * TOK), BF16),
        pltpu.VMEM((8 * TOK, 8 * TOK), F32),
        pltpu.VMEM((1, 8 * TOK), F32),
        pltpu.VMEM((1, 8 * TOK), F32),
        pltpu.VMEM((TOK, 8 * TOK), F32),
        pltpu.VMEM((8, HD, TOK), BF16),
        pltpu.VMEM((HALF, TOK), BF16),
        pltpu.VMEM((TOK, D), BF16),
        pltpu.VMEM((TOK, D), BF16),
        pltpu.VMEM((3, TOK, HALF), F32),
        pltpu.VMEM((4, 8, TOK), F32),
        pltpu.VMEM((4, EXPERTS * CAP, TOK), BF16),
        pltpu.VMEM((4, 2 * TOK, EXPERTS * CAP), BF16),
        pltpu.VMEM((4, 2, TOK, TOK), F32),
        pltpu.VMEM((4, TOK, REST), BF16),
        pltpu.VMEM(pairs, BF16),
        pltpu.VMEM(fours, F32),
        pltpu.VMEM(fours, BF16),
        pltpu.VMEM((4, 2) + pairs, BF16),
        pltpu.VMEM((2,) + fours, BF16),
        pltpu.VMEM((EXPERTS * CAP, 2 * BULK), BF16),
        pltpu.VMEM((4, EXPERTS * CAP, 2 * REST), BF16),
        pltpu.VMEM((4, 2, EXPERTS * CAP, HALF), F32),
        pltpu.VMEM((4, EXPERTS * CAP, HALF), BF16),
        pltpu.VMEM((4, EXPERTS * CAP, HALF), BF16),
        pltpu.VMEM((4,) + pairs, BF16),
        pltpu.VMEM((2, 8, 2 * CAP, REST), BF16),
        pltpu.VMEM((2,) + pairs, BF16),
        pltpu.VMEM(pairs, BF16),
        pltpu.VMEM(pairs, BF16),
        pltpu.VMEM((2,) + pairs, BF16),
        pltpu.VMEM((2,) + pairs, BF16),
        pltpu.VMEM((4, TOK, REST), BF16),
        pltpu.VMEM((4, TOK, REST), BF16),
        dma((2, 8)),
        dma((2, 8)),
        dma((8,)),
        dma((8,)),
        dma((4, 2)),
        dma((4, 2)),
        dma((4, 2)),
        dma((4, 2)),
        dma((8,)),
        dma((8,)),
        dma((2,)),
        dma((4,)),
        dma((4,)),
        dma((4,)),
        dma((4,)),
        dma((16,)),
        dma((16,)),
        dma((16,)),
        dma((16,)),
        dma((4, 4)),
        dma((4, 4)),
        dma((4, 4)),
        dma((4, 4)),
        dma((4,)),
        dma((4,)),
        dma((4,)),
        dma((4,)),
        dma((6, 2)),
        dma((6, 2)),
        dma((2, 16)),
        dma((2, 16)),
        dma((4,)),
        dma((4,)),
        dma((16,)),
        dma((16,)),
    ]
    return pl.pallas_call(
        layer_kernel,
        out_shape=jax.ShapeDtypeStruct((TOK, HALF), BF16),
        in_specs=[hbm] * 9,
        out_specs=vmem,
        scratch_shapes=scratch,
        compiler_params=pltpu.CompilerParams(
            collective_id=0, has_side_effects=True, vmem_limit_bytes=60 * 1024 * 1024
        ),
        cost_estimate=pl.CostEstimate(
            flops=30_000_000_000, bytes_accessed=17_000_000, transcendentals=9_000_000
        ),
    )(
        tokens,
        attn_weight,
        out_weight,
        norm_attn,
        norm_moe,
        routes.T,
        route_weight.T,
        expert_in,
        expert_out,
    )


def solution(mesh):
    return jax.shard_map(
        on_device,
        mesh=mesh,
        in_specs=(
            P("seq", None),
            P(None, None, "tensor"),
            P("tensor", None),
            P(),
            P(),
            P("seq", None),
            P("seq", None),
            P("seq", None, None, "tensor"),
            P("seq", "tensor", None),
        ),
        out_specs=P("seq", "tensor"),
        check_vma=False,
    )
```

```python
import math

import jax
import jax.numpy as jnp
from jax import lax
from jax.experimental import pallas as pl
from jax.experimental.pallas import tpu as pltpu
from jax.sharding import PartitionSpec as P

MESH = pl.DeviceIdType.MESH
D = 1536
HALF = 768
BULK = 512
REST = 256
ORDER = (2, 1, 3, 0)
GROUPS = (0, 1, 3, 2)
HD = 96
TOK = 128
EXPERTS = 16
CAP = 24
EPS = 1e-6
F32 = jnp.float32
BF16 = jnp.bfloat16
SCALE = HD ** (-0.5) * math.log2(math.e)


def dot(a, b):
    return jnp.dot(a, b, preferred_element_type=F32)


def remote(src, dst, send_sem, recv_sem, device):
    return pltpu.make_async_remote_copy(
        src_ref=src,
        dst_ref=dst,
        send_sem=send_sem,
        recv_sem=recv_sem,
        device_id=device,
        device_id_type=MESH,
    )


def layer_kernel(
    tokens_in,
    attn_w,
    out_w,
    norm_attn_in,
    norm_moe_in,
    routes_in,
    route_weight_in,
    expert_in,
    expert_out,
    out,
    tokens,
    norm_attn,
    norm_moe,
    routes,
    route_weight,
    small_sem,
    w_buf,
    ow_buf,
    wd_buf,
    w_sem,
    normed_buf,
    kv_send,
    q_t,
    kvb,
    score_buf,
    top,
    peak,
    acc,
    o_send,
    heads_t,
    proj_send,
    proj_recv,
    moe_half,
    info,
    spread,
    picks,
    shares,
    tok_rest,
    disp_bulk,
    disp_wide,
    disp_rest,
    x_bulk,
    x_rest,
    rows_bulk,
    rows_rest,
    sums,
    y_send,
    y_recv,
    parts,
    diag_recv,
    side_recv,
    back,
    ret,
    rest_send,
    rest_recv,
    sum_send,
    sum_recv,
    kv_ss,
    kv_rs,
    q_ss,
    q_rs,
    ring_ss,
    ring_rs,
    twin_ss,
    twin_rs,
    o_ss,
    o_rs,
    proj_sem,
    info_ss,
    info_rs,
    tok_ss,
    tok_rs,
    d_ss,
    d_rs,
    e_ss,
    e_rs,
    xr_ss,
    xr_rs,
    xt_ss,
    xt_rs,
    xe_ss,
    xe_rs,
    y_ss,
    y_rs,
    r_ss,
    r_rs,
    rest_ss,
    rest_rs,
    sum_ss,
    sum_rs,
    b_ss,
    b_rs,
):
    s = lax.axis_index("seq")
    c = lax.axis_index("tensor")
    x = s % 4
    plane = s // 4
    z = plane // 4
    y = plane % 4
    side = z // 2
    slot = (z % 2) * 4 + y
    left = (s - x + (x + 3) % 4, c)
    right = (s - x + (x + 1) % 4, c)
    twin = (s, 1 - c)

    def along(dx):
        return (s - x + (x + dx) % 4, c)

    def mate(i):
        return ((2 * c + i // 4) * 16 + (i % 4) * 4 + x, side)

    def is_me(i):
        return jnp.logical_and(c == side, i == slot)

    def plane_dev(p):
        return (p * 4 + x, c)

    barrier = pltpu.get_barrier_semaphore()

    def greet(device):
        pl.semaphore_signal(barrier, inc=1, device_id=device, device_id_type=MESH)

    for device in (left, right, along(2), twin):
        greet(device)

    @pl.loop(0, 8)
    def _(i):
        @pl.when(jnp.logical_not(is_me(i)))
        def _():
            greet(mate(i))

    @pl.loop(0, 16)
    def _(p):
        @pl.when(p != plane)
        def _():
            greet(plane_dev(p))

    small = [
        pltpu.make_async_copy(src, dst, small_sem.at[i])
        for i, (src, dst) in enumerate(
            (
                (tokens_in, tokens),
                (norm_attn_in, norm_attn),
                (routes_in, routes),
                (route_weight_in, route_weight),
                (norm_moe_in, norm_moe),
            )
        )
    ]
    for copy in small:
        copy.start()

    weight_copies = [
        pltpu.make_async_copy(attn_w.at[1], w_buf.at[1], w_sem.at[1]),
        pltpu.make_async_copy(attn_w.at[2], w_buf.at[2], w_sem.at[2]),
        pltpu.make_async_copy(attn_w.at[0], w_buf.at[0], w_sem.at[0]),
        pltpu.make_async_copy(out_w, ow_buf, w_sem.at[3]),
        pltpu.make_async_copy(expert_out.at[0, :, pl.ds(0, HALF)], wd_buf.at[0], w_sem.at[4]),
        pltpu.make_async_copy(expert_out.at[0, :, pl.ds(HALF, HALF)], wd_buf.at[1], w_sem.at[5]),
    ]
    moves = (
        (0, 0, BULK),
        (HALF, BULK, BULK),
        (BULK, 2 * BULK, REST),
        (HALF + BULK, 2 * BULK + REST, REST),
    )
    weight_copies += [
        pltpu.make_async_copy(
            expert_in.at[0, k, pl.ds(start, rows)],
            w_buf.at[1 + k, pl.ds(to, rows)],
            w_sem.at[6 + 4 * k + i],
        )
        for k in range(2)
        for i, (start, to, rows) in enumerate(moves)
    ]
    for copy in weight_copies[:3]:
        copy.start()

    small[0].wait()
    small[1].wait()
    tok = tokens[...].astype(F32)
    mean_square = jnp.mean(tok * tok, axis=1, keepdims=True)
    normed_buf[...] = (tok * lax.rsqrt(mean_square + EPS) * norm_attn[...].reshape(1, D)).astype(BF16)

    def exchange(i, src, dst, send_sem, recv_sem, start):
        copy = remote(src, dst, send_sem, recv_sem, mate(i))

        @pl.when(jnp.logical_not(is_me(i)))
        def _():
            if start:
                copy.start()
            else:
                copy.wait_send()

        if start:

            @pl.when(is_me(i))
            def _():
                pltpu.make_async_copy(src, dst, recv_sem).start()

    def far(a):
        return (z + jnp.where(c == side, 1, 0) + a) % 2

    def lanes(i):
        return pl.ds(pl.multiple_of(i * TOK, TOK), TOK)

    def kv_copy(h, i, start):
        exchange(
            i,
            kv_send.at[h, i],
            kvb.at[0, pl.ds(h * HD, HD), lanes(slot)],
            kv_ss.at[h, i],
            kv_rs.at[h, slot],
            start,
        )

    def q_copy(i, start):
        exchange(i, kv_send.at[2, i], q_t.at[:, lanes(slot)], q_ss.at[i], q_rs.at[slot], start)

    @pl.loop(0, 3)
    def _(h):
        at = (h + 1) % 3
        pltpu.make_async_copy(attn_w.at[at], w_buf.at[at], w_sem.at[at]).wait()
        scale = jnp.where(h == 2, SCALE, 1.0)
        kv_send[h] = (dot(normed_buf[...], w_buf[at]) * scale).T.astype(BF16).reshape(8, HD, TOK)

    for copy in weight_copies[3:]:
        copy.start()

    @pl.loop(0, 8)
    def _(b):
        kvb[b, 2 * HD : 2 * HD + 32, :] = jnp.ones((32, 8 * TOK), BF16)

    peak[...] = jnp.full(peak.shape, -1e30, F32)
    acc[...] = jnp.zeros(acc.shape, F32)

    for copy in small[2:]:
        copy.wait()
    expert_ids = lax.broadcasted_iota(jnp.int32, (EXPERTS, TOK), 0)
    hot = [(routes[k : k + 1, :] == expert_ids).astype(F32) for k in range(2)]
    earlier = (
        lax.broadcasted_iota(jnp.int32, (TOK, TOK), 0)
        < lax.broadcasted_iota(jnp.int32, (TOK, TOK), 1)
    ).astype(BF16)
    before = dot((hot[0] + hot[1]).astype(BF16), earlier)
    place = [
        jnp.sum(before * hot[k], axis=0, keepdims=True)
        + routes[k : k + 1, :].astype(F32) * float(CAP)
        for k in range(2)
    ]
    info[0] = jnp.zeros((8, TOK), F32)
    for k in range(2):
        info[0, k : k + 1, :] = place[k]
        info[0, 2 + k : 3 + k, :] = route_weight[k : k + 1, :]

    pl.semaphore_wait(barrier, 4 + 15 + 8 - jnp.where(c == side, 1, 0))
    @pl.loop(0, 16)
    def _(i):
        kv_copy(i // 8, far(i) * 4 + (y + 2 + 3 * (i // 2)) % 4, True)

    @pl.loop(0, 8)
    def _(i):
        q_copy(far(i) * 4 + (y + 2 + 3 * (i // 2)) % 4, True)

    def to_line(ref, send_sem, recv_sem, dx):
        return remote(
            ref.at[0], ref.at[4 - dx], send_sem.at[dx], recv_sem.at[4 - dx], along(dx)
        )

    for dx in (2, 1, 3):
        to_line(info, info_ss, info_rs, dx).start()

    def kv_part(dx, dc, h):
        return kvb.at[2 * dx + dc, pl.ds(h * HD, HD)]

    def ring_copy(to, src_dx, dst_dx, h):
        device = right if to == 0 else left
        return remote(
            kv_part(src_dx, 0, h),
            kv_part(dst_dx, 0, h),
            ring_ss.at[dst_dx, h],
            ring_rs.at[dst_dx, h],
            device,
        )

    def twin_copy(dx, h):
        return remote(kv_part(dx, 0, h), kv_part(dx, 1, h), twin_ss.at[dx, h], twin_rs.at[dx, h], twin)

    ring_own = [[ring_copy(0, 0, 3, h), ring_copy(1, 0, 1, h)] for h in range(2)]
    ring_on = [ring_copy(0, 3, 2, 0), ring_copy(1, 1, 2, 1)]
    for h in range(2):

        @pl.loop(0, 8)
        def _(i):
            remote(
                kv_send.at[h, i],
                kvb.at[0, pl.ds(h * HD, HD), lanes(i)],
                kv_ss.at[h, i],
                kv_rs.at[h, i],
                mate(i),
            ).wait_recv()

        ring_own[h][0].start()
        ring_own[h][1].start()
        twin_copy(0, h).start()

    @pl.loop(0, 8)
    def _(i):
        remote(
            kv_send.at[2, i], q_t.at[:, lanes(i)], q_ss.at[i], q_rs.at[i], mate(i)
        ).wait_recv()

    def block(step):
        dc = jnp.where(step < 2, step, jnp.where(step < 6, step // 4, step - 6))
        dx = jnp.where(step < 2, 0, jnp.where(step < 6, 3 - 2 * (step % 2), 2))
        return 2 * dx + dc

    def scores_of(b, at):
        return dot(kvb[b, 0:HD, at : at + 256].astype(F32).T.astype(BF16), q_t[...])

    def attend(this, following):
        old = peak[...]
        new = jnp.maximum(old, top[...])
        update = acc[...] * jnp.exp2(old - new)
        highest = None
        for at in range(0, 8 * TOK, 256):
            if following is not None:
                scores = scores_of(following, at)
                here = jnp.max(scores, axis=0, keepdims=True)
                highest = here if highest is None else jnp.maximum(highest, here)
            probs = jnp.exp2(score_buf[at : at + 256, :] - new).astype(BF16)
            update = update + dot(kvb[this, HD : HD + TOK, at : at + 256], probs)
            if following is not None:
                score_buf[at : at + 256, :] = scores
        acc[...] = update
        peak[...] = new
        if following is not None:
            top[...] = highest

    highest = None
    for at in range(0, 8 * TOK, 256):
        scores = scores_of(0, at)
        here = jnp.max(scores, axis=0, keepdims=True)
        highest = here if highest is None else jnp.maximum(highest, here)
        score_buf[at : at + 256, :] = scores
    top[...] = highest

    @pl.loop(1, 8)
    def _(step):
        @pl.when(step == 1)
        def _():
            twin_copy(0, 0).wait_recv()

        @pl.when(step == 2)
        def _():
            ring_own[0][0].wait_recv()
            ring_on[0].start()
            twin_copy(3, 0).start()
            ring_own[0][1].wait_recv()
            twin_copy(1, 0).start()
            twin_copy(0, 1).wait_recv()

        @pl.when(step == 3)
        def _():
            ring_own[1][1].wait_recv()
            ring_on[1].start()
            twin_copy(1, 1).start()
            ring_own[1][0].wait_recv()
            twin_copy(3, 1).start()

        @pl.when(step == 4)
        def _():
            twin_copy(3, 0).wait_recv()

        @pl.when(step == 5)
        def _():
            twin_copy(1, 0).wait_recv()
            twin_copy(3, 1).wait_recv()

        @pl.when(step == 6)
        def _():
            ring_on[0].wait_recv()
            twin_copy(2, 0).start()
            twin_copy(1, 1).wait_recv()

        @pl.when(step == 7)
        def _():
            ring_on[1].wait_recv()
            twin_copy(2, 1).start()
            twin_copy(2, 0).wait_recv()

        attend(block(step - 1), block(step))

    twin_copy(2, 1).wait_recv()
    attend(5, None)

    def o_copy(i, start):
        exchange(
            i,
            o_send.at[i],
            heads_t.at[pl.ds(pl.multiple_of(slot * HD, HD), HD), :],
            o_ss.at[i],
            o_rs.at[slot],
            start,
        )

    @pl.loop(0, 8)
    def _(i):
        o_send[i] = (acc[0:HD, lanes(i)] / acc[HD : HD + 1, lanes(i)]).astype(BF16)
        o_copy(i, True)

    weight_copies[3].wait()

    @pl.loop(0, 8)
    def _(i):
        remote(
            o_send.at[i],
            heads_t.at[pl.ds(pl.multiple_of(i * HD, HD), HD), :],
            o_ss.at[i],
            o_rs.at[i],
            mate(i),
        ).wait_recv()

    heads = heads_t[...].astype(F32).T.astype(BF16)
    proj = dot(heads, ow_buf[...])
    proj_send[...] = proj.astype(BF16)
    proj_copy = remote(proj_send, proj_recv, proj_sem.at[0], proj_sem.at[1], twin)
    proj_copy.start()

    def column(row):
        return jnp.broadcast_to(row, (TOK, TOK)).T

    def fill_spread(dx):
        ids = lax.broadcasted_iota(jnp.int32, (EXPERTS * CAP, TOK), 0).astype(F32)
        hit = jnp.logical_or(ids == info[dx, 0:1, :], ids == info[dx, 1:2, :])
        spread[dx] = hit.astype(F32).astype(BF16)

    def fill_picks(dx):
        ids = lax.broadcasted_iota(jnp.int32, (TOK, EXPERTS * CAP), 1).astype(F32)
        for k in range(2):
            hit = ids == column(info[dx, k : k + 1, :])[:, 0:1]
            picks[dx, k * TOK : (k + 1) * TOK, :] = hit.astype(F32).astype(BF16)
            shares[dx, k] = column(info[dx, 2 + k : 3 + k, :])

    def combine(dx, table):
        rows = dot(picks[dx], table)
        return rows[0:TOK] * shares[dx, 0, :, 0:1] + rows[TOK:] * shares[dx, 1, :, 0:1]

    for dx in (1, 3, 2):
        to_line(info, info_ss, info_rs, 4 - dx).wait_recv()
    for dx in range(4):
        fill_spread(dx)
    proj_copy.wait_recv()
    hidden = tokens[...].astype(F32) + proj + proj_recv[...].astype(F32)
    inverse = lax.rsqrt(jnp.mean(hidden * hidden, axis=1, keepdims=True) + EPS)
    moe = hidden * inverse * norm_moe[...].reshape(1, D)
    sums[0, 0, 0:TOK, :] = hidden[:, 0:HALF]
    sums[0, 1, 0:TOK, :] = hidden[:, HALF:]
    moe_half[2] = sums[0, c, 0:TOK, :]
    moe_half[0] = moe[:, 0:HALF]
    moe_half[1] = moe[:, HALF:]
    mine = moe_half[c].astype(BF16)

    tok_rest[0] = mine[:, BULK:]
    for dx in (2, 1, 3):
        to_line(tok_rest, tok_ss, tok_rs, dx).start()
    rows = dot(spread[0], mine[:, 0:BULK]).reshape(EXPERTS, CAP, BULK)
    disp_bulk[:, 0:CAP, :] = rows[:, :, 0:REST].astype(BF16)
    disp_bulk[:, CAP:, :] = rows[:, :, REST:].astype(BF16)

    def to_plane(p, src, dst, send_sem, recv_sem):
        @pl.when(p == plane)
        def _():
            pltpu.make_async_copy(src.at[p], dst.at[plane], recv_sem.at[plane]).start()

        @pl.when(p != plane)
        def _():
            remote(
                src.at[p], dst.at[plane], send_sem.at[p], recv_sem.at[plane], plane_dev(p)
            ).start()

    def over_plane(src, dst, send_sem, recv_sem, near=False):
        @pl.loop(0, 16)
        def _(i):
            turn = i // 4
            if near:
                a = jnp.where(turn == 2, 3, jnp.where(turn == 3, 2, turn))
            else:
                a = (2 + 3 * turn) % 4
            p = ((z + a) % 4) * 4 + (y + 2 + 3 * i) % 4
            to_plane(p, src, dst, send_sem, recv_sem)

    def plane_gone(src, dst, send_sem, recv_sem, p):
        remote(src.at[p], dst.at[plane], send_sem.at[p], recv_sem.at[plane], plane_dev(p)).wait_send()

    bulk_way = (disp_bulk, x_bulk.at[0, c], d_ss, d_rs)
    rest_way = (disp_rest, x_rest.at[c], e_ss, e_rs)
    over_plane(*bulk_way, near=True)

    def group(a):
        return pl.ds(((z + 4 - a) % 4) * 4, 4)

    def x_ring(to, src_dx, dst_dx, a):
        return remote(
            x_bulk.at[src_dx, c, group(a)],
            x_bulk.at[dst_dx, c, group(a)],
            xr_ss.at[dst_dx, a],
            xr_rs.at[dst_dx, a],
            right if to == 0 else left,
        )

    def x_twin(dx, a, arriving):
        part = x_bulk.at[dx, 1 - c if arriving else c, group(a)]
        return remote(part, part, xt_ss.at[dx, a], xt_rs.at[dx, a], twin)

    def rest_twin(a, arriving):
        part = x_rest.at[1 - c if arriving else c, group(a)]
        return remote(part, part, xe_ss.at[a], xe_rs.at[a], twin)

    def wait_group(a, src, dst, send_sem, recv_sem):
        @pl.loop(0, 4)
        def _(b):
            p = ((z + 4 - a) % 4) * 4 + b
            remote(src.at[p], dst.at[p], send_sem.at[p], recv_sem.at[p], plane_dev(p)).wait_recv()

    def ring_group(a):
        wait_group(a, *bulk_way)
        x_ring(0, 0, 3, a).start()
        x_ring(1, 0, 1, a).start()
        x_twin(0, a, False).start()

    ring_group(GROUPS[0])
    disp_wide[:, 0:CAP, :] = dot(spread[0], tok_rest[0]).reshape(EXPERTS, CAP, REST)
    for dx in (1, 3, 2):
        to_line(tok_rest, tok_ss, tok_rs, 4 - dx).wait_recv()
        disp_wide[:, dx * CAP : (dx + 1) * CAP, :] = dot(spread[dx], tok_rest[dx]).reshape(
            EXPERTS, CAP, REST
        )
    disp_rest[...] = disp_wide[...].astype(BF16)
    over_plane(*rest_way)

    for a in GROUPS[1:]:
        ring_group(a)
    for dx in range(4):
        fill_picks(dx)

    def y_copy(dx):
        return remote(y_send.at[dx], y_recv.at[dx], y_ss.at[dx], y_rs.at[dx], twin)

    def first_part(dx):
        for core in range(2):
            piece = x_bulk[dx, core].astype(F32)
            for h in range(2):
                at = core * BULK + h * REST
                rows_bulk[:, at : at + REST] = (
                    piece[:, h * CAP : (h + 1) * CAP, :].reshape(EXPERTS * CAP, REST).astype(BF16)
                )
        for k in range(2):
            sums[dx, k] = dot(rows_bulk[...], w_buf[1 + k, 0 : 2 * BULK, :])

    def second_part(dx):
        rows = rows_rest[dx]
        gate = sums[dx, 0] + dot(rows, w_buf[1, 2 * BULK :, :])
        up = sums[dx, 1] + dot(rows, w_buf[2, 2 * BULK :, :])
        active = (gate / (1.0 + jnp.exp(-gate)) * up).astype(BF16)
        y_send[dx] = dot(active, wd_buf[1 - c]).astype(BF16)
        y_copy(dx).start()
        sums[dx, 0] = dot(active, wd_buf[c])

    def settle(dx):
        y_copy(dx).wait_recv()
        total = (sums[dx, 0] + y_recv[dx].astype(F32)).reshape(EXPERTS, CAP, HALF)
        parts[dx, :, 0:CAP, :] = total[:, :, 0:REST].astype(BF16)
        parts[dx, :, CAP:, :] = total[:, :, REST:BULK].astype(BF16)
        pair, at = (0 if dx in (1, 3) else 1), (0 if dx > 1 else CAP)
        rest_send[pair, :, at : at + CAP, :] = total[:, :, BULK:].astype(BF16)

    for copy in weight_copies[4:]:
        copy.wait()
    def piece_of(h, q):
        return pl.ds(8 * h + 4 * q, 4)

    def far_copy(h, q):
        return remote(
            parts.at[2, piece_of(h, q)],
            diag_recv.at[h, pl.ds(4 * q, 4)],
            r_ss.at[h, q],
            r_rs.at[h, q],
            right if h == 0 else left,
        )

    def near_copy(dx, h, q):
        number = 2 + (dx // 2) * 2 + h
        return remote(
            parts.at[dx, piece_of(h, q)],
            side_recv.at[dx // 2, piece_of(h, q)],
            r_ss.at[number, q],
            r_rs.at[number, q],
            right if dx == 1 else left,
        )

    rest_back = [
        (rest_send.at[pair], rest_recv.at[pair], rest_ss.at[pair], rest_rs.at[pair])
        for pair in range(2)
    ]
    back_way = (back, ret, b_ss, b_rs)

    def sum_copy(dx):
        return remote(
            sum_send.at[dx], sum_recv.at[4 - dx], sum_ss.at[dx], sum_rs.at[4 - dx], along(dx)
        )

    @pl.loop(0, 8)
    def _(step):
        def at(number):
            return pl.when(step == number)

        @at(0)
        def _():
            for a in GROUPS:
                x_twin(0, a, True).wait_recv()

        @at(1)
        def _():
            for i, a in enumerate(GROUPS):
                x_ring(0, 0, 3, a).wait_recv()
                if i < 2:
                    x_ring(0, 3, 2, a).start()
                x_twin(3, a, False).start()
                x_ring(1, 0, 1, a).wait_recv()
                if i >= 2:
                    x_ring(1, 1, 2, a).start()
                x_twin(1, a, False).start()
            for a in GROUPS:
                x_twin(3, a, True).wait_recv()

        @at(2)
        def _():
            for a in GROUPS:
                x_twin(1, a, True).wait_recv()

        @at(3)
        def _():
            for a in ORDER:
                wait_group(a, *rest_way)
                rest_twin(a, False).start()
            for a in ORDER:
                rest_twin(a, True).wait_recv()
            for core in range(2):
                wide = x_rest[core].astype(F32)
                for dx in range(4):
                    rows_rest[dx, :, core * REST : (core + 1) * REST] = (
                        wide[:, dx * CAP : (dx + 1) * CAP, :]
                        .reshape(EXPERTS * CAP, REST)
                        .astype(BF16)
                    )

        @at(4)
        def _():
            for i, a in enumerate(GROUPS):
                x_ring(0 if i < 2 else 1, 0, 2, a).wait_recv()
                x_twin(2, a, False).start()

        @at(5)
        def _():
            for a in GROUPS:
                x_twin(2, a, True).wait_recv()

        @at(6)
        def _():
            settle(3)
            for q in range(2):
                near_copy(3, 0, q).start()
            settle(1)
            for q in range(2):
                near_copy(1, 1, q).start()
            over_plane(*rest_back[0])

        @at(7)
        def _():
            settle(2)
            for q in range(2):
                far_copy(0, q).start()
                far_copy(1, q).start()

        is_first = jnp.logical_or(step < 3, step == 5)
        dx = jnp.where(
            jnp.logical_or(step == 0, step == 7),
            0,
            jnp.where(
                jnp.logical_or(step == 1, step == 3),
                3,
                jnp.where(jnp.logical_or(step == 2, step == 4), 1, 2),
            ),
        )

        @pl.when(is_first)
        def _():
            first_part(dx)

        @pl.when(jnp.logical_not(is_first))
        def _():
            second_part(dx)

    settle(0)
    over_plane(*rest_back[1])
    for q in range(2):
        for h, dx in ((0, 1), (1, 3)):
            far_copy(h, q).wait_recv()
            at = slice(8 * h + 4 * q, 8 * h + 4 * q + 4)
            far_part = diag_recv[h, 4 * q : 4 * q + 4].astype(F32)
            parts[dx, at] = (parts[dx, at].astype(F32) + far_part).astype(BF16)
            near_copy(dx, h, q).start()

    def rest_sums(pair):
        @pl.loop(0, 16)
        def _(p):
            remote(
                rest_send.at[pair, p],
                rest_recv.at[pair, p],
                rest_ss.at[pair, p],
                rest_rs.at[pair, p],
                plane_dev(p),
            ).wait_recv()

        both = rest_recv[pair].astype(F32)
        found = []
        for i, dx in enumerate((3, 1) if pair == 0 else (2, 0)):
            table = both[:, i * CAP : (i + 1) * CAP, :].reshape(EXPERTS * CAP, REST).astype(BF16)
            found.append(combine(dx, table))
        return found

    for q in range(2):
        for h in range(2):
            near_copy(1, h, q).wait_recv()
            near_copy(3, h, q).wait_recv()
            at = slice(8 * h + 4 * q, 8 * h + 4 * q + 4)
            near_parts = side_recv[0, at].astype(F32) + side_recv[1, at].astype(F32)
            back[at] = (parts[0, at].astype(F32) + near_parts).astype(BF16)

        @pl.loop(0, 8)
        def _(i):
            to_plane(2 * 4 * far(i) + 4 * q + (y + 2 + 3 * (i // 2)) % 4, *back_way)

        if q == 0:
            found = rest_sums(0)
            for i, dx in enumerate((3, 1)):
                sum_send[dx] = found[i].astype(BF16)
                sum_copy(dx).start()

    found = rest_sums(1)
    sum_send[2] = found[0].astype(BF16)
    sum_copy(2).start()
    rest = moe_half[2, :, BULK:] + found[1]
    for dx in (2, 1, 3):
        sum_copy(4 - dx).wait_recv()
        rest = rest + sum_recv[dx].astype(F32)
    out[:, BULK:] = rest.astype(BF16)

    @pl.loop(0, 16)
    def _(p):
        remote(back.at[p], ret.at[p], b_ss.at[p], b_rs.at[p], plane_dev(p)).wait_recv()

    both = ret[...].astype(F32)
    for h in range(2):
        cols = slice(h * REST, (h + 1) * REST)
        table = both[:, h * CAP : (h + 1) * CAP, :].reshape(EXPERTS * CAP, REST).astype(BF16)
        out[:, cols] = (moe_half[2, :, cols] + combine(0, table)).astype(BF16)

    @pl.loop(0, 8)
    def _(i):
        kv_copy(0, i, False)
        kv_copy(1, i, False)
        q_copy(i, False)
        o_copy(i, False)

    for h in range(2):
        ring_own[h][0].wait_send()
        ring_own[h][1].wait_send()
        ring_on[h].wait_send()
        for dx in range(4):
            twin_copy(dx, h).wait_send()
    proj_copy.wait_send()

    @pl.loop(0, 16)
    def _(p):
        @pl.when(p != plane)
        def _():
            for way in (bulk_way, rest_way, rest_back[0], rest_back[1], back_way):
                plane_gone(*way, p)

    for dx in (1, 2, 3):
        to_line(info, info_ss, info_rs, dx).wait_send()
        to_line(tok_rest, tok_ss, tok_rs, dx).wait_send()
        sum_copy(dx).wait_send()
    for i, a in enumerate(GROUPS):
        x_ring(0, 0, 3, a).wait_send()
        x_ring(1, 0, 1, a).wait_send()
        (x_ring(0, 3, 2, a) if i < 2 else x_ring(1, 1, 2, a)).wait_send()
        for dx in range(4):
            x_twin(dx, a, False).wait_send()
        rest_twin(a, False).wait_send()
    for dx in range(4):
        y_copy(dx).wait_send()
    for h in range(2):
        for q in range(2):
            far_copy(h, q).wait_send()
            near_copy(1, h, q).wait_send()
            near_copy(3, h, q).wait_send()


def on_device(
    tokens,
    attn_weight,
    out_weight,
    norm_attn,
    norm_moe,
    routes,
    route_weight,
    expert_in,
    expert_out,
):
    vmem = pl.BlockSpec(memory_space=pltpu.VMEM)
    hbm = pl.BlockSpec(memory_space=pl.ANY)
    dma = pltpu.SemaphoreType.DMA
    pairs = (EXPERTS, 2 * CAP, REST)
    fours = (EXPERTS, 4 * CAP, REST)
    scratch = [
        pltpu.VMEM((TOK, D), BF16),
        pltpu.VMEM((D,), F32),
        pltpu.VMEM((D,), F32),
        pltpu.VMEM((2, TOK), jnp.int32),
        pltpu.VMEM((2, TOK), F32),
        dma((5,)),
        pltpu.VMEM((3, D, HALF), BF16),
        pltpu.VMEM((HALF, D), BF16),
        pltpu.VMEM((2, HALF, HALF), BF16),
        dma((14,)),
        pltpu.VMEM((TOK, D), BF16),
        pltpu.VMEM((3, 8, HD, TOK), BF16),
        pltpu.VMEM((HD, 8 * TOK), BF16),
        pltpu.VMEM((8, 2 * HD + 32, 8 * TOK), BF16),
        pltpu.VMEM((8 * TOK, 8 * TOK), F32),
        pltpu.VMEM((1, 8 * TOK), F32),
        pltpu.VMEM((1, 8 * TOK), F32),
        pltpu.VMEM((TOK, 8 * TOK), F32),
        pltpu.VMEM((8, HD, TOK), BF16),
        pltpu.VMEM((HALF, TOK), BF16),
        pltpu.VMEM((TOK, D), BF16),
        pltpu.VMEM((TOK, D), BF16),
        pltpu.VMEM((3, TOK, HALF), F32),
        pltpu.VMEM((4, 8, TOK), F32),
        pltpu.VMEM((4, EXPERTS * CAP, TOK), BF16),
        pltpu.VMEM((4, 2 * TOK, EXPERTS * CAP), BF16),
        pltpu.VMEM((4, 2, TOK, TOK), F32),
        pltpu.VMEM((4, TOK, REST), BF16),
        pltpu.VMEM(pairs, BF16),
        pltpu.VMEM(fours, F32),
        pltpu.VMEM(fours, BF16),
        pltpu.VMEM((4, 2) + pairs, BF16),
        pltpu.VMEM((2,) + fours, BF16),
        pltpu.VMEM((EXPERTS * CAP, 2 * BULK), BF16),
        pltpu.VMEM((4, EXPERTS * CAP, 2 * REST), BF16),
        pltpu.VMEM((4, 2, EXPERTS * CAP, HALF), F32),
        pltpu.VMEM((4, EXPERTS * CAP, HALF), BF16),
        pltpu.VMEM((4, EXPERTS * CAP, HALF), BF16),
        pltpu.VMEM((4,) + pairs, BF16),
        pltpu.VMEM((2, 8, 2 * CAP, REST), BF16),
        pltpu.VMEM((2,) + pairs, BF16),
        pltpu.VMEM(pairs, BF16),
        pltpu.VMEM(pairs, BF16),
        pltpu.VMEM((2,) + pairs, BF16),
        pltpu.VMEM((2,) + pairs, BF16),
        pltpu.VMEM((4, TOK, REST), BF16),
        pltpu.VMEM((4, TOK, REST), BF16),
        dma((2, 8)),
        dma((2, 8)),
        dma((8,)),
        dma((8,)),
        dma((4, 2)),
        dma((4, 2)),
        dma((4, 2)),
        dma((4, 2)),
        dma((8,)),
        dma((8,)),
        dma((2,)),
        dma((4,)),
        dma((4,)),
        dma((4,)),
        dma((4,)),
        dma((16,)),
        dma((16,)),
        dma((16,)),
        dma((16,)),
        dma((4, 4)),
        dma((4, 4)),
        dma((4, 4)),
        dma((4, 4)),
        dma((4,)),
        dma((4,)),
        dma((4,)),
        dma((4,)),
        dma((6, 2)),
        dma((6, 2)),
        dma((2, 16)),
        dma((2, 16)),
        dma((4,)),
        dma((4,)),
        dma((16,)),
        dma((16,)),
    ]
    return pl.pallas_call(
        layer_kernel,
        out_shape=jax.ShapeDtypeStruct((TOK, HALF), BF16),
        in_specs=[hbm] * 9,
        out_specs=vmem,
        scratch_shapes=scratch,
        compiler_params=pltpu.CompilerParams(
            collective_id=0, has_side_effects=True, vmem_limit_bytes=60 * 1024 * 1024
        ),
        cost_estimate=pl.CostEstimate(
            flops=30_000_000_000, bytes_accessed=17_000_000, transcendentals=9_000_000
        ),
    )(
        tokens,
        attn_weight,
        out_weight,
        norm_attn,
        norm_moe,
        routes.T,
        route_weight.T,
        expert_in,
        expert_out,
    )


def solution(mesh):
    return jax.shard_map(
        on_device,
        mesh=mesh,
        in_specs=(
            P("seq", None),
            P(None, None, "tensor"),
            P("tensor", None),
            P(),
            P(),
            P("seq", None),
            P("seq", None),
            P("seq", None, None, "tensor"),
            P("seq", "tensor", None),
        ),
        out_specs=P("seq", "tensor"),
        check_vma=False,
    )
```

```python
import math

import jax
import jax.numpy as jnp
from jax import lax
from jax.experimental import pallas as pl
from jax.experimental.pallas import tpu as pltpu
from jax.sharding import PartitionSpec as P

MESH = pl.DeviceIdType.MESH
D = 1536
HALF = 768
BULK = 512
REST = 256
ORDER = (2, 1, 3, 0)
GROUPS = (0, 1, 3, 2)
HD = 96
TOK = 128
EXPERTS = 16
CAP = 24
EPS = 1e-6
F32 = jnp.float32
BF16 = jnp.bfloat16
SCALE = HD ** (-0.5) * math.log2(math.e)


def dot(a, b):
    return jnp.dot(a, b, preferred_element_type=F32)


def remote(src, dst, send_sem, recv_sem, device):
    return pltpu.make_async_remote_copy(
        src_ref=src,
        dst_ref=dst,
        send_sem=send_sem,
        recv_sem=recv_sem,
        device_id=device,
        device_id_type=MESH,
    )


def layer_kernel(
    tokens_in,
    attn_w,
    out_w,
    norm_attn_in,
    norm_moe_in,
    routes_in,
    route_weight_in,
    expert_in,
    expert_out,
    out,
    tokens,
    norm_attn,
    norm_moe,
    routes,
    route_weight,
    small_sem,
    w_buf,
    ow_buf,
    wd_buf,
    w_sem,
    normed_buf,
    kv_send,
    q_t,
    kvb,
    score_buf,
    top,
    peak,
    acc,
    o_send,
    heads_t,
    proj_send,
    proj_recv,
    moe_half,
    info,
    spread,
    picks,
    shares,
    tok_rest,
    disp_bulk,
    disp_wide,
    disp_rest,
    x_bulk,
    x_rest,
    rows_bulk,
    rows_rest,
    sums,
    y_send,
    y_recv,
    parts,
    diag_recv,
    side_recv,
    back,
    ret,
    rest_send,
    rest_recv,
    sum_send,
    sum_recv,
    kv_ss,
    kv_rs,
    q_ss,
    q_rs,
    ring_ss,
    ring_rs,
    twin_ss,
    twin_rs,
    o_ss,
    o_rs,
    proj_sem,
    info_ss,
    info_rs,
    tok_ss,
    tok_rs,
    d_ss,
    d_rs,
    e_ss,
    e_rs,
    xr_ss,
    xr_rs,
    xt_ss,
    xt_rs,
    xe_ss,
    xe_rs,
    y_ss,
    y_rs,
    r_ss,
    r_rs,
    rest_ss,
    rest_rs,
    sum_ss,
    sum_rs,
    b_ss,
    b_rs,
):
    s = lax.axis_index("seq")
    c = lax.axis_index("tensor")
    x = s % 4
    plane = s // 4
    z = plane // 4
    y = plane % 4
    side = z // 2
    slot = (z % 2) * 4 + y
    left = (s - x + (x + 3) % 4, c)
    right = (s - x + (x + 1) % 4, c)
    twin = (s, 1 - c)

    def along(dx):
        return (s - x + (x + dx) % 4, c)

    def mate(i):
        return ((2 * c + i // 4) * 16 + (i % 4) * 4 + x, side)

    def is_me(i):
        return jnp.logical_and(c == side, i == slot)

    def plane_dev(p):
        return (p * 4 + x, c)

    barrier = pltpu.get_barrier_semaphore()

    def greet(device):
        pl.semaphore_signal(barrier, inc=1, device_id=device, device_id_type=MESH)

    for device in (left, right, along(2), twin):
        greet(device)

    @pl.loop(0, 8)
    def _(i):
        @pl.when(jnp.logical_not(is_me(i)))
        def _():
            greet(mate(i))

    @pl.loop(0, 16)
    def _(p):
        @pl.when(p != plane)
        def _():
            greet(plane_dev(p))

    small = [
        pltpu.make_async_copy(src, dst, small_sem.at[i])
        for i, (src, dst) in enumerate(
            (
                (tokens_in, tokens),
                (norm_attn_in, norm_attn),
                (routes_in, routes),
                (route_weight_in, route_weight),
                (norm_moe_in, norm_moe),
            )
        )
    ]
    for copy in small:
        copy.start()

    weight_copies = [
        pltpu.make_async_copy(attn_w.at[1], w_buf.at[1], w_sem.at[1]),
        pltpu.make_async_copy(attn_w.at[2], w_buf.at[2], w_sem.at[2]),
        pltpu.make_async_copy(attn_w.at[0], w_buf.at[0], w_sem.at[0]),
        pltpu.make_async_copy(out_w, ow_buf, w_sem.at[3]),
        pltpu.make_async_copy(expert_out.at[0, :, pl.ds(0, HALF)], wd_buf.at[0], w_sem.at[4]),
        pltpu.make_async_copy(expert_out.at[0, :, pl.ds(HALF, HALF)], wd_buf.at[1], w_sem.at[5]),
    ]
    moves = (
        (0, 0, BULK),
        (HALF, BULK, BULK),
        (BULK, 2 * BULK, REST),
        (HALF + BULK, 2 * BULK + REST, REST),
    )
    weight_copies += [
        pltpu.make_async_copy(
            expert_in.at[0, k, pl.ds(start, rows)],
            w_buf.at[1 + k, pl.ds(to, rows)],
            w_sem.at[6 + 4 * k + i],
        )
        for k in range(2)
        for i, (start, to, rows) in enumerate(moves)
    ]
    for copy in weight_copies[:3]:
        copy.start()

    small[0].wait()
    small[1].wait()
    tok = tokens[...].astype(F32)
    mean_square = jnp.mean(tok * tok, axis=1, keepdims=True)
    normed_buf[...] = (tok * lax.rsqrt(mean_square + EPS) * norm_attn[...].reshape(1, D)).astype(BF16)

    def exchange(i, src, dst, send_sem, recv_sem, start):
        copy = remote(src, dst, send_sem, recv_sem, mate(i))

        @pl.when(jnp.logical_not(is_me(i)))
        def _():
            if start:
                copy.start()
            else:
                copy.wait_send()

        if start:

            @pl.when(is_me(i))
            def _():
                pltpu.make_async_copy(src, dst, recv_sem).start()

    def far(a):
        return (z + jnp.where(c == side, 1, 0) + a) % 2

    def lanes(i):
        return pl.ds(pl.multiple_of(i * TOK, TOK), TOK)

    def kv_copy(h, i, start):
        exchange(
            i,
            kv_send.at[h, i],
            kvb.at[0, pl.ds(h * HD, HD), lanes(slot)],
            kv_ss.at[h, i],
            kv_rs.at[h, slot],
            start,
        )

    def q_copy(i, start):
        exchange(i, kv_send.at[2, i], q_t.at[:, lanes(slot)], q_ss.at[i], q_rs.at[slot], start)

    @pl.loop(0, 3)
    def _(h):
        at = (h + 1) % 3
        pltpu.make_async_copy(attn_w.at[at], w_buf.at[at], w_sem.at[at]).wait()
        scale = jnp.where(h == 2, SCALE, 1.0)
        kv_send[h] = (dot(normed_buf[...], w_buf[at]) * scale).T.astype(BF16).reshape(8, HD, TOK)

    for copy in weight_copies[3:]:
        copy.start()

    @pl.loop(0, 8)
    def _(b):
        kvb[b, 2 * HD : 2 * HD + 32, :] = jnp.ones((32, 8 * TOK), BF16)

    peak[...] = jnp.full(peak.shape, -1e30, F32)
    acc[...] = jnp.zeros(acc.shape, F32)

    for copy in small[2:]:
        copy.wait()
    expert_ids = lax.broadcasted_iota(jnp.int32, (EXPERTS, TOK), 0)
    hot = [(routes[k : k + 1, :] == expert_ids).astype(F32) for k in range(2)]
    earlier = (
        lax.broadcasted_iota(jnp.int32, (TOK, TOK), 0)
        < lax.broadcasted_iota(jnp.int32, (TOK, TOK), 1)
    ).astype(BF16)
    before = dot((hot[0] + hot[1]).astype(BF16), earlier)
    place = [
        jnp.sum(before * hot[k], axis=0, keepdims=True)
        + routes[k : k + 1, :].astype(F32) * float(CAP)
        for k in range(2)
    ]
    info[0] = jnp.zeros((8, TOK), F32)
    for k in range(2):
        info[0, k : k + 1, :] = place[k]
        info[0, 2 + k : 3 + k, :] = route_weight[k : k + 1, :]

    pl.semaphore_wait(barrier, 4 + 15 + 8 - jnp.where(c == side, 1, 0))
    @pl.loop(0, 16)
    def _(i):
        kv_copy(i // 8, far(i) * 4 + (y + 2 + 3 * (i // 2)) % 4, True)

    @pl.loop(0, 8)
    def _(i):
        q_copy(far(i) * 4 + (y + 2 + 3 * (i // 2)) % 4, True)

    def to_line(ref, send_sem, recv_sem, dx):
        return remote(
            ref.at[0], ref.at[4 - dx], send_sem.at[dx], recv_sem.at[4 - dx], along(dx)
        )

    for dx in (2, 1, 3):
        to_line(info, info_ss, info_rs, dx).start()

    def kv_part(dx, dc, h):
        return kvb.at[2 * dx + dc, pl.ds(h * HD, HD)]

    def ring_part(dx, h, part):
        if part is None:
            return kv_part(dx, 0, h)
        return kvb.at[2 * dx, pl.ds(h * HD, HD), pl.ds(part * 4 * TOK, 4 * TOK)]

    def ring_copy(to, src_dx, dst_dx, h, part=None):
        return remote(
            ring_part(src_dx, h, part),
            ring_part(dst_dx, h, part),
            ring_ss.at[dst_dx, h, part or 0],
            ring_rs.at[dst_dx, h, part or 0],
            right if to == 0 else left,
        )

    def twin_copy(dx, h):
        return remote(kv_part(dx, 0, h), kv_part(dx, 1, h), twin_ss.at[dx, h], twin_rs.at[dx, h], twin)

    ring_own = [
        [[ring_copy(0, 0, 3, 0)], [ring_copy(1, 0, 1, 0)]],
        [[ring_copy(0, 0, 3, 1)], [ring_copy(1, 0, 1, 1, part) for part in range(2)]],
    ]
    ring_on = [[ring_copy(0, 3, 2, 0)], [ring_copy(1, 1, 2, 1, part) for part in range(2)]]
    for h in range(2):

        @pl.loop(0, 8)
        def _(i):
            remote(
                kv_send.at[h, i],
                kvb.at[0, pl.ds(h * HD, HD), lanes(i)],
                kv_ss.at[h, i],
                kv_rs.at[h, i],
                mate(i),
            ).wait_recv()

        for copy in ring_own[h][0] + ring_own[h][1]:
            copy.start()
        twin_copy(0, h).start()

    @pl.loop(0, 8)
    def _(i):
        remote(
            kv_send.at[2, i], q_t.at[:, lanes(i)], q_ss.at[i], q_rs.at[i], mate(i)
        ).wait_recv()

    def block(step):
        dc = jnp.where(step < 2, step, jnp.where(step < 6, step // 4, step - 6))
        dx = jnp.where(step < 2, 0, jnp.where(step < 6, 3 - 2 * (step % 2), 2))
        return 2 * dx + dc

    def scores_of(b, at):
        return dot(kvb[b, 0:HD, at : at + 256].astype(F32).T.astype(BF16), q_t[...])

    def attend(this, following):
        old = peak[...]
        new = jnp.maximum(old, top[...])
        update = acc[...] * jnp.exp2(old - new)
        highest = None
        for at in range(0, 8 * TOK, 256):
            if following is not None:
                scores = scores_of(following, at)
                here = jnp.max(scores, axis=0, keepdims=True)
                highest = here if highest is None else jnp.maximum(highest, here)
            probs = jnp.exp2(score_buf[at : at + 256, :] - new).astype(BF16)
            update = update + dot(kvb[this, HD : HD + TOK, at : at + 256], probs)
            if following is not None:
                score_buf[at : at + 256, :] = scores
        acc[...] = update
        peak[...] = new
        if following is not None:
            top[...] = highest

    highest = None
    for at in range(0, 8 * TOK, 256):
        scores = scores_of(0, at)
        here = jnp.max(scores, axis=0, keepdims=True)
        highest = here if highest is None else jnp.maximum(highest, here)
        score_buf[at : at + 256, :] = scores
    top[...] = highest

    @pl.loop(1, 8)
    def _(step):
        @pl.when(step == 1)
        def _():
            twin_copy(0, 0).wait_recv()

        @pl.when(step == 2)
        def _():
            ring_own[0][0][0].wait_recv()
            ring_on[0][0].start()
            twin_copy(3, 0).start()
            ring_own[0][1][0].wait_recv()
            twin_copy(1, 0).start()
            twin_copy(0, 1).wait_recv()

        @pl.when(step == 3)
        def _():
            for part in range(2):
                ring_own[1][1][part].wait_recv()
                ring_on[1][part].start()
            twin_copy(1, 1).start()
            ring_own[1][0][0].wait_recv()
            twin_copy(3, 1).start()

        @pl.when(step == 4)
        def _():
            twin_copy(3, 0).wait_recv()

        @pl.when(step == 5)
        def _():
            twin_copy(1, 0).wait_recv()
            twin_copy(3, 1).wait_recv()

        @pl.when(step == 6)
        def _():
            ring_on[0][0].wait_recv()
            twin_copy(2, 0).start()
            twin_copy(1, 1).wait_recv()

        @pl.when(step == 7)
        def _():
            for copy in ring_on[1]:
                copy.wait_recv()
            twin_copy(2, 1).start()
            twin_copy(2, 0).wait_recv()

        attend(block(step - 1), block(step))

    twin_copy(2, 1).wait_recv()
    attend(5, None)

    def o_copy(i, start):
        exchange(
            i,
            o_send.at[i],
            heads_t.at[pl.ds(pl.multiple_of(slot * HD, HD), HD), :],
            o_ss.at[i],
            o_rs.at[slot],
            start,
        )

    @pl.loop(0, 8)
    def _(i):
        o_send[i] = (acc[0:HD, lanes(i)] / acc[HD : HD + 1, lanes(i)]).astype(BF16)
        o_copy(i, True)

    weight_copies[3].wait()

    @pl.loop(0, 8)
    def _(i):
        remote(
            o_send.at[i],
            heads_t.at[pl.ds(pl.multiple_of(i * HD, HD), HD), :],
            o_ss.at[i],
            o_rs.at[i],
            mate(i),
        ).wait_recv()

    heads = heads_t[...].astype(F32).T.astype(BF16)
    proj = dot(heads, ow_buf[...])
    proj_send[...] = proj.astype(BF16)
    proj_copy = remote(proj_send, proj_recv, proj_sem.at[0], proj_sem.at[1], twin)
    proj_copy.start()

    def column(row):
        return jnp.broadcast_to(row, (TOK, TOK)).T

    def fill_spread(dx):
        ids = lax.broadcasted_iota(jnp.int32, (EXPERTS * CAP, TOK), 0).astype(F32)
        hit = jnp.logical_or(ids == info[dx, 0:1, :], ids == info[dx, 1:2, :])
        spread[dx] = hit.astype(F32).astype(BF16)

    def fill_picks(dx):
        ids = lax.broadcasted_iota(jnp.int32, (TOK, EXPERTS * CAP), 1).astype(F32)
        for k in range(2):
            hit = ids == column(info[dx, k : k + 1, :])[:, 0:1]
            picks[dx, k * TOK : (k + 1) * TOK, :] = hit.astype(F32).astype(BF16)
            shares[dx, k] = column(info[dx, 2 + k : 3 + k, :])

    def combine(dx, table):
        rows = dot(picks[dx], table)
        return rows[0:TOK] * shares[dx, 0, :, 0:1] + rows[TOK:] * shares[dx, 1, :, 0:1]

    for dx in (1, 3, 2):
        to_line(info, info_ss, info_rs, 4 - dx).wait_recv()
    for dx in range(4):
        fill_spread(dx)
    proj_copy.wait_recv()
    hidden = tokens[...].astype(F32) + proj + proj_recv[...].astype(F32)
    inverse = lax.rsqrt(jnp.mean(hidden * hidden, axis=1, keepdims=True) + EPS)
    moe = hidden * inverse * norm_moe[...].reshape(1, D)
    sums[0, 0, 0:TOK, :] = hidden[:, 0:HALF]
    sums[0, 1, 0:TOK, :] = hidden[:, HALF:]
    moe_half[2] = sums[0, c, 0:TOK, :]
    moe_half[0] = moe[:, 0:HALF]
    moe_half[1] = moe[:, HALF:]
    mine = moe_half[c].astype(BF16)

    tok_rest[0] = mine[:, BULK:]
    for dx in (2, 1, 3):
        to_line(tok_rest, tok_ss, tok_rs, dx).start()
    rows = dot(spread[0], mine[:, 0:BULK]).reshape(EXPERTS, CAP, BULK)
    disp_bulk[:, 0:CAP, :] = rows[:, :, 0:REST].astype(BF16)
    disp_bulk[:, CAP:, :] = rows[:, :, REST:].astype(BF16)

    def to_plane(p, src, dst, send_sem, recv_sem):
        @pl.when(p == plane)
        def _():
            pltpu.make_async_copy(src.at[p], dst.at[plane], recv_sem.at[plane]).start()

        @pl.when(p != plane)
        def _():
            remote(
                src.at[p], dst.at[plane], send_sem.at[p], recv_sem.at[plane], plane_dev(p)
            ).start()

    def over_plane(src, dst, send_sem, recv_sem, near=False):
        @pl.loop(0, 16)
        def _(i):
            turn = i // 4
            if near:
                a = jnp.where(turn == 2, 3, jnp.where(turn == 3, 2, turn))
            else:
                a = (2 + 3 * turn) % 4
            p = ((z + a) % 4) * 4 + (y + 2 + 3 * i) % 4
            to_plane(p, src, dst, send_sem, recv_sem)

    def plane_gone(src, dst, send_sem, recv_sem, p):
        remote(src.at[p], dst.at[plane], send_sem.at[p], recv_sem.at[plane], plane_dev(p)).wait_send()

    bulk_way = (disp_bulk, x_bulk.at[0, c], d_ss, d_rs)
    rest_way = (disp_rest, x_rest.at[c], e_ss, e_rs)
    over_plane(*bulk_way, near=True)

    def group(a):
        return pl.ds(((z + 4 - a) % 4) * 4, 4)

    def x_ring(to, src_dx, dst_dx, a):
        return remote(
            x_bulk.at[src_dx, c, group(a)],
            x_bulk.at[dst_dx, c, group(a)],
            xr_ss.at[dst_dx, a],
            xr_rs.at[dst_dx, a],
            right if to == 0 else left,
        )

    def x_twin(dx, a, arriving):
        part = x_bulk.at[dx, 1 - c if arriving else c, group(a)]
        return remote(part, part, xt_ss.at[dx, a], xt_rs.at[dx, a], twin)

    def rest_twin(a, arriving):
        part = x_rest.at[1 - c if arriving else c, group(a)]
        return remote(part, part, xe_ss.at[a], xe_rs.at[a], twin)

    def wait_group(a, src, dst, send_sem, recv_sem):
        @pl.loop(0, 4)
        def _(b):
            p = ((z + 4 - a) % 4) * 4 + b
            remote(src.at[p], dst.at[p], send_sem.at[p], recv_sem.at[p], plane_dev(p)).wait_recv()

    def ring_group(a):
        wait_group(a, *bulk_way)
        x_ring(0, 0, 3, a).start()
        x_ring(1, 0, 1, a).start()
        x_twin(0, a, False).start()

    ring_group(GROUPS[0])
    disp_wide[:, 0:CAP, :] = dot(spread[0], tok_rest[0]).reshape(EXPERTS, CAP, REST)
    for dx in (1, 3, 2):
        to_line(tok_rest, tok_ss, tok_rs, 4 - dx).wait_recv()
        disp_wide[:, dx * CAP : (dx + 1) * CAP, :] = dot(spread[dx], tok_rest[dx]).reshape(
            EXPERTS, CAP, REST
        )
    disp_rest[...] = disp_wide[...].astype(BF16)
    over_plane(*rest_way)

    for a in GROUPS[1:]:
        ring_group(a)
    for dx in range(4):
        fill_picks(dx)

    def y_copy(dx):
        return remote(y_send.at[dx], y_recv.at[dx], y_ss.at[dx], y_rs.at[dx], twin)

    def first_part(dx):
        for core in range(2):
            piece = x_bulk[dx, core].astype(F32)
            for h in range(2):
                at = core * BULK + h * REST
                rows_bulk[:, at : at + REST] = (
                    piece[:, h * CAP : (h + 1) * CAP, :].reshape(EXPERTS * CAP, REST).astype(BF16)
                )
        for k in range(2):
            sums[dx, k] = dot(rows_bulk[...], w_buf[1 + k, 0 : 2 * BULK, :])

    def second_part(dx):
        rows = rows_rest[dx]
        gate = sums[dx, 0] + dot(rows, w_buf[1, 2 * BULK :, :])
        up = sums[dx, 1] + dot(rows, w_buf[2, 2 * BULK :, :])
        active = (gate / (1.0 + jnp.exp(-gate)) * up).astype(BF16)
        y_send[dx] = dot(active, wd_buf[1 - c]).astype(BF16)
        y_copy(dx).start()
        sums[dx, 0] = dot(active, wd_buf[c])

    def settle(dx):
        y_copy(dx).wait_recv()
        total = (sums[dx, 0] + y_recv[dx].astype(F32)).reshape(EXPERTS, CAP, HALF)
        parts[dx, :, 0:CAP, :] = total[:, :, 0:REST].astype(BF16)
        parts[dx, :, CAP:, :] = total[:, :, REST:BULK].astype(BF16)
        pair, at = (0 if dx in (1, 3) else 1), (0 if dx > 1 else CAP)
        rest_send[pair, :, at : at + CAP, :] = total[:, :, BULK:].astype(BF16)

    for copy in weight_copies[4:]:
        copy.wait()
    def piece_of(h, q):
        return pl.ds(8 * h + 4 * q, 4)

    def far_copy(h, q):
        return remote(
            parts.at[2, piece_of(h, q)],
            diag_recv.at[h, pl.ds(4 * q, 4)],
            r_ss.at[h, q],
            r_rs.at[h, q],
            right if h == 0 else left,
        )

    def near_copy(dx, h, q):
        number = 2 + (dx // 2) * 2 + h
        return remote(
            parts.at[dx, piece_of(h, q)],
            side_recv.at[dx // 2, piece_of(h, q)],
            r_ss.at[number, q],
            r_rs.at[number, q],
            right if dx == 1 else left,
        )

    rest_back = [
        (rest_send.at[pair], rest_recv.at[pair], rest_ss.at[pair], rest_rs.at[pair])
        for pair in range(2)
    ]
    back_way = (back, ret, b_ss, b_rs)

    def sum_copy(dx):
        return remote(
            sum_send.at[dx], sum_recv.at[4 - dx], sum_ss.at[dx], sum_rs.at[4 - dx], along(dx)
        )

    @pl.loop(0, 8)
    def _(step):
        def at(number):
            return pl.when(step == number)

        @at(0)
        def _():
            for a in GROUPS:
                x_twin(0, a, True).wait_recv()

        @at(1)
        def _():
            for i, a in enumerate(GROUPS):
                x_ring(0, 0, 3, a).wait_recv()
                if i < 2:
                    x_ring(0, 3, 2, a).start()
                x_twin(3, a, False).start()
                x_ring(1, 0, 1, a).wait_recv()
                if i >= 2:
                    x_ring(1, 1, 2, a).start()
                x_twin(1, a, False).start()
            for a in GROUPS:
                x_twin(3, a, True).wait_recv()

        @at(2)
        def _():
            for a in GROUPS:
                x_twin(1, a, True).wait_recv()

        @at(3)
        def _():
            for a in ORDER:
                wait_group(a, *rest_way)
                rest_twin(a, False).start()
            for a in ORDER:
                rest_twin(a, True).wait_recv()
            for core in range(2):
                wide = x_rest[core].astype(F32)
                for dx in range(4):
                    rows_rest[dx, :, core * REST : (core + 1) * REST] = (
                        wide[:, dx * CAP : (dx + 1) * CAP, :]
                        .reshape(EXPERTS * CAP, REST)
                        .astype(BF16)
                    )

        @at(4)
        def _():
            for i, a in enumerate(GROUPS):
                x_ring(0 if i < 2 else 1, 0, 2, a).wait_recv()
                x_twin(2, a, False).start()

        @at(5)
        def _():
            settle(3)
            for q in range(2):
                near_copy(3, 0, q).start()
            for a in GROUPS:
                x_twin(2, a, True).wait_recv()

        @at(6)
        def _():
            settle(1)
            for q in range(2):
                near_copy(1, 1, q).start()
            over_plane(*rest_back[0])

        @at(7)
        def _():
            settle(2)
            for q in range(2):
                far_copy(0, q).start()
                far_copy(1, q).start()

        is_first = jnp.logical_or(step < 3, step == 5)
        dx = jnp.where(
            jnp.logical_or(step == 0, step == 7),
            0,
            jnp.where(
                jnp.logical_or(step == 1, step == 3),
                3,
                jnp.where(jnp.logical_or(step == 2, step == 4), 1, 2),
            ),
        )

        @pl.when(is_first)
        def _():
            first_part(dx)

        @pl.when(jnp.logical_not(is_first))
        def _():
            second_part(dx)

    settle(0)
    over_plane(*rest_back[1])
    for q in range(2):
        for h, dx in ((0, 1), (1, 3)):
            far_copy(h, q).wait_recv()
            at = slice(8 * h + 4 * q, 8 * h + 4 * q + 4)
            far_part = diag_recv[h, 4 * q : 4 * q + 4].astype(F32)
            parts[dx, at] = (parts[dx, at].astype(F32) + far_part).astype(BF16)
            near_copy(dx, h, q).start()

    def rest_sums(pair):
        @pl.loop(0, 16)
        def _(p):
            remote(
                rest_send.at[pair, p],
                rest_recv.at[pair, p],
                rest_ss.at[pair, p],
                rest_rs.at[pair, p],
                plane_dev(p),
            ).wait_recv()

        both = rest_recv[pair].astype(F32)
        found = []
        for i, dx in enumerate((3, 1) if pair == 0 else (2, 0)):
            table = both[:, i * CAP : (i + 1) * CAP, :].reshape(EXPERTS * CAP, REST).astype(BF16)
            found.append(combine(dx, table))
        return found

    for q in range(2):
        for h in range(2):
            near_copy(1, h, q).wait_recv()
            near_copy(3, h, q).wait_recv()
            at = slice(8 * h + 4 * q, 8 * h + 4 * q + 4)
            near_parts = side_recv[0, at].astype(F32) + side_recv[1, at].astype(F32)
            back[at] = (parts[0, at].astype(F32) + near_parts).astype(BF16)

        @pl.loop(0, 8)
        def _(i):
            to_plane(2 * 4 * far(i) + 4 * q + (y + 2 + 3 * (i // 2)) % 4, *back_way)

        if q == 0:
            found = rest_sums(0)
            for i, dx in enumerate((3, 1)):
                sum_send[dx] = found[i].astype(BF16)
                sum_copy(dx).start()

    found = rest_sums(1)
    sum_send[2] = found[0].astype(BF16)
    sum_copy(2).start()
    rest = moe_half[2, :, BULK:] + found[1]
    for dx in (2, 1, 3):
        sum_copy(4 - dx).wait_recv()
        rest = rest + sum_recv[dx].astype(F32)
    out[:, BULK:] = rest.astype(BF16)

    @pl.loop(0, 16)
    def _(p):
        remote(back.at[p], ret.at[p], b_ss.at[p], b_rs.at[p], plane_dev(p)).wait_recv()

    both = ret[...].astype(F32)
    for h in range(2):
        cols = slice(h * REST, (h + 1) * REST)
        table = both[:, h * CAP : (h + 1) * CAP, :].reshape(EXPERTS * CAP, REST).astype(BF16)
        out[:, cols] = (moe_half[2, :, cols] + combine(0, table)).astype(BF16)

    @pl.loop(0, 8)
    def _(i):
        kv_copy(0, i, False)
        kv_copy(1, i, False)
        q_copy(i, False)
        o_copy(i, False)

    for h in range(2):
        for copy in ring_own[h][0] + ring_own[h][1] + ring_on[h]:
            copy.wait_send()
        for dx in range(4):
            twin_copy(dx, h).wait_send()
    proj_copy.wait_send()

    @pl.loop(0, 16)
    def _(p):
        @pl.when(p != plane)
        def _():
            for way in (bulk_way, rest_way, rest_back[0], rest_back[1], back_way):
                plane_gone(*way, p)

    for dx in (1, 2, 3):
        to_line(info, info_ss, info_rs, dx).wait_send()
        to_line(tok_rest, tok_ss, tok_rs, dx).wait_send()
        sum_copy(dx).wait_send()
    for i, a in enumerate(GROUPS):
        x_ring(0, 0, 3, a).wait_send()
        x_ring(1, 0, 1, a).wait_send()
        (x_ring(0, 3, 2, a) if i < 2 else x_ring(1, 1, 2, a)).wait_send()
        for dx in range(4):
            x_twin(dx, a, False).wait_send()
        rest_twin(a, False).wait_send()
    for dx in range(4):
        y_copy(dx).wait_send()
    for h in range(2):
        for q in range(2):
            far_copy(h, q).wait_send()
            near_copy(1, h, q).wait_send()
            near_copy(3, h, q).wait_send()


def on_device(
    tokens,
    attn_weight,
    out_weight,
    norm_attn,
    norm_moe,
    routes,
    route_weight,
    expert_in,
    expert_out,
):
    vmem = pl.BlockSpec(memory_space=pltpu.VMEM)
    hbm = pl.BlockSpec(memory_space=pl.ANY)
    dma = pltpu.SemaphoreType.DMA
    pairs = (EXPERTS, 2 * CAP, REST)
    fours = (EXPERTS, 4 * CAP, REST)
    scratch = [
        pltpu.VMEM((TOK, D), BF16),
        pltpu.VMEM((D,), F32),
        pltpu.VMEM((D,), F32),
        pltpu.VMEM((2, TOK), jnp.int32),
        pltpu.VMEM((2, TOK), F32),
        dma((5,)),
        pltpu.VMEM((3, D, HALF), BF16),
        pltpu.VMEM((HALF, D), BF16),
        pltpu.VMEM((2, HALF, HALF), BF16),
        dma((14,)),
        pltpu.VMEM((TOK, D), BF16),
        pltpu.VMEM((3, 8, HD, TOK), BF16),
        pltpu.VMEM((HD, 8 * TOK), BF16),
        pltpu.VMEM((8, 2 * HD + 32, 8 * TOK), BF16),
        pltpu.VMEM((8 * TOK, 8 * TOK), F32),
        pltpu.VMEM((1, 8 * TOK), F32),
        pltpu.VMEM((1, 8 * TOK), F32),
        pltpu.VMEM((TOK, 8 * TOK), F32),
        pltpu.VMEM((8, HD, TOK), BF16),
        pltpu.VMEM((HALF, TOK), BF16),
        pltpu.VMEM((TOK, D), BF16),
        pltpu.VMEM((TOK, D), BF16),
        pltpu.VMEM((3, TOK, HALF), F32),
        pltpu.VMEM((4, 8, TOK), F32),
        pltpu.VMEM((4, EXPERTS * CAP, TOK), BF16),
        pltpu.VMEM((4, 2 * TOK, EXPERTS * CAP), BF16),
        pltpu.VMEM((4, 2, TOK, TOK), F32),
        pltpu.VMEM((4, TOK, REST), BF16),
        pltpu.VMEM(pairs, BF16),
        pltpu.VMEM(fours, F32),
        pltpu.VMEM(fours, BF16),
        pltpu.VMEM((4, 2) + pairs, BF16),
        pltpu.VMEM((2,) + fours, BF16),
        pltpu.VMEM((EXPERTS * CAP, 2 * BULK), BF16),
        pltpu.VMEM((4, EXPERTS * CAP, 2 * REST), BF16),
        pltpu.VMEM((4, 2, EXPERTS * CAP, HALF), F32),
        pltpu.VMEM((4, EXPERTS * CAP, HALF), BF16),
        pltpu.VMEM((4, EXPERTS * CAP, HALF), BF16),
        pltpu.VMEM((4,) + pairs, BF16),
        pltpu.VMEM((2, 8, 2 * CAP, REST), BF16),
        pltpu.VMEM((2,) + pairs, BF16),
        pltpu.VMEM(pairs, BF16),
        pltpu.VMEM(pairs, BF16),
        pltpu.VMEM((2,) + pairs, BF16),
        pltpu.VMEM((2,) + pairs, BF16),
        pltpu.VMEM((4, TOK, REST), BF16),
        pltpu.VMEM((4, TOK, REST), BF16),
        dma((2, 8)),
        dma((2, 8)),
        dma((8,)),
        dma((8,)),
        dma((4, 2, 2)),
        dma((4, 2, 2)),
        dma((4, 2)),
        dma((4, 2)),
        dma((8,)),
        dma((8,)),
        dma((2,)),
        dma((4,)),
        dma((4,)),
        dma((4,)),
        dma((4,)),
        dma((16,)),
        dma((16,)),
        dma((16,)),
        dma((16,)),
        dma((4, 4)),
        dma((4, 4)),
        dma((4, 4)),
        dma((4, 4)),
        dma((4,)),
        dma((4,)),
        dma((4,)),
        dma((4,)),
        dma((6, 2)),
        dma((6, 2)),
        dma((2, 16)),
        dma((2, 16)),
        dma((4,)),
        dma((4,)),
        dma((16,)),
        dma((16,)),
    ]
    return pl.pallas_call(
        layer_kernel,
        out_shape=jax.ShapeDtypeStruct((TOK, HALF), BF16),
        in_specs=[hbm] * 9,
        out_specs=vmem,
        scratch_shapes=scratch,
        compiler_params=pltpu.CompilerParams(
            collective_id=0, has_side_effects=True, vmem_limit_bytes=60 * 1024 * 1024
        ),
        cost_estimate=pl.CostEstimate(
            flops=30_000_000_000, bytes_accessed=17_000_000, transcendentals=9_000_000
        ),
    )(
        tokens,
        attn_weight,
        out_weight,
        norm_attn,
        norm_moe,
        routes.T,
        route_weight.T,
        expert_in,
        expert_out,
    )


def solution(mesh):
    return jax.shard_map(
        on_device,
        mesh=mesh,
        in_specs=(
            P("seq", None),
            P(None, None, "tensor"),
            P("tensor", None),
            P(),
            P(),
            P("seq", None),
            P("seq", None),
            P("seq", None, None, "tensor"),
            P("seq", "tensor", None),
        ),
        out_specs=P("seq", "tensor"),
        check_vma=False,
    )
```

```python
import math

import jax
import jax.numpy as jnp
from jax import lax
from jax.experimental import pallas as pl
from jax.experimental.pallas import tpu as pltpu
from jax.sharding import PartitionSpec as P

MESH = pl.DeviceIdType.MESH
D = 1536
HALF = 768
BULK = 512
REST = 256
ORDER = (2, 1, 3, 0)
GROUPS = (0, 1, 3, 2)
HD = 96
TOK = 128
EXPERTS = 16
CAP = 24
EPS = 1e-6
F32 = jnp.float32
BF16 = jnp.bfloat16
SCALE = HD ** (-0.5) * math.log2(math.e)


def dot(a, b):
    return jnp.dot(a, b, preferred_element_type=F32)


def remote(src, dst, send_sem, recv_sem, device):
    return pltpu.make_async_remote_copy(
        src_ref=src,
        dst_ref=dst,
        send_sem=send_sem,
        recv_sem=recv_sem,
        device_id=device,
        device_id_type=MESH,
    )


def layer_kernel(
    tokens_in,
    attn_w,
    out_w,
    norm_attn_in,
    norm_moe_in,
    routes_in,
    route_weight_in,
    expert_in,
    expert_out,
    out,
    tokens,
    norm_attn,
    norm_moe,
    routes,
    route_weight,
    small_sem,
    w_buf,
    ow_buf,
    wd_buf,
    w_sem,
    normed_buf,
    kv_send,
    q_t,
    kvb,
    score_buf,
    top,
    peak,
    acc,
    o_send,
    heads_t,
    proj_send,
    proj_recv,
    moe_half,
    info,
    spread,
    picks,
    shares,
    tok_rest,
    disp_bulk,
    disp_wide,
    disp_rest,
    x_bulk,
    x_rest,
    rows_bulk,
    rows_rest,
    sums,
    y_send,
    y_recv,
    parts,
    diag_recv,
    side_recv,
    back,
    ret,
    rest_send,
    rest_recv,
    sum_send,
    sum_recv,
    kv_ss,
    kv_rs,
    q_ss,
    q_rs,
    ring_ss,
    ring_rs,
    twin_ss,
    twin_rs,
    o_ss,
    o_rs,
    proj_sem,
    info_ss,
    info_rs,
    tok_ss,
    tok_rs,
    d_ss,
    d_rs,
    e_ss,
    e_rs,
    xr_ss,
    xr_rs,
    xt_ss,
    xt_rs,
    xe_ss,
    xe_rs,
    y_ss,
    y_rs,
    r_ss,
    r_rs,
    rest_ss,
    rest_rs,
    sum_ss,
    sum_rs,
    b_ss,
    b_rs,
):
    s = lax.axis_index("seq")
    c = lax.axis_index("tensor")
    x = s % 4
    plane = s // 4
    z = plane // 4
    y = plane % 4
    side = z // 2
    slot = (z % 2) * 4 + y
    left = (s - x + (x + 3) % 4, c)
    right = (s - x + (x + 1) % 4, c)
    twin = (s, 1 - c)

    def along(dx):
        return (s - x + (x + dx) % 4, c)

    def mate(i):
        return ((2 * c + i // 4) * 16 + (i % 4) * 4 + x, side)

    def is_me(i):
        return jnp.logical_and(c == side, i == slot)

    def plane_dev(p):
        return (p * 4 + x, c)

    barrier = pltpu.get_barrier_semaphore()

    def greet(device):
        pl.semaphore_signal(barrier, inc=1, device_id=device, device_id_type=MESH)

    for device in (left, right, along(2), twin):
        greet(device)

    @pl.loop(0, 8)
    def _(i):
        @pl.when(jnp.logical_not(is_me(i)))
        def _():
            greet(mate(i))

    @pl.loop(0, 16)
    def _(p):
        @pl.when(p != plane)
        def _():
            greet(plane_dev(p))

    small = [
        pltpu.make_async_copy(src, dst, small_sem.at[i])
        for i, (src, dst) in enumerate(
            (
                (tokens_in, tokens),
                (norm_attn_in, norm_attn),
                (routes_in, routes),
                (route_weight_in, route_weight),
                (norm_moe_in, norm_moe),
            )
        )
    ]
    for copy in small:
        copy.start()

    weight_copies = [
        pltpu.make_async_copy(attn_w.at[1], w_buf.at[1], w_sem.at[1]),
        pltpu.make_async_copy(attn_w.at[2], w_buf.at[2], w_sem.at[2]),
        pltpu.make_async_copy(attn_w.at[0], w_buf.at[0], w_sem.at[0]),
        pltpu.make_async_copy(out_w, ow_buf, w_sem.at[3]),
        pltpu.make_async_copy(expert_out.at[0, :, pl.ds(0, HALF)], wd_buf.at[0], w_sem.at[4]),
        pltpu.make_async_copy(expert_out.at[0, :, pl.ds(HALF, HALF)], wd_buf.at[1], w_sem.at[5]),
    ]
    moves = (
        (0, 0, BULK),
        (HALF, BULK, BULK),
        (BULK, 2 * BULK, REST),
        (HALF + BULK, 2 * BULK + REST, REST),
    )
    weight_copies += [
        pltpu.make_async_copy(
            expert_in.at[0, k, pl.ds(start, rows)],
            w_buf.at[1 + k, pl.ds(to, rows)],
            w_sem.at[6 + 4 * k + i],
        )
        for k in range(2)
        for i, (start, to, rows) in enumerate(moves)
    ]
    for copy in weight_copies[:3]:
        copy.start()

    small[0].wait()
    small[1].wait()
    tok = tokens[...].astype(F32)
    mean_square = jnp.mean(tok * tok, axis=1, keepdims=True)
    normed_buf[...] = (tok * lax.rsqrt(mean_square + EPS) * norm_attn[...].reshape(1, D)).astype(BF16)

    def exchange(i, src, dst, send_sem, recv_sem, start):
        copy = remote(src, dst, send_sem, recv_sem, mate(i))

        @pl.when(jnp.logical_not(is_me(i)))
        def _():
            if start:
                copy.start()
            else:
                copy.wait_send()

        if start:

            @pl.when(is_me(i))
            def _():
                pltpu.make_async_copy(src, dst, recv_sem).start()

    def far(a):
        return (z + jnp.where(c == side, 1, 0) + a) % 2

    def lanes(i):
        return pl.ds(pl.multiple_of(i * TOK, TOK), TOK)

    def kv_copy(h, i, start):
        exchange(
            i,
            kv_send.at[h, i],
            kvb.at[0, pl.ds(h * HD, HD), lanes(slot)],
            kv_ss.at[h, i],
            kv_rs.at[h, slot],
            start,
        )

    def q_copy(i, start):
        exchange(i, kv_send.at[2, i], q_t.at[:, lanes(slot)], q_ss.at[i], q_rs.at[slot], start)

    @pl.loop(0, 3)
    def _(h):
        at = (h + 1) % 3
        pltpu.make_async_copy(attn_w.at[at], w_buf.at[at], w_sem.at[at]).wait()
        scale = jnp.where(h == 2, SCALE, 1.0)
        kv_send[h] = (dot(normed_buf[...], w_buf[at]) * scale).T.astype(BF16).reshape(8, HD, TOK)

    for copy in weight_copies[3:]:
        copy.start()

    @pl.loop(0, 8)
    def _(b):
        kvb[b, 2 * HD : 2 * HD + 32, :] = jnp.ones((32, 8 * TOK), BF16)

    peak[...] = jnp.full(peak.shape, -1e30, F32)
    acc[...] = jnp.zeros(acc.shape, F32)

    for copy in small[2:]:
        copy.wait()
    expert_ids = lax.broadcasted_iota(jnp.int32, (EXPERTS, TOK), 0)
    hot = [(routes[k : k + 1, :] == expert_ids).astype(F32) for k in range(2)]
    earlier = (
        lax.broadcasted_iota(jnp.int32, (TOK, TOK), 0)
        < lax.broadcasted_iota(jnp.int32, (TOK, TOK), 1)
    ).astype(BF16)
    before = dot((hot[0] + hot[1]).astype(BF16), earlier)
    place = [
        jnp.sum(before * hot[k], axis=0, keepdims=True)
        + routes[k : k + 1, :].astype(F32) * float(CAP)
        for k in range(2)
    ]
    info[0] = jnp.zeros((8, TOK), F32)
    for k in range(2):
        info[0, k : k + 1, :] = place[k]
        info[0, 2 + k : 3 + k, :] = route_weight[k : k + 1, :]

    pl.semaphore_wait(barrier, 4 + 15 + 8 - jnp.where(c == side, 1, 0))
    @pl.loop(0, 16)
    def _(i):
        kv_copy(i // 8, far(i) * 4 + (y + 2 + 3 * (i // 2)) % 4, True)

    @pl.loop(0, 8)
    def _(i):
        q_copy(far(i) * 4 + (y + 2 + 3 * (i // 2)) % 4, True)

    def to_line(ref, send_sem, recv_sem, dx):
        return remote(
            ref.at[0], ref.at[4 - dx], send_sem.at[dx], recv_sem.at[4 - dx], along(dx)
        )

    for dx in (2, 1, 3):
        to_line(info, info_ss, info_rs, dx).start()

    def kv_part(dx, dc, h):
        return kvb.at[2 * dx + dc, pl.ds(h * HD, HD)]

    def ring_part(dx, h, part):
        if part is None:
            return kv_part(dx, 0, h)
        return kvb.at[2 * dx, pl.ds(h * HD, HD), pl.ds(part * 4 * TOK, 4 * TOK)]

    def ring_copy(to, src_dx, dst_dx, h, part=None):
        return remote(
            ring_part(src_dx, h, part),
            ring_part(dst_dx, h, part),
            ring_ss.at[dst_dx, h, part or 0],
            ring_rs.at[dst_dx, h, part or 0],
            right if to == 0 else left,
        )

    def twin_copy(dx, h):
        return remote(kv_part(dx, 0, h), kv_part(dx, 1, h), twin_ss.at[dx, h], twin_rs.at[dx, h], twin)

    ring_own = [
        [[ring_copy(0, 0, 3, 0)], [ring_copy(1, 0, 1, 0)]],
        [[ring_copy(0, 0, 3, 1)], [ring_copy(1, 0, 1, 1, part) for part in range(2)]],
    ]
    ring_on = [[ring_copy(0, 3, 2, 0)], [ring_copy(1, 1, 2, 1, part) for part in range(2)]]
    for h in range(2):

        @pl.loop(0, 8)
        def _(i):
            remote(
                kv_send.at[h, i],
                kvb.at[0, pl.ds(h * HD, HD), lanes(i)],
                kv_ss.at[h, i],
                kv_rs.at[h, i],
                mate(i),
            ).wait_recv()

        for copy in ring_own[h][0] + ring_own[h][1]:
            copy.start()
        twin_copy(0, h).start()

    @pl.loop(0, 8)
    def _(i):
        remote(
            kv_send.at[2, i], q_t.at[:, lanes(i)], q_ss.at[i], q_rs.at[i], mate(i)
        ).wait_recv()

    def block(step):
        dc = jnp.where(step < 2, step, jnp.where(step < 6, step // 4, step - 6))
        dx = jnp.where(step < 2, 0, jnp.where(step < 6, 3 - 2 * (step % 2), 2))
        return 2 * dx + dc

    def scores_of(b, at):
        return dot(kvb[b, 0:HD, at : at + 256].astype(F32).T.astype(BF16), q_t[...])

    def attend(this, following):
        old = peak[...]
        new = jnp.maximum(old, top[...])
        update = acc[...] * jnp.exp2(old - new)
        highest = None
        for at in range(0, 8 * TOK, 256):
            if following is not None:
                scores = scores_of(following, at)
                here = jnp.max(scores, axis=0, keepdims=True)
                highest = here if highest is None else jnp.maximum(highest, here)
            probs = jnp.exp2(score_buf[at : at + 256, :] - new).astype(BF16)
            update = update + dot(kvb[this, HD : HD + TOK, at : at + 256], probs)
            if following is not None:
                score_buf[at : at + 256, :] = scores
        acc[...] = update
        peak[...] = new
        if following is not None:
            top[...] = highest

    highest = None
    for at in range(0, 8 * TOK, 256):
        scores = scores_of(0, at)
        here = jnp.max(scores, axis=0, keepdims=True)
        highest = here if highest is None else jnp.maximum(highest, here)
        score_buf[at : at + 256, :] = scores
    top[...] = highest

    @pl.loop(1, 8)
    def _(step):
        @pl.when(step == 1)
        def _():
            twin_copy(0, 0).wait_recv()

        @pl.when(step == 2)
        def _():
            ring_own[0][0][0].wait_recv()
            ring_on[0][0].start()
            twin_copy(3, 0).start()
            ring_own[0][1][0].wait_recv()
            twin_copy(1, 0).start()
            twin_copy(0, 1).wait_recv()

        @pl.when(step == 3)
        def _():
            for part in range(2):
                ring_own[1][1][part].wait_recv()
                ring_on[1][part].start()
            twin_copy(1, 1).start()
            ring_own[1][0][0].wait_recv()
            twin_copy(3, 1).start()

        @pl.when(step == 4)
        def _():
            twin_copy(3, 0).wait_recv()

        @pl.when(step == 5)
        def _():
            twin_copy(1, 0).wait_recv()
            twin_copy(3, 1).wait_recv()

        @pl.when(step == 6)
        def _():
            ring_on[0][0].wait_recv()
            twin_copy(2, 0).start()
            twin_copy(1, 1).wait_recv()

        @pl.when(step == 7)
        def _():
            for copy in ring_on[1]:
                copy.wait_recv()
            twin_copy(2, 1).start()
            twin_copy(2, 0).wait_recv()

        attend(block(step - 1), block(step))

    twin_copy(2, 1).wait_recv()
    attend(5, None)

    def o_copy(i, start):
        exchange(
            i,
            o_send.at[i],
            heads_t.at[pl.ds(pl.multiple_of(slot * HD, HD), HD), :],
            o_ss.at[i],
            o_rs.at[slot],
            start,
        )

    @pl.loop(0, 8)
    def _(i):
        o_send[i] = (acc[0:HD, lanes(i)] / acc[HD : HD + 1, lanes(i)]).astype(BF16)
        o_copy(i, True)

    weight_copies[3].wait()

    @pl.loop(0, 8)
    def _(i):
        remote(
            o_send.at[i],
            heads_t.at[pl.ds(pl.multiple_of(i * HD, HD), HD), :],
            o_ss.at[i],
            o_rs.at[i],
            mate(i),
        ).wait_recv()

    heads = heads_t[...].astype(F32).T.astype(BF16)
    proj = dot(heads, ow_buf[...])
    proj_send[...] = proj.astype(BF16)
    proj_copy = remote(proj_send, proj_recv, proj_sem.at[0], proj_sem.at[1], twin)
    proj_copy.start()

    def column(row):
        return jnp.broadcast_to(row, (TOK, TOK)).T

    def fill_spread(dx):
        ids = lax.broadcasted_iota(jnp.int32, (EXPERTS * CAP, TOK), 0).astype(F32)
        hit = jnp.logical_or(ids == info[dx, 0:1, :], ids == info[dx, 1:2, :])
        spread[dx] = hit.astype(F32).astype(BF16)

    def fill_picks(dx):
        ids = lax.broadcasted_iota(jnp.int32, (TOK, EXPERTS * CAP), 1).astype(F32)
        for k in range(2):
            hit = ids == column(info[dx, k : k + 1, :])[:, 0:1]
            picks[dx, k * TOK : (k + 1) * TOK, :] = hit.astype(F32).astype(BF16)
            shares[dx, k] = column(info[dx, 2 + k : 3 + k, :])

    def combine(dx, table):
        rows = dot(picks[dx], table)
        return rows[0:TOK] * shares[dx, 0, :, 0:1] + rows[TOK:] * shares[dx, 1, :, 0:1]

    for dx in (1, 3, 2):
        to_line(info, info_ss, info_rs, 4 - dx).wait_recv()
    for dx in range(4):
        fill_spread(dx)
    proj_copy.wait_recv()
    hidden = tokens[...].astype(F32) + proj + proj_recv[...].astype(F32)
    inverse = lax.rsqrt(jnp.mean(hidden * hidden, axis=1, keepdims=True) + EPS)
    moe = hidden * inverse * norm_moe[...].reshape(1, D)
    sums[0, 0, 0:TOK, :] = hidden[:, 0:HALF]
    sums[0, 1, 0:TOK, :] = hidden[:, HALF:]
    moe_half[2] = sums[0, c, 0:TOK, :]
    moe_half[0] = moe[:, 0:HALF]
    moe_half[1] = moe[:, HALF:]
    mine = moe_half[c].astype(BF16)

    tok_rest[0] = mine[:, BULK:]
    for dx in (2, 1, 3):
        to_line(tok_rest, tok_ss, tok_rs, dx).start()
    rows = dot(spread[0], mine[:, 0:BULK]).reshape(EXPERTS, CAP, BULK)
    disp_bulk[:, 0:CAP, :] = rows[:, :, 0:REST].astype(BF16)
    disp_bulk[:, CAP:, :] = rows[:, :, REST:].astype(BF16)

    def to_plane(p, src, dst, send_sem, recv_sem):
        @pl.when(p == plane)
        def _():
            pltpu.make_async_copy(src.at[p], dst.at[plane], recv_sem.at[plane]).start()

        @pl.when(p != plane)
        def _():
            remote(
                src.at[p], dst.at[plane], send_sem.at[p], recv_sem.at[plane], plane_dev(p)
            ).start()

    def over_plane(src, dst, send_sem, recv_sem, near=False):
        @pl.loop(0, 16)
        def _(i):
            turn = i // 4
            if near:
                a = jnp.where(turn == 2, 3, jnp.where(turn == 3, 2, turn))
            else:
                a = (2 + 3 * turn) % 4
            p = ((z + a) % 4) * 4 + (y + 2 + 3 * i) % 4
            to_plane(p, src, dst, send_sem, recv_sem)

    def plane_gone(src, dst, send_sem, recv_sem, p):
        remote(src.at[p], dst.at[plane], send_sem.at[p], recv_sem.at[plane], plane_dev(p)).wait_send()

    bulk_way = (disp_bulk, x_bulk.at[0, c], d_ss, d_rs)
    rest_way = (disp_rest, x_rest.at[c], e_ss, e_rs)
    over_plane(*bulk_way, near=True)

    def group(a):
        return pl.ds(((z + 4 - a) % 4) * 4, 4)

    def x_ring(to, src_dx, dst_dx, a):
        return remote(
            x_bulk.at[src_dx, c, group(a)],
            x_bulk.at[dst_dx, c, group(a)],
            xr_ss.at[dst_dx, a],
            xr_rs.at[dst_dx, a],
            right if to == 0 else left,
        )

    def x_twin(dx, a, arriving):
        part = x_bulk.at[dx, 1 - c if arriving else c, group(a)]
        return remote(part, part, xt_ss.at[dx, a], xt_rs.at[dx, a], twin)

    def rest_twin(a, arriving):
        part = x_rest.at[1 - c if arriving else c, group(a)]
        return remote(part, part, xe_ss.at[a], xe_rs.at[a], twin)

    def wait_group(a, src, dst, send_sem, recv_sem):
        @pl.loop(0, 4)
        def _(b):
            p = ((z + 4 - a) % 4) * 4 + b
            remote(src.at[p], dst.at[p], send_sem.at[p], recv_sem.at[p], plane_dev(p)).wait_recv()

    def ring_group(a):
        wait_group(a, *bulk_way)
        x_ring(0, 0, 3, a).start()
        x_ring(1, 0, 1, a).start()
        x_twin(0, a, False).start()

    ring_group(GROUPS[0])
    disp_wide[:, 0:CAP, :] = dot(spread[0], tok_rest[0]).reshape(EXPERTS, CAP, REST)
    for dx in (1, 3, 2):
        to_line(tok_rest, tok_ss, tok_rs, 4 - dx).wait_recv()
        disp_wide[:, dx * CAP : (dx + 1) * CAP, :] = dot(spread[dx], tok_rest[dx]).reshape(
            EXPERTS, CAP, REST
        )
    disp_rest[...] = disp_wide[...].astype(BF16)
    over_plane(*rest_way)

    for a in GROUPS[1:]:
        ring_group(a)
    for dx in range(4):
        fill_picks(dx)

    def y_copy(dx):
        return remote(y_send.at[dx], y_recv.at[dx], y_ss.at[dx], y_rs.at[dx], twin)

    def first_part(dx):
        for core in range(2):
            piece = x_bulk[dx, core].astype(F32)
            for h in range(2):
                at = core * BULK + h * REST
                rows_bulk[:, at : at + REST] = (
                    piece[:, h * CAP : (h + 1) * CAP, :].reshape(EXPERTS * CAP, REST).astype(BF16)
                )
        for k in range(2):
            sums[dx, k] = dot(rows_bulk[...], w_buf[1 + k, 0 : 2 * BULK, :])

    def second_part(dx):
        rows = rows_rest[dx]
        gate = sums[dx, 0] + dot(rows, w_buf[1, 2 * BULK :, :])
        up = sums[dx, 1] + dot(rows, w_buf[2, 2 * BULK :, :])
        active = (gate / (1.0 + jnp.exp(-gate)) * up).astype(BF16)
        y_send[dx] = dot(active, wd_buf[1 - c]).astype(BF16)
        y_copy(dx).start()
        sums[dx, 0] = dot(active, wd_buf[c])

    def settle(dx):
        y_copy(dx).wait_recv()
        total = (sums[dx, 0] + y_recv[dx].astype(F32)).reshape(EXPERTS, CAP, HALF)
        parts[dx, :, 0:CAP, :] = total[:, :, 0:REST].astype(BF16)
        parts[dx, :, CAP:, :] = total[:, :, REST:BULK].astype(BF16)
        pair, at = (0 if dx in (1, 3) else 1), (0 if dx > 1 else CAP)
        rest_send[pair, :, at : at + CAP, :] = total[:, :, BULK:].astype(BF16)

    for copy in weight_copies[4:]:
        copy.wait()
    def piece_of(h, q):
        return pl.ds(8 * h + 4 * q, 4)

    def far_copy(h, q):
        return remote(
            parts.at[2, piece_of(h, q)],
            diag_recv.at[h, pl.ds(4 * q, 4)],
            r_ss.at[h, q],
            r_rs.at[h, q],
            right if h == 0 else left,
        )

    def near_copy(dx, h, q):
        number = 2 + (dx // 2) * 2 + h
        return remote(
            parts.at[dx, piece_of(h, q)],
            side_recv.at[dx // 2, piece_of(h, q)],
            r_ss.at[number, q],
            r_rs.at[number, q],
            right if dx == 1 else left,
        )

    rest_back = [
        (rest_send.at[pair], rest_recv.at[pair], rest_ss.at[pair], rest_rs.at[pair])
        for pair in range(2)
    ]
    back_way = (back, ret, b_ss, b_rs)

    def sum_copy(dx):
        return remote(
            sum_send.at[dx], sum_recv.at[4 - dx], sum_ss.at[dx], sum_rs.at[4 - dx], along(dx)
        )

    @pl.loop(0, 8)
    def _(step):
        def at(number):
            return pl.when(step == number)

        @at(0)
        def _():
            for a in GROUPS:
                x_twin(0, a, True).wait_recv()

        @at(1)
        def _():
            for i, a in enumerate(GROUPS):
                x_ring(0, 0, 3, a).wait_recv()
                if i < 2:
                    x_ring(0, 3, 2, a).start()
                x_twin(3, a, False).start()
                x_ring(1, 0, 1, a).wait_recv()
                if i >= 2:
                    x_ring(1, 1, 2, a).start()
                x_twin(1, a, False).start()
            for a in GROUPS:
                x_twin(3, a, True).wait_recv()

        @at(2)
        def _():
            for a in GROUPS:
                x_twin(1, a, True).wait_recv()

        @at(3)
        def _():
            for a in ORDER:
                wait_group(a, *rest_way)
                rest_twin(a, False).start()
            for a in ORDER:
                rest_twin(a, True).wait_recv()
            for core in range(2):
                wide = x_rest[core].astype(F32)
                for dx in range(4):
                    rows_rest[dx, :, core * REST : (core + 1) * REST] = (
                        wide[:, dx * CAP : (dx + 1) * CAP, :]
                        .reshape(EXPERTS * CAP, REST)
                        .astype(BF16)
                    )

        @at(4)
        def _():
            for i, a in enumerate(GROUPS):
                x_ring(0 if i < 2 else 1, 0, 2, a).wait_recv()
                x_twin(2, a, False).start()

        @at(5)
        def _():
            settle(3)
            for q in range(2):
                near_copy(3, 0, q).start()
            for a in GROUPS:
                x_twin(2, a, True).wait_recv()

        @at(6)
        def _():
            settle(1)
            for q in range(2):
                near_copy(1, 1, q).start()

        @at(7)
        def _():
            over_plane(*rest_back[0])
            settle(2)
            for q in range(2):
                far_copy(0, q).start()
                far_copy(1, q).start()

        is_first = jnp.logical_or(step < 3, step == 5)
        dx = jnp.where(
            jnp.logical_or(step == 0, step == 7),
            0,
            jnp.where(
                jnp.logical_or(step == 1, step == 3),
                3,
                jnp.where(jnp.logical_or(step == 2, step == 4), 1, 2),
            ),
        )

        @pl.when(is_first)
        def _():
            first_part(dx)

        @pl.when(jnp.logical_not(is_first))
        def _():
            second_part(dx)

    settle(0)
    over_plane(*rest_back[1])
    for q in range(2):
        for h, dx in ((0, 1), (1, 3)):
            far_copy(h, q).wait_recv()
            at = slice(8 * h + 4 * q, 8 * h + 4 * q + 4)
            far_part = diag_recv[h, 4 * q : 4 * q + 4].astype(F32)
            parts[dx, at] = (parts[dx, at].astype(F32) + far_part).astype(BF16)
            near_copy(dx, h, q).start()

    def rest_sums(pair):
        @pl.loop(0, 16)
        def _(p):
            remote(
                rest_send.at[pair, p],
                rest_recv.at[pair, p],
                rest_ss.at[pair, p],
                rest_rs.at[pair, p],
                plane_dev(p),
            ).wait_recv()

        both = rest_recv[pair].astype(F32)
        found = []
        for i, dx in enumerate((3, 1) if pair == 0 else (2, 0)):
            table = both[:, i * CAP : (i + 1) * CAP, :].reshape(EXPERTS * CAP, REST).astype(BF16)
            found.append(combine(dx, table))
        return found

    for q in range(2):
        for h in range(2):
            near_copy(1, h, q).wait_recv()
            near_copy(3, h, q).wait_recv()
            at = slice(8 * h + 4 * q, 8 * h + 4 * q + 4)
            near_parts = side_recv[0, at].astype(F32) + side_recv[1, at].astype(F32)
            back[at] = (parts[0, at].astype(F32) + near_parts).astype(BF16)

        @pl.loop(0, 8)
        def _(i):
            to_plane(2 * 4 * far(i) + 4 * q + (y + 2 + 3 * (i // 2)) % 4, *back_way)

        if q == 0:
            found = rest_sums(0)
            for i, dx in enumerate((3, 1)):
                sum_send[dx] = found[i].astype(BF16)
                sum_copy(dx).start()

    found = rest_sums(1)
    sum_send[2] = found[0].astype(BF16)
    sum_copy(2).start()
    rest = moe_half[2, :, BULK:] + found[1]
    for dx in (2, 1, 3):
        sum_copy(4 - dx).wait_recv()
        rest = rest + sum_recv[dx].astype(F32)
    out[:, BULK:] = rest.astype(BF16)

    @pl.loop(0, 16)
    def _(p):
        remote(back.at[p], ret.at[p], b_ss.at[p], b_rs.at[p], plane_dev(p)).wait_recv()

    both = ret[...].astype(F32)
    for h in range(2):
        cols = slice(h * REST, (h + 1) * REST)
        table = both[:, h * CAP : (h + 1) * CAP, :].reshape(EXPERTS * CAP, REST).astype(BF16)
        out[:, cols] = (moe_half[2, :, cols] + combine(0, table)).astype(BF16)

    @pl.loop(0, 8)
    def _(i):
        kv_copy(0, i, False)
        kv_copy(1, i, False)
        q_copy(i, False)
        o_copy(i, False)

    for h in range(2):
        for copy in ring_own[h][0] + ring_own[h][1] + ring_on[h]:
            copy.wait_send()
        for dx in range(4):
            twin_copy(dx, h).wait_send()
    proj_copy.wait_send()

    @pl.loop(0, 16)
    def _(p):
        @pl.when(p != plane)
        def _():
            for way in (bulk_way, rest_way, rest_back[0], rest_back[1], back_way):
                plane_gone(*way, p)

    for dx in (1, 2, 3):
        to_line(info, info_ss, info_rs, dx).wait_send()
        to_line(tok_rest, tok_ss, tok_rs, dx).wait_send()
        sum_copy(dx).wait_send()
    for i, a in enumerate(GROUPS):
        x_ring(0, 0, 3, a).wait_send()
        x_ring(1, 0, 1, a).wait_send()
        (x_ring(0, 3, 2, a) if i < 2 else x_ring(1, 1, 2, a)).wait_send()
        for dx in range(4):
            x_twin(dx, a, False).wait_send()
        rest_twin(a, False).wait_send()
    for dx in range(4):
        y_copy(dx).wait_send()
    for h in range(2):
        for q in range(2):
            far_copy(h, q).wait_send()
            near_copy(1, h, q).wait_send()
            near_copy(3, h, q).wait_send()


def on_device(
    tokens,
    attn_weight,
    out_weight,
    norm_attn,
    norm_moe,
    routes,
    route_weight,
    expert_in,
    expert_out,
):
    vmem = pl.BlockSpec(memory_space=pltpu.VMEM)
    hbm = pl.BlockSpec(memory_space=pl.ANY)
    dma = pltpu.SemaphoreType.DMA
    pairs = (EXPERTS, 2 * CAP, REST)
    fours = (EXPERTS, 4 * CAP, REST)
    scratch = [
        pltpu.VMEM((TOK, D), BF16),
        pltpu.VMEM((D,), F32),
        pltpu.VMEM((D,), F32),
        pltpu.VMEM((2, TOK), jnp.int32),
        pltpu.VMEM((2, TOK), F32),
        dma((5,)),
        pltpu.VMEM((3, D, HALF), BF16),
        pltpu.VMEM((HALF, D), BF16),
        pltpu.VMEM((2, HALF, HALF), BF16),
        dma((14,)),
        pltpu.VMEM((TOK, D), BF16),
        pltpu.VMEM((3, 8, HD, TOK), BF16),
        pltpu.VMEM((HD, 8 * TOK), BF16),
        pltpu.VMEM((8, 2 * HD + 32, 8 * TOK), BF16),
        pltpu.VMEM((8 * TOK, 8 * TOK), F32),
        pltpu.VMEM((1, 8 * TOK), F32),
        pltpu.VMEM((1, 8 * TOK), F32),
        pltpu.VMEM((TOK, 8 * TOK), F32),
        pltpu.VMEM((8, HD, TOK), BF16),
        pltpu.VMEM((HALF, TOK), BF16),
        pltpu.VMEM((TOK, D), BF16),
        pltpu.VMEM((TOK, D), BF16),
        pltpu.VMEM((3, TOK, HALF), F32),
        pltpu.VMEM((4, 8, TOK), F32),
        pltpu.VMEM((4, EXPERTS * CAP, TOK), BF16),
        pltpu.VMEM((4, 2 * TOK, EXPERTS * CAP), BF16),
        pltpu.VMEM((4, 2, TOK, TOK), F32),
        pltpu.VMEM((4, TOK, REST), BF16),
        pltpu.VMEM(pairs, BF16),
        pltpu.VMEM(fours, F32),
        pltpu.VMEM(fours, BF16),
        pltpu.VMEM((4, 2) + pairs, BF16),
        pltpu.VMEM((2,) + fours, BF16),
        pltpu.VMEM((EXPERTS * CAP, 2 * BULK), BF16),
        pltpu.VMEM((4, EXPERTS * CAP, 2 * REST), BF16),
        pltpu.VMEM((4, 2, EXPERTS * CAP, HALF), F32),
        pltpu.VMEM((4, EXPERTS * CAP, HALF), BF16),
        pltpu.VMEM((4, EXPERTS * CAP, HALF), BF16),
        pltpu.VMEM((4,) + pairs, BF16),
        pltpu.VMEM((2, 8, 2 * CAP, REST), BF16),
        pltpu.VMEM((2,) + pairs, BF16),
        pltpu.VMEM(pairs, BF16),
        pltpu.VMEM(pairs, BF16),
        pltpu.VMEM((2,) + pairs, BF16),
        pltpu.VMEM((2,) + pairs, BF16),
        pltpu.VMEM((4, TOK, REST), BF16),
        pltpu.VMEM((4, TOK, REST), BF16),
        dma((2, 8)),
        dma((2, 8)),
        dma((8,)),
        dma((8,)),
        dma((4, 2, 2)),
        dma((4, 2, 2)),
        dma((4, 2)),
        dma((4, 2)),
        dma((8,)),
        dma((8,)),
        dma((2,)),
        dma((4,)),
        dma((4,)),
        dma((4,)),
        dma((4,)),
        dma((16,)),
        dma((16,)),
        dma((16,)),
        dma((16,)),
        dma((4, 4)),
        dma((4, 4)),
        dma((4, 4)),
        dma((4, 4)),
        dma((4,)),
        dma((4,)),
        dma((4,)),
        dma((4,)),
        dma((6, 2)),
        dma((6, 2)),
        dma((2, 16)),
        dma((2, 16)),
        dma((4,)),
        dma((4,)),
        dma((16,)),
        dma((16,)),
    ]
    return pl.pallas_call(
        layer_kernel,
        out_shape=jax.ShapeDtypeStruct((TOK, HALF), BF16),
        in_specs=[hbm] * 9,
        out_specs=vmem,
        scratch_shapes=scratch,
        compiler_params=pltpu.CompilerParams(
            collective_id=0, has_side_effects=True, vmem_limit_bytes=60 * 1024 * 1024
        ),
        cost_estimate=pl.CostEstimate(
            flops=30_000_000_000, bytes_accessed=17_000_000, transcendentals=9_000_000
        ),
    )(
        tokens,
        attn_weight,
        out_weight,
        norm_attn,
        norm_moe,
        routes.T,
        route_weight.T,
        expert_in,
        expert_out,
    )


def solution(mesh):
    return jax.shard_map(
        on_device,
        mesh=mesh,
        in_specs=(
            P("seq", None),
            P(None, None, "tensor"),
            P("tensor", None),
            P(),
            P(),
            P("seq", None),
            P("seq", None),
            P("seq", None, None, "tensor"),
            P("seq", "tensor", None),
        ),
        out_specs=P("seq", "tensor"),
        check_vma=False,
    )
```
